32 devices in a mesh: dp: 2 (over core), blk: 16 (over z, y, x).
Axes of the slice: x: 2, y: 2, z: 4, core: 2. Of those that a mesh axis runs over, the one named last changes fastest.
Arguments:
- features: bfloat16 [2, 8192, 128], P('dp', 'blk'), may hold values from -6 to 6
- tile_mask: int32 [2, 16], P('dp', 'blk'), may hold values 0 or 1
- w_first: bfloat16 [3456, 128], replicated, may hold values from -0.109375 to 0.109375
- w_second: bfloat16 [3456, 128], replicated, may hold values from -0.109375 to 0.109375
- cotangent: bfloat16 [2, 8192, 128], P('dp', 'blk'), may hold values from -6 to 6
Outputs:
- grad_first: float32 [3456, 128], replicated
- grad_second: float32 [3456, 128], replicated
- feature_grad: bfloat16 [2, 8192, 128], P('dp', 'blk')
The draws below stay inside these ranges and needn't reach their ends.
All inputs are finite; a program needn't handle non-finite values. No bound on the sum of `tile_mask` on one device may be relied on, other than what follows from the above.
Results may differ from the reference program's by a relative error of at most 0.0039.
Values may be sent and summed in bfloat16 or wider, within the bound.
No kernel may reach another device: no remote copies, remote signals or barrier semaphores. Data moves between devices by JAX's collectives and lax.ppermute only.
A program may use at most 64 MiB of HBM per device.

```python
import jax
import jax.numpy as jnp
from jax import lax

C = 128
TILE = 8
TX = 1
SAMPLES = 2
TILES = 16
CELLS = 8192
N_BLK = 16


def with_ends(entries, rng, smallest, high):
    spot = [jax.random.randint(jax.random.fold_in(rng, axis), (), 0, length) for axis, length in enumerate(entries.shape)]
    widest = entries.shape.index(max(entries.shape))
    neighbour = spot[:widest] + [(spot[widest] + 1) % entries.shape[widest]] + spot[widest + 1:]
    return entries.at[tuple(spot)].set(smallest).at[tuple(neighbour)].set(high)


def raised(values, stream_key, source, target, blocks, factor):
    def block_of(axis_at):
        return (jnp.arange(values.shape[axis_at]) // (values.shape[axis_at] // blocks)).reshape((-1,) + (1,) * (values.ndim - 1 - axis_at))

    one_side = jax.random.permutation(stream_key, blocks)[block_of(target)]
    other_side = (block_of(target) + blocks // 2) % blocks
    return jnp.where((block_of(source) == one_side) | (block_of(source) == other_side), factor * values, values)


def steps_of(stream_key, shape, pieces, smallest, largest):
    def one(dim, blocks):
        steps = jax.random.uniform(jax.random.fold_in(jax.random.fold_in(stream_key, 6), dim), (blocks,), jnp.float32, smallest / len(pieces), largest / len(pieces))
        return jnp.repeat(jnp.exp(steps), shape[dim] // blocks).reshape((-1,) + (1,) * (len(shape) - dim - 1))

    factor_of = one(*pieces[0])
    for cut in pieces[1:]:
        factor_of = factor_of * one(*cut)
    return factor_of


def centred(key, dims, scale, bound, split=(), kind=jnp.bfloat16):
    drawn = scale * jax.random.normal(key, dims, jnp.float32)
    if split:
        drawn = drawn * steps_of(key, dims, split, -0.22, 0.18)
    return jnp.clip(drawn, -bound, bound).astype(kind)


def bell_draw_with(key, shape, scale, limit, cuts, heavy, held_as=jnp.bfloat16):
    values = scale * jax.random.normal(key, shape, jnp.float32)
    if cuts:
        values = values * steps_of(key, shape, cuts, -0.22, 0.18)
    return jnp.clip(raised(values, jax.random.fold_in(key, 3), *heavy), -limit, limit).astype(held_as)


def setup_inputs(seed: int = 0) -> dict:
    keys = jax.random.split(jax.random.key(seed), 6)
    features = bell_draw_with(keys[0], (SAMPLES, CELLS, C), 1.0, 6.0, ((0, 2), (1, 16)), (1, 2, 16, 2.0))
    tile_mask = with_ends((jax.random.randint(keys[1], (SAMPLES, TILES), 0, 4) < 3).astype(jnp.int32), jax.random.fold_in(keys[1], 1), 0, 1)
    w_first = centred(keys[2], (27 * C, C), (27 * C) ** -0.5, 0.109375)
    w_second = centred(keys[3], (27 * C, C), (27 * C) ** -0.5, 0.109375)
    cotangent = centred(keys[4], (SAMPLES, CELLS, C), 1.0, 6.0, ((0, 2), (1, 16)))
    return {"features": features, "tile_mask": tile_mask, "w_first": w_first, "w_second": w_second, "cotangent": cotangent}


unscale = 1.0 / 512.0


def stack_depth(padded, depth_z):
    return jnp.concatenate([padded[:, :, shift_z:shift_z + depth_z, :] for shift_z in range(3)], axis=-1)


def arrange(weight):
    width_in = weight.shape[0] // 27
    width_out = weight.shape[1]
    shaped = weight.reshape(width_in, 3, 3, 3, width_out).transpose(1, 2, 3, 0, 4)
    return shaped.reshape(3, 3, 3 * width_in, width_out)


def arrange_flipped(weight):
    width_in = weight.shape[0] // 27
    width_out = weight.shape[1]
    shaped = weight.reshape(width_in, 3, 3, 3, width_out)[:, ::-1, ::-1, ::-1, :].transpose(1, 2, 3, 4, 0)
    return shaped.reshape(3, 3, 3 * width_out, width_in)


def convolve(padded, kernel):
    size_x = padded.shape[0] - 2
    size_y = padded.shape[1] - 2
    size_z = padded.shape[2] - 2
    stacked = stack_depth(padded, size_z)
    summed = jnp.zeros((size_x * size_y * size_z, kernel.shape[-1]), jnp.float32)
    for step_x in range(3):
        for step_y in range(3):
            slab_rows = stacked[step_x:step_x + size_x, step_y:step_y + size_y].reshape(-1, stacked.shape[-1])
            summed = summed + jnp.dot(slab_rows, kernel[step_x, step_y], preferred_element_type=jnp.float32)
    return summed


def correlate(padded, grads):
    size_x = padded.shape[0] - 2
    size_y = padded.shape[1] - 2
    size_z = padded.shape[2] - 2
    width_in = padded.shape[3]
    width_out = grads.shape[1]
    stacked = stack_depth(padded, size_z)
    blocks = []
    for step_x in range(3):
        for step_y in range(3):
            slab_rows = stacked[step_x:step_x + size_x, step_y:step_y + size_y].reshape(-1, stacked.shape[-1])
            blocks.append(lax.dot_general(slab_rows, grads, (((0,), (0,)), ((), ())), preferred_element_type=jnp.float32))
    joined = jnp.stack(blocks).reshape(3, 3, 3, width_in, width_out).transpose(3, 0, 1, 2, 4)
    return joined.reshape(27 * width_in, width_out)


def to_grid(rows, width):
    shaped = rows.reshape(N_BLK // 16, 4, 4, TX * TILE, TILE, TILE, width).transpose(0, 3, 1, 4, 2, 5, 6)
    return shaped.reshape((N_BLK // 16) * TX * TILE, 4 * TILE, 4 * TILE, width)


def to_rows(grid, width):
    shaped = grid.reshape(N_BLK // 16, TX * TILE, 4, TILE, 4, TILE, width).transpose(0, 2, 4, 1, 3, 5, 6)
    return shaped.reshape(N_BLK * TX * TILE * TILE * TILE, width)


def surround(grid):
    return jnp.pad(grid, ((1, 1), (1, 1), (1, 1), (0, 0)))


def reference(features, tile_mask, w_first, w_second, cotangent):
    kernel_first = arrange(w_first)
    kernel_second_back = arrange_flipped(w_second)
    kernel_first_back = arrange_flipped(w_first)
    width = features.shape[2]
    grad_first = jnp.zeros((27 * width, width), jnp.float32)
    grad_second = jnp.zeros((27 * width, width), jnp.float32)
    results = []
    for sample in range(features.shape[0]):
        keep_rows = jnp.repeat(tile_mask[sample], TILE * TILE * TILE).astype(features.dtype)[:, None]
        grid_shape = to_grid(keep_rows, 1).shape
        keep = to_grid(keep_rows, 1).reshape(-1, 1)
        inputs = to_grid(features[sample] * keep_rows, width)
        grads_out = to_grid(cotangent[sample] * keep_rows, width)
        grads_flat = grads_out.reshape(-1, width)
        pad_in = surround(inputs)
        pre_act = convolve(pad_in, kernel_first)
        hidden = (jax.nn.silu(pre_act) * keep.astype(jnp.float32)).astype(features.dtype)
        hidden_grid = hidden.reshape(grid_shape[:3] + (width,))
        grad_second = grad_second + correlate(surround(hidden_grid), grads_flat) * unscale
        back = convolve(surround(grads_out), kernel_second_back)
        sigma = jax.nn.sigmoid(pre_act)
        pre_grad = (back * sigma * (1.0 + pre_act * (1.0 - sigma)) * keep.astype(jnp.float32)).astype(features.dtype)
        grad_first = grad_first + correlate(pad_in, pre_grad) * unscale
        pre_grid = pre_grad.reshape(grid_shape[:3] + (width,))
        summed = grads_flat.astype(jnp.float32) + convolve(surround(pre_grid), kernel_first_back)
        result = (summed * keep.astype(jnp.float32)).astype(features.dtype)
        results.append(to_rows(result.reshape(grid_shape[:3] + (width,)), width))
    return grad_first, grad_second, jnp.stack(results)
```

```python
import functools

import jax
import jax.numpy as jnp
from jax import lax
from jax.experimental import pallas as pl
from jax.experimental.pallas import tpu as pltpu
from jax.sharding import PartitionSpec as P

TILE = 8
FACE = TILE * TILE
RIM = TILE + 2
GROWN = TILE + 4
IN_PITCH = 160
PITCH = 128
OUT_PITCH = 96
TAPS = 27
INNER = 4
BF = jnp.bfloat16
F32 = jnp.float32
unscale = 1.0 / 512.0
LIMIT = 48 * 2**20

VM = pl.BlockSpec(memory_space=pltpu.VMEM)
SM = pl.BlockSpec(memory_space=pltpu.SMEM)
AWAY = pl.BlockSpec(memory_space=pl.ANY)


def call(body, outs, ins, scratch=(), smem=(), away=(), flops=0):
    specs = [SM if i in smem else AWAY if i in away else VM for i in range(len(ins))]
    moved = sum(a.size * a.dtype.itemsize for a in list(ins) + list(outs))
    return pl.pallas_call(
        body,
        out_shape=list(outs),
        in_specs=specs,
        out_specs=[VM] * len(outs),
        scratch_shapes=list(scratch),
        compiler_params=pltpu.CompilerParams(vmem_limit_bytes=LIMIT),
        cost_estimate=pl.CostEstimate(flops=flops, bytes_accessed=moved, transcendentals=0),
    )(*ins)


def shape(dims, kind):
    return jax.ShapeDtypeStruct(dims, kind)


def parity(stride):
    return lax.axis_index("blk") // stride % 2


def pack_rows(planes, tile_of, mask_rows, mask, feat, cot, inp, grads, marks, even, odd, raw, sem):
    copies = [
        pltpu.make_async_copy(src, raw.at[at], sem.at[at]) for at, src in enumerate((feat, cot))
    ]
    for copy in copies:
        copy.start()
    row = lax.broadcasted_iota(jnp.int32, (mask_rows, 128), 0)
    filled = jnp.zeros((mask_rows, 128), F32)
    kept_of = [mask[0, tile_of(e)].astype(F32) for e in range(planes)]
    for e in range(planes):
        filled = jnp.where(row == e, kept_of[e], filled)
    filled = filled.astype(BF)
    marks[...] = filled
    even[4 * planes * TILE :, :] = filled
    odd[4 * planes * TILE :, :] = filled
    for copy in copies:
        copy.wait()
    side = parity(4)
    for at, dst in enumerate((inp, grads)):
        for e in range(planes):
            kept = (raw[at, e * FACE : (e + 1) * FACE, :].astype(F32) * kept_of[e]).astype(BF)
            dst[e * FACE : (e + 1) * FACE, :] = kept

    def faces(lo, hi):
        for at, src in enumerate((inp, grads)):
            for e in range(planes):
                to = slice((at * planes + e) * 2 * TILE, (at * planes + e + 1) * 2 * TILE)
                lo[to, :] = src[e * FACE : e * FACE + 2 * TILE, :]
                hi[to, :] = src[(e + 1) * FACE - 2 * TILE : (e + 1) * FACE, :]

    @pl.when(side == 0)
    def _():
        faces(odd, even)

    @pl.when(side == 1)
    def _():
        faces(even, odd)


def pack_depth(
    planes, mask_rows, inp, grads, marks, y_even, y_odd, even, odd, tall_in, tall_g, marks3, grown
):
    strip = planes * GROWN
    line = GROWN * TILE
    tail = 4 * planes * TILE

    def middle(from_lo, from_hi):
        for at, (src, dst) in enumerate(((inp, tall_in), (grads, tall_g))):
            for e in range(planes):
                base = (at * planes + e) * 2 * TILE
                top = e * line
                dst[top : top + 2 * TILE, :] = from_lo[base : base + 2 * TILE, :]
                dst[top + 2 * TILE : top + 2 * TILE + FACE, :] = src[e * FACE : (e + 1) * FACE, :]
                dst[top + 2 * TILE + FACE : top + line, :] = from_hi[base : base + 2 * TILE, :]
        for at, rows in enumerate((from_lo[tail:, :], marks[...], from_hi[tail:, :])):
            marks3[at * mask_rows : (at + 1) * mask_rows, :] = rows

    @pl.when(parity(4) == 0)
    def _():
        middle(y_odd, y_even)

    @pl.when(parity(4) == 1)
    def _():
        middle(y_even, y_odd)

    for ref in (even, odd):
        ref[4 * strip :, :] = marks3[...]
    side = parity(1)
    for at, src in enumerate((tall_in, tall_g)):
        grown[...] = src[...].astype(F32)

        def faces(lo, hi, at=at):
            for k in range(2):
                to = slice((at * 2 + k) * strip, (at * 2 + k + 1) * strip)
                lo[to, :] = grown[pl.ds(k, strip, stride=TILE), :].astype(BF)
                hi[to, :] = grown[pl.ds(TILE - 2 + k, strip, stride=TILE), :].astype(BF)

        @pl.when(side == 0)
        def _():
            faces(odd, even)

        @pl.when(side == 1)
        def _():
            faces(even, odd)


def lay_weights(first, second, first_rows, first_wide, second_wide, raw, wide, sem):
    copies = [
        pltpu.make_async_copy(src, raw.at[at], sem.at[at])
        for at, src in enumerate((first, second))
    ]
    for copy in copies:
        copy.start()
    for at, (rows, columns) in enumerate(((first_rows, first_wide), (None, second_wide))):
        copies[at].wait()
        wide[...] = raw[at].astype(F32)
        for tap in range(TAPS):
            block = wide[pl.ds(tap, 128, stride=TAPS), :].astype(BF)
            if rows is not None:
                rows[tap * 128 : (tap + 1) * 128, :] = block
            columns[:, tap * 128 : (tap + 1) * 128] = block


def dot(a, b):
    return lax.dot_general(a, b, (((1,), (0,)), ((), ())), preferred_element_type=F32)


def dot_t(a, b):
    return lax.dot_general(a, b, (((1,), (1,)), ((), ())), preferred_element_type=F32)


def spread(planes, first_plane, at, tall, z_even, z_odd, grid):
    grid[...] = jnp.zeros_like(grid)
    strip = planes * GROWN
    for e in range(planes):
        top = (first_plane + e) * IN_PITCH + 2
        for y in range(0, GROWN, 2):
            pair = tall[(e * GROWN + y) * TILE : (e * GROWN + y + 2) * TILE, :].astype(F32)
            grid[top + y * GROWN : top + y * GROWN + TILE, :] = pair[:TILE]
            grid[top + (y + 1) * GROWN : top + (y + 1) * GROWN + TILE, :] = pair[TILE:]
    swapped = parity(1) == 0
    for k in range(2):
        rows = slice((at * 2 + k) * strip, (at * 2 + k + 1) * strip)
        one, two = z_even[rows, :].astype(F32), z_odd[rows, :].astype(F32)
        left, right = jnp.where(swapped, two, one), jnp.where(swapped, one, two)
        for e in range(planes):
            top = (first_plane + e) * IN_PITCH
            grid[pl.ds(top + k, GROWN, stride=GROWN), :] = left[e * GROWN : (e + 1) * GROWN]
            grid[pl.ds(top + 2 + TILE + k, GROWN, stride=GROWN), :] = right[
                e * GROWN : (e + 1) * GROWN
            ]


def stack(n_planes, grid, stacked, flipped):
    for p in range(n_planes):
        for b in range(3):
            for c in range(3):
                step = (2 - b) * GROWN + 2 - c if flipped else b * GROWN + c
                at = (3 * b + c) * 128
                stacked[p * PITCH : (p + 1) * PITCH, at : at + 128] = grid[
                    p * IN_PITCH + step : p * IN_PITCH + step + PITCH, :
                ].astype(BF)


def own_lines(grid, at):
    return jnp.concatenate([grid[at : at + TILE, :], grid[at + GROWN : at + GROWN + TILE, :]], 0)


def stack_own(n_planes, pitch, skip, grid, stacked):
    for p in range(n_planes):
        for y in range(0, TILE, 2):
            to = p * FACE + y * TILE
            for b in range(3):
                for c in range(3):
                    at = p * pitch + (y + skip + 2 - b) * GROWN + skip + 2 - c
                    stacked[to : to + 2 * TILE, (3 * b + c) * 128 : (3 * b + c + 1) * 128] = (
                        own_lines(grid, at).astype(BF)
                    )


def emit(core, at, value, kept, sent):
    half = value.shape[0] // 2
    columns = slice(at, at + value.shape[1])

    @pl.when(core == 0)
    def _():
        kept[:, columns] = value[:half]
        sent[:, columns] = value[half:].astype(BF)

    @pl.when(core == 1)
    def _():
        kept[:, columns] = value[half:]
        sent[:, columns] = value[:half].astype(BF)


def marked(planes, mask_rows, marks3, z_even, z_odd):
    tail = 4 * planes * GROWN
    swapped = parity(1) == 0

    def mark(by, bz, e):
        at = by * mask_rows + e
        if bz == 1:
            return marks3[at : at + 1, :].astype(F32)
        one = z_even[tail + at : tail + at + 1, :].astype(F32)
        two = z_odd[tail + at : tail + at + 1, :].astype(F32)
        return jnp.where(swapped, two, one) if bz == 0 else jnp.where(swapped, one, two)

    return mark


def spans(rows, ends):
    row = lax.broadcasted_iota(jnp.int32, (rows, 128), 0)
    line = row // GROWN
    depth = row - line * GROWN
    return [(line >= lo) & (line <= hi) for lo, hi in ends], [
        (depth >= lo) & (depth <= hi) for lo, hi in ends
    ]


def pad_terms(*refs):
    used = TAPS * 128
    for ref in refs:
        if ref.shape[1] > used:
            ref[:, used:] = jnp.zeros((ref.shape[0], ref.shape[1] - used), ref.dtype)


def forward(
    planes, deep, mask_rows,
    tall_in, tall_g, marks3, z_even, z_odd, w1_rows,
    kept, sent, act, grid_g,
    grid_in, st_in, st_own, hidden,
):
    core = lax.axis_index("dp")
    size_x = planes - 4 * deep
    n_in = size_x + 2 + 2 * deep
    n_out = size_x + 2 * deep
    third = 9 * 128
    spread(planes, 1 - deep, 0, tall_in, z_even, z_odd, grid_in)
    stack(n_in, grid_in, st_in, False)
    rows = n_out * PITCH
    total = dot(st_in[0:rows, :], w1_rows[0:third, :])
    for a in (1, 2):
        total = total + dot(
            st_in[a * PITCH : a * PITCH + rows, :], w1_rows[a * third : (a + 1) * third, :]
        )
    act[...] = total
    spread(planes, 1 - deep, 1, tall_g, z_even, z_odd, grid_g)
    stack_own(n_in, IN_PITCH, 1, grid_g, st_own)
    for p in range(size_x):
        at = mask_rows + p + 2 * deep
        keep = marks3[at : at + 1, :].astype(F32)
        for y in range(0, TILE, 2):
            pre = own_lines(act, (p + deep) * PITCH + (y + 1) * GROWN + 1)
            to = p * FACE + y * TILE
            hidden[to : to + 2 * TILE, :] = pre * jax.nn.sigmoid(pre) * keep
    hid_t = hidden[...].T.astype(BF)
    rows = size_x * FACE
    for a in range(3):
        at = (deep + 2 - a) * FACE
        part = dot(hid_t, st_own[at : at + rows, :]) * unscale
        emit(core, a * third, part, kept, sent)
    pad_terms(kept, sent)


def backward(
    planes, deep, mask_rows, tile_of,
    grid_g, act, inp, marks3, z_even, z_odd, w2_wide,
    kept, sent, st_own,
    st_g, pg,
):
    core = lax.axis_index("dp")
    size_x = planes - 4 * deep
    n_in = size_x + 2 + 2 * deep
    n_out = size_x + 2 * deep
    third = 9 * 128
    mark = marked(planes, mask_rows, marks3, z_even, z_odd)
    in_line, in_depth = spans(PITCH, ((0, 0), (1, TILE), (RIM - 1, RIM - 1)))
    stack(n_in, grid_g, st_g, True)
    rows = n_out * PITCH
    back = jnp.zeros((rows, 128), F32)
    for a in range(3):
        at = (2 - a) * PITCH
        back = back + dot_t(st_g[at : at + rows, :], w2_wide[:, a * third : (a + 1) * third])
    if not deep:
        for at in (0, (size_x + 1) * PITCH):
            pg[at : at + PITCH, :] = jnp.zeros((PITCH, 128), F32)
    tile, keep = None, None
    for p in range(n_out):
        if tile_of(p + deep) != tile:
            tile, keep = tile_of(p + deep), jnp.zeros((PITCH, 128), F32)
            for by in range(3):
                for bz in range(3):
                    keep = jnp.where(in_line[by] & in_depth[bz], mark(by, bz, p + deep), keep)
        pre = act[p * PITCH : (p + 1) * PITCH, :]
        sigma = jax.nn.sigmoid(pre)
        grad = back[p * PITCH : (p + 1) * PITCH] * sigma * (1.0 + pre * (1.0 - sigma))
        at = (p + 1 - deep) * PITCH
        pg[at : at + PITCH, :] = (grad * keep).astype(BF).astype(F32)
    stack_own(size_x + 2, PITCH, 0, pg, st_own)
    rows = size_x * FACE
    top = 2 * deep * FACE
    in_t = inp[top : top + rows, :].astype(F32).T.astype(BF)
    for a in range(3):
        at = (2 - a) * FACE
        part = dot(in_t, st_own[at : at + rows, :]) * unscale
        emit(core, a * third, part, kept, sent)
    pad_terms(kept, sent)


def last(planes, deep, mask_rows, st_own, grads, marks3, w1_wide, result):
    size_x = planes - 4 * deep
    third = 9 * 128
    rows = size_x * FACE
    total = jnp.zeros((rows, 128), F32)
    for a in range(3):
        at = (2 - a) * FACE
        total = total + dot_t(st_own[at : at + rows, :], w1_wide[:, a * third : (a + 1) * third])
    for p in range(size_x):
        e = p + 2 * deep
        m = marks3[mask_rows + e : mask_rows + e + 1, :].astype(F32)
        own = slice(p * FACE, (p + 1) * FACE)
        summed = (grads[e * FACE : (e + 1) * FACE, :].astype(F32) + total[own]) * m
        result[own, :] = summed.astype(BF)


def swap(value, axis, bits):
    count = lax.axis_size(axis)
    return lax.ppermute(value, axis, [(source, source ^ bits) for source in range(count)])


def split_rows(parts, kept, got, own, *sent):
    me = lax.axis_index("blk") % INNER
    rows = own.shape[0]
    for k in range(parts):
        at = pl.ds(pl.multiple_of((me ^ k) * rows, rows), rows)
        value = kept[at, :] + got[at, :].astype(F32)
        if k == 0:
            own[...] = value
        else:
            sent[k - 1][...] = value.astype(BF)


def split_columns(parts, *refs):
    kept, got, own, sent = refs[0], refs[1:INNER], refs[INNER], refs[INNER + 1 :]
    me = lax.axis_index("blk") // INNER
    columns = own.shape[1]
    for k in range(parts):
        at = pl.ds(pl.multiple_of((me ^ k) * columns, 128), columns)
        value = kept[:, at]
        for ref in got:
            value = value + ref[:, at].astype(F32)
        if k == 0:
            own[...] = value
        else:
            sent[k - 1][...] = value.astype(BF)


def add_pair(one, two, out):
    out[...] = (one[...].astype(F32) + two[...].astype(F32)).astype(BF)


def add_all(parts, *refs):
    value = refs[0][...]
    for ref in refs[1:parts]:
        value = value + ref[...].astype(F32)
    refs[parts][...] = value.astype(BF)


def join_columns(parts, *refs):
    me = lax.axis_index("blk") // INNER
    out = refs[parts]
    columns = refs[0].shape[1]
    for k in range(parts):
        out[:, pl.ds(pl.multiple_of((me ^ k) * columns, 128), columns)] = refs[k][...]


def join_rows(parts, *refs):
    me = lax.axis_index("blk") % INNER
    out = refs[parts]
    rows = refs[0].shape[0]
    for k in range(parts):
        out[pl.ds(pl.multiple_of((me ^ k) * rows, rows), rows), :] = refs[k][...]


def finish(own, other, out):
    core = lax.axis_index("dp")
    half = own.shape[0]

    def write(low, high):
        for at, ref in ((0, low), (half, high)):
            for tap in range(TAPS):
                out[pl.ds(at * TAPS + tap, half, stride=TAPS), :] = ref[
                    :, tap * 128 : (tap + 1) * 128
                ].astype(F32)

    @pl.when(core == 0)
    def _():
        write(own, other)

    @pl.when(core == 1)
    def _():
        write(other, own)


def after(value, *others):
    return lax.optimization_barrier((value, *others))[0]


def near(values):
    return [swap(v, "blk", k + 1) for k, v in enumerate(values)]


def far(values):
    return [swap(v, "blk", INNER * (k + 1)) for k, v in enumerate(values)]


def split_stage(kept, got):
    half, columns = kept.shape
    rows = half // INNER
    return call(
        functools.partial(split_rows, INNER),
        [shape((rows, columns), F32)] + [shape((rows, columns), BF)] * (INNER - 1),
        [kept, got],
    )


def sum_stage(own, gots):
    parts = len(gots) + 1
    return call(functools.partial(add_all, parts), [shape(own.shape, BF)], [own] + gots)[0]


def pair_stage(value, got):
    return call(add_pair, [shape(value.shape, BF)], [value, got])[0]


def back_stage(wide, gots):
    rows, columns = wide.shape
    return call(
        functools.partial(join_rows, INNER), [shape((rows * INNER, columns), BF)], [wide] + gots
    )[0]


def wide_sum(own, gots):
    outer = lax.axis_size("blk") // INNER
    rows, columns = own.shape
    part = columns // outer
    own, *send = call(
        functools.partial(split_columns, outer),
        [shape((rows, part), F32)] + [shape((rows, part), BF)] * (outer - 1),
        [own] + gots,
    )
    done = sum_stage(own, far(send))
    return call(
        functools.partial(join_columns, outer),
        [shape((rows, columns), BF)],
        [done] + far([done] * (outer - 1)),
    )[0]


def finished(mine, other):
    return call(finish, [shape((2 * mine.shape[0] * TAPS, 128), F32)], [mine, other])[0]


def reduce_rest(own, send):
    outer = lax.axis_size("blk") // INNER
    gots = near(send)
    if outer > 4:
        value = wide_sum(own, gots)
    else:
        value = sum_stage(own, gots)
        step = 1
        while step < outer:
            value = pair_stage(value, swap(value, "blk", INNER * step))
            step *= 2
    mine = back_stage(value, near([value] * (INNER - 1)))
    return finished(mine, swap(mine, "dp", 1))


def on_device(features, tile_mask, w_first, w_second, cotangent):
    width = features.shape[2]
    tiles = tile_mask.shape[1]
    size_x = tiles * TILE
    count = lax.axis_size("blk")
    deep = 1 if count // 16 > 1 else 0
    planes = size_x + 4 * deep
    feat, cot, mask = features[0], cotangent[0], tile_mask

    def along(value, stride, extent, toward):
        pairs = [
            (s, s + toward * stride)
            for s in range(count)
            if 0 <= s // stride % extent + toward < extent
        ]
        return lax.ppermute(value, "blk", pairs)

    if deep:
        wide_mask = jnp.broadcast_to(
            jnp.repeat(tile_mask[0], TILE)[:, None], (size_x, width)
        ).astype(BF)
        keep = jnp.repeat(wide_mask, FACE, axis=0)
        feat, cot = feat * keep, cot * keep
        slab = 2 * FACE
        up = jnp.concatenate([feat[-slab:], cot[-slab:], wide_mask[-16:]], 0)
        down = jnp.concatenate([feat[:slab], cot[:slab], wide_mask[:16]], 0)
        before = along(up, 16, count // 16, 1)
        behind = along(down, 16, count // 16, -1)
        feat = jnp.concatenate([before[:slab], feat, behind[:slab]], 0)
        cot = jnp.concatenate([before[slab : 2 * slab], cot, behind[slab : 2 * slab]], 0)
        ends = [v[2 * slab : 2 * slab + 1, :1].astype(jnp.int32) for v in (before, behind)]
        mask = jnp.concatenate([ends[0], tile_mask, ends[1]], 1)

    def tile_of(e):
        if not deep:
            return e // TILE
        return (e + TILE - 2) // TILE

    def beside(one, two, stride, extent):
        pairs = ([], [])
        for s in range(count):
            place = s // stride % extent
            if place + 1 < extent:
                pairs[place % 2].extend([(s, s + stride), (s + stride, s)])
        return lax.ppermute(one, "blk", pairs[0]), lax.ppermute(two, "blk", pairs[1])

    mask_rows = -(-planes // 16) * 16
    side = 4 * planes * TILE + mask_rows
    cells = planes * FACE
    inp, grads, marks, even, odd = call(
        functools.partial(pack_rows, planes, tile_of, mask_rows),
        [shape((cells, width), BF)] * 2
        + [shape((mask_rows, width), BF)]
        + [shape((side, width), BF)] * 2,
        [mask, feat, cot],
        scratch=[pltpu.VMEM((2, cells, width), BF), pltpu.SemaphoreType.DMA((2,))],
        smem=(0,),
        away=(1, 2),
    )
    y_even, y_odd = beside(even, odd, 4, 4)
    w1_rows, w1_wide, w2_wide = call(
        lay_weights,
        [shape((TAPS * width, width), BF)] + [shape((width, TAPS * width), BF)] * 2,
        [w_first, w_second],
        scratch=[
            pltpu.VMEM((2, TAPS * width, width), BF),
            pltpu.VMEM((TAPS * width, width), F32),
            pltpu.SemaphoreType.DMA((2,)),
        ],
        away=(0, 1),
    )
    edge = 4 * planes * GROWN + 3 * mask_rows
    even, odd, tall_in, tall_g, marks3 = call(
        functools.partial(pack_depth, planes, mask_rows),
        [shape((edge, width), BF)] * 2
        + [shape((planes * GROWN * TILE, width), BF)] * 2
        + [shape((3 * mask_rows, width), BF)],
        [inp, grads, marks, y_even, y_odd],
        scratch=[pltpu.VMEM((planes * GROWN * TILE, width), F32)],
    )
    z_even, z_odd = beside(even, odd, 1, 4)
    outer = count // INNER
    columns = TAPS * width if outer <= 4 else -(-TAPS // outer) * outer * width
    n_in = size_x + 2 + 2 * deep
    n_out = size_x + 2 * deep
    half = width // 2
    work = 2 * size_x * FACE * TAPS * width * width
    terms = [shape((half, columns), F32), shape((half, columns), BF)]
    kept_a, sent_a, act, grid_g = call(
        functools.partial(forward, planes, deep, mask_rows),
        terms + [shape((n_out * PITCH, width), F32), shape((n_in * IN_PITCH, width), F32)],
        [tall_in, tall_g, marks3, z_even, z_odd, w1_rows],
        scratch=[
            pltpu.VMEM((n_in * IN_PITCH, width), F32),
            pltpu.VMEM((n_in * PITCH, 9 * width), BF),
            pltpu.VMEM((n_in * FACE, 9 * width), BF),
            pltpu.VMEM((size_x * FACE, width), F32),
        ],
        flops=2 * work,
    )
    own_a, *send_a = split_stage(kept_a, swap(sent_a, "dp", 1))
    act = after(act, own_a)
    kept_b, sent_b, st_own = call(
        functools.partial(backward, planes, deep, mask_rows, tile_of),
        terms + [shape(((size_x + 2) * FACE, 9 * width), BF)],
        [grid_g, act, inp, marks3, z_even, z_odd, w2_wide],
        scratch=[
            pltpu.VMEM((n_in * PITCH, 9 * width), BF),
            pltpu.VMEM(((size_x + 2) * PITCH, width), F32),
        ],
        flops=2 * work,
    )
    own_b, *send_b = split_stage(kept_b, swap(sent_b, "dp", 1))
    st_own = after(st_own, own_b)
    (result,) = call(
        functools.partial(last, planes, deep, mask_rows),
        [shape((size_x * FACE, width), BF)],
        [st_own, grads, marks3, w1_wide],
        flops=work,
    )
    grad_second = reduce_rest(own_a, send_a)
    grad_first = reduce_rest(own_b, send_b)
    return (grad_first, grad_second, result[None])


def solution(mesh):
    in_specs = (P("dp", "blk", None), P("dp", "blk"), P(), P(), P("dp", "blk", None))
    out_specs = (P(), P(), P("dp", "blk", None))
    return jax.shard_map(
        on_device, mesh=mesh, in_specs=in_specs, out_specs=out_specs, check_vma=False
    )
```

```python
import functools

import jax
import jax.numpy as jnp
from jax import lax
from jax.experimental import pallas as pl
from jax.experimental.pallas import tpu as pltpu
from jax.sharding import PartitionSpec as P

TILE = 8
FACE = TILE * TILE
RIM = TILE + 2
GROWN = TILE + 4
IN_PITCH = 160
PITCH = 128
INNER_PITCH = 80
OUTER_PITCH = 48
EDGE = 24
SPARE = 16
TAPS = 27
INNER = 4
BF = jnp.bfloat16
F32 = jnp.float32
unscale = 1.0 / 512.0
LIMIT = 24 * 2**20

VM = pl.BlockSpec(memory_space=pltpu.VMEM)
SM = pl.BlockSpec(memory_space=pltpu.SMEM)


def call(body, outs, ins, scratch=(), smem=(), flops=0):
    specs = [SM if i in smem else VM for i in range(len(ins))]
    moved = sum(a.size * a.dtype.itemsize for a in list(ins) + list(outs))
    return pl.pallas_call(
        body,
        out_shape=list(outs),
        in_specs=specs,
        out_specs=[VM] * len(outs),
        scratch_shapes=list(scratch),
        compiler_params=pltpu.CompilerParams(vmem_limit_bytes=LIMIT),
        cost_estimate=pl.CostEstimate(flops=flops, bytes_accessed=moved, transcendentals=0),
    )(*ins)


def shape(dims, kind):
    return jax.ShapeDtypeStruct(dims, kind)


def parity(stride):
    return lax.axis_index("blk") // stride % 2


def pack_depth(planes, tile_of, mask_rows, mask, feat, cot, inp, grads, marks, even, odd, wide):
    lines = planes * TILE
    row = lax.broadcasted_iota(jnp.int32, (mask_rows, 128), 0)
    filled = jnp.zeros((mask_rows, 128), F32)
    kept_of = [mask[0, tile_of(e)].astype(F32) for e in range(planes)]
    for e in range(planes):
        filled = jnp.where(row == e, kept_of[e], filled)
    filled = filled.astype(BF)
    marks[...] = filled
    even[4 * lines :, :] = filled
    odd[4 * lines :, :] = filled
    side = parity(1)
    for at, (src, dst) in enumerate(((feat, inp), (cot, grads))):
        for e in range(planes):
            rows = slice(e * FACE, (e + 1) * FACE)
            kept = src[rows, :].astype(F32) * kept_of[e]
            wide[rows, :] = kept
            dst[rows, :] = kept.astype(BF)

        def faces(lo, hi, at=at):
            for k in range(2):
                to = slice((at * 2 + k) * lines, (at * 2 + k + 1) * lines)
                lo[to, :] = wide[pl.ds(k, lines, stride=TILE), :].astype(BF)
                hi[to, :] = wide[pl.ds(TILE - 2 + k, lines, stride=TILE), :].astype(BF)

        @pl.when(side == 0)
        def _():
            faces(odd, even)

        @pl.when(side == 1)
        def _():
            faces(even, odd)


def pack_lines(
    planes, mask_rows, inp, grads, marks, z_even, z_odd, even, odd, deep_in, deep_g, marks3
):
    lines = planes * TILE
    plane = TILE * GROWN
    edge = 2 * GROWN
    swapped = parity(1) == 0

    def sides(rows):
        one, two = z_even[rows, :].astype(F32), z_odd[rows, :].astype(F32)
        return jnp.where(swapped, two, one), jnp.where(swapped, one, two)

    left, right = sides(slice(4 * lines, 4 * lines + mask_rows))
    for at, rows in enumerate((left, marks[...].astype(F32), right)):
        marks3[at * mask_rows : (at + 1) * mask_rows, :] = rows.astype(BF)
    for ref in (even, odd):
        ref[4 * planes * GROWN :, :] = marks3[...]
    side = parity(4)
    for at, (src, dst) in enumerate(((inp, deep_in), (grads, deep_g))):
        dst[lines * GROWN :, :] = jnp.zeros((SPARE, 128), F32)
        for pair in range(0, lines, 2):
            cells = src[pair * TILE : (pair + 2) * TILE, :].astype(F32)
            top = pair * GROWN + 2
            dst[top : top + TILE, :] = cells[:TILE]
            dst[top + GROWN : top + GROWN + TILE, :] = cells[TILE:]
        for k in range(2):
            left, right = sides(slice((at * 2 + k) * lines, (at * 2 + k + 1) * lines))
            dst[pl.ds(k, lines, stride=GROWN), :] = left
            dst[pl.ds(2 + TILE + k, lines, stride=GROWN), :] = right

        def faces(lo, hi, at=at, dst=dst):
            for e in range(0, planes, 2):
                to = slice((at * planes + e) * edge, (at * planes + e + 2) * edge)
                for ref, start in ((lo, 0), (hi, plane - edge)):
                    ref[to, :] = jnp.concatenate(
                        [
                            dst[p * plane + start : p * plane + start + edge, :]
                            for p in (e, e + 1)
                        ],
                        0,
                    ).astype(BF)

        @pl.when(side == 0)
        def _():
            faces(odd, even)

        @pl.when(side == 1)
        def _():
            faces(even, odd)


def lay_weights(src, *refs):
    *outs, wide = refs
    wide[...] = src[...].astype(F32)
    for tap in range(TAPS):
        a, bc = tap // 9, tap % 9
        block = wide[pl.ds(tap, 128, stride=TAPS), :].astype(BF)
        outs[0][a * 128 : (a + 1) * 128, bc * 128 : (bc + 1) * 128] = block
        for out in outs[1:]:
            out[bc * 128 : (bc + 1) * 128, a * 128 : (a + 1) * 128] = block


def dot(a, b):
    return lax.dot_general(a, b, (((1,), (0,)), ((), ())), preferred_element_type=F32)


def dot_t(a, b):
    return lax.dot_general(a, b, (((1,), (1,)), ((), ())), preferred_element_type=F32)


def spread(planes, first_plane, at, deep, y_even, y_odd, grid):
    plane = TILE * GROWN
    edge = 2 * GROWN
    swapped = parity(4) == 0
    used = edge + plane + edge
    for p in range(grid.shape[0] // IN_PITCH):
        top = p * IN_PITCH
        if first_plane <= p < first_plane + planes:
            grid[top + used : top + IN_PITCH, :] = jnp.zeros((IN_PITCH - used, 128), F32)
            e = p - first_plane
            grid[top + edge : top + edge + plane, :] = deep[e * plane : (e + 1) * plane, :]
        else:
            grid[top : top + IN_PITCH, :] = jnp.zeros((IN_PITCH, 128), F32)
    for e in range(0, planes, 2):
        rows = slice((at * planes + e) * edge, (at * planes + e + 2) * edge)
        one, two = y_even[rows, :].astype(F32), y_odd[rows, :].astype(F32)
        low, high = jnp.where(swapped, two, one), jnp.where(swapped, one, two)
        for k in range(2):
            top = (first_plane + e + k) * IN_PITCH
            grid[top : top + edge, :] = low[k * edge : (k + 1) * edge]
            grid[top + edge + plane : top + used, :] = high[k * edge : (k + 1) * edge]


def stack(planes, first, pitch, parts, grid, stacked, out_pitch, flipped):
    for j in range(planes):
        for b in range(3):
            for c in range(3):
                step = (2 - b) * GROWN + 2 - c if flipped else b * GROWN + c
                at = (3 * b + c) * 128
                cells = [
                    grid[(j + first) * pitch + lo + step : (j + first) * pitch + lo + step + n, :]
                    for lo, n in parts
                ]
                cells = cells[0] if len(cells) == 1 else jnp.concatenate(cells, 0)
                to = j * out_pitch
                stacked[to : to + out_pitch, at : at + 128] = cells.astype(BF)


def add_planes(planes, pitch, shift, pair, single, p):
    total = jnp.zeros((pitch, 128), F32)
    for a, (ref, at) in enumerate(((pair, 0), (pair, 128), (single, 0))):
        j = p - shift(a)
        if 0 <= j < planes:
            total = total + ref[j * pitch : (j + 1) * pitch, at : at + 128]
    return total


def own_lines(grid, at):
    return jnp.concatenate([grid[at : at + TILE, :], grid[at + GROWN : at + GROWN + TILE, :]], 0)


def stack_own(planes, first, pitch, skip, grid, stacked):
    for p in range(planes):
        for y in range(0, TILE, 2):
            to = p * FACE + y * TILE
            for b in range(3):
                for c in range(3):
                    at = (p + first) * pitch + (y + skip + 2 - b) * GROWN + skip + 2 - c
                    stacked[to : to + 2 * TILE, (3 * b + c) * 128 : (3 * b + c + 1) * 128] = (
                        own_lines(grid, at).astype(BF)
                    )


def emit(core, at, value, kept, sent):
    half = value.shape[0] // 2
    columns = slice(at, at + value.shape[1])

    @pl.when(core == 0)
    def _():
        kept[:, columns] = value[:half]
        sent[:, columns] = value[half:].astype(BF)

    @pl.when(core == 1)
    def _():
        kept[:, columns] = value[half:]
        sent[:, columns] = value[:half].astype(BF)


def marked(planes, mask_rows, marks3, y_even, y_odd):
    tail = 4 * planes * GROWN
    swapped = parity(4) == 0

    def mark(by, bz, e):
        at = bz * mask_rows + e
        if by == 1:
            return marks3[at : at + 1, :].astype(F32)
        one = y_even[tail + at : tail + at + 1, :].astype(F32)
        two = y_odd[tail + at : tail + at + 1, :].astype(F32)
        return jnp.where(swapped, two, one) if by == 0 else jnp.where(swapped, one, two)

    return mark


def spans(rows, ends):
    row = lax.broadcasted_iota(jnp.int32, (rows, 128), 0)
    line = row // GROWN
    depth = row - line * GROWN
    return [(line >= lo) & (line <= hi) for lo, hi in ends], [
        (depth >= lo) & (depth <= hi) for lo, hi in ends
    ]


def pad_terms(*refs):
    used = TAPS * 128
    for ref in refs:
        if ref.shape[1] > used:
            ref[:, used:] = jnp.zeros((ref.shape[0], ref.shape[1] - used), ref.dtype)


def ahead(
    planes, deep,
    deep_in, deep_g, inp, w1_tall, w2_wide,
    act, back, in_t,
    stacked, pair, single, padded,
):
    size_x = planes - 4 * deep
    n_out = size_x + 2 * deep
    parts = ((0, INNER_PITCH),)
    plane = TILE * GROWN
    stack(planes, 0, plane, parts, deep_in, stacked, INNER_PITCH, False)
    pair[...] = dot(stacked[...], w1_tall[:, 0:256])
    single[...] = dot(stacked[...], w1_tall[:, 256:384])
    for p in range(n_out):
        act[p * INNER_PITCH : (p + 1) * INNER_PITCH, :] = add_planes(
            planes, INNER_PITCH, lambda a: 1 - deep - a, pair, single, p
        )
    stack(planes, 0, plane, parts, deep_g, stacked, INNER_PITCH, True)
    pair[...] = dot_t(stacked[...], w2_wide[0:256, :])
    single[...] = dot_t(stacked[...], w2_wide[256:384, :])
    for p in range(n_out):
        back[p * INNER_PITCH : (p + 1) * INNER_PITCH, :] = add_planes(
            planes, INNER_PITCH, lambda a: a - 1 - deep, pair, single, p
        )
    padded[...] = jnp.zeros_like(padded)
    top = (1 + deep) * FACE
    rows = size_x * FACE
    padded[top : top + rows, :] = inp[2 * deep * FACE : 2 * deep * FACE + rows, :].astype(F32)
    in_t[...] = padded[...].T.astype(BF)


def whole_plane(inner, outer, p):
    ends = outer[p * OUTER_PITCH : (p + 1) * OUTER_PITCH]
    middle = inner[p * INNER_PITCH : p * INNER_PITCH + PITCH - 2 * EDGE - TILE, :]
    rest = jnp.zeros((TILE, 128), F32)
    return jnp.concatenate([ends[:EDGE], middle, ends[EDGE:], rest], 0)


OUTER_PARTS = ((0, EDGE), (PITCH - EDGE - TILE, EDGE))


def correlate(turned_rows, stacked, columns):
    left = jnp.concatenate([turned_rows[:, a * FACE : a * FACE + columns] for a in range(3)], 0)
    return dot(left, stacked) * unscale


def forward(
    planes, deep, mask_rows,
    deep_in, deep_g, marks3, y_even, y_odd, inner, w1_tall,
    kept, sent, act, grid_g,
    grid_in, outer, pair, single, st_own, hidden,
):
    core = lax.axis_index("dp")
    size_x = planes - 4 * deep
    n_out = size_x + 2 * deep
    first = 1 - deep
    third = 9 * 128
    spread(planes, first, 0, deep_in, y_even, y_odd, grid_in)
    stack(planes, first, IN_PITCH, OUTER_PARTS, grid_in, outer, OUTER_PITCH, False)
    pair[...] = dot(outer[...], w1_tall[:, 0:256])
    single[...] = dot(outer[...], w1_tall[:, 256:384])
    for p in range(n_out):
        ends = add_planes(planes, OUTER_PITCH, lambda a: 1 - deep - a, pair, single, p)
        act[p * PITCH : (p + 1) * PITCH, :] = whole_plane(
            inner.at[p * INNER_PITCH : (p + 1) * INNER_PITCH, :], ends, 0
        )
    spread(planes, first, 1, deep_g, y_even, y_odd, grid_g)
    stack_own(planes, first, IN_PITCH, 1, grid_g, st_own)
    hidden[...] = jnp.zeros_like(hidden)
    for p in range(size_x):
        at = mask_rows + p + 2 * deep
        keep = marks3[at : at + 1, :].astype(F32)
        for y in range(0, TILE, 2):
            pre = own_lines(act, (p + deep) * PITCH + (y + 1) * GROWN + 1)
            to = (p + 1 + 2 * deep) * FACE + y * TILE
            hidden[to : to + 2 * TILE, :] = pre * jax.nn.sigmoid(pre) * keep
    part = correlate(hidden[...].T.astype(BF), st_own[...], planes * FACE)
    for a in range(3):
        emit(core, a * third, part[a * 128 : (a + 1) * 128], kept, sent)
    pad_terms(kept, sent)


def backward(
    planes, deep, mask_rows, tile_of,
    grid_g, act, inner, in_t, marks3, y_even, y_odd, w2_wide,
    kept, sent, st_own,
    outer, pair, single, pg,
):
    core = lax.axis_index("dp")
    size_x = planes - 4 * deep
    n_out = size_x + 2 * deep
    third = 9 * 128
    mark = marked(planes, mask_rows, marks3, y_even, y_odd)
    in_line, in_depth = spans(PITCH, ((0, 0), (1, TILE), (RIM - 1, RIM - 1)))
    stack(planes, 1 - deep, IN_PITCH, OUTER_PARTS, grid_g, outer, OUTER_PITCH, True)
    pair[...] = dot_t(outer[...], w2_wide[0:256, :])
    single[...] = dot_t(outer[...], w2_wide[256:384, :])
    tile, keep = None, None
    for p in range(n_out):
        if tile_of(p + deep) != tile:
            tile, keep = tile_of(p + deep), jnp.zeros((PITCH, 128), F32)
            for by in range(3):
                for bz in range(3):
                    keep = jnp.where(in_line[by] & in_depth[bz], mark(by, bz, p + deep), keep)
        ends = add_planes(planes, OUTER_PITCH, lambda a: a - 1 - deep, pair, single, p)
        back = whole_plane(inner.at[p * INNER_PITCH : (p + 1) * INNER_PITCH, :], ends, 0)
        pre = act[p * PITCH : (p + 1) * PITCH, :]
        sigma = jax.nn.sigmoid(pre)
        grad = back * sigma * (1.0 + pre * (1.0 - sigma))
        pg[p * PITCH : (p + 1) * PITCH, :] = (grad * keep).astype(BF).astype(F32)
    stack_own(n_out, 0, PITCH, 0, pg, st_own)
    part = correlate(in_t, st_own[...], n_out * FACE)
    for a in range(3):
        emit(core, a * third, part[a * 128 : (a + 1) * 128], kept, sent)
    pad_terms(kept, sent)


def last(planes, deep, mask_rows, st_own, grads, marks3, w1_wide, result, pair, single):
    size_x = planes - 4 * deep
    n_out = size_x + 2 * deep
    pair[...] = dot_t(st_own[...], w1_wide[0:256, :])
    single[...] = dot_t(st_own[...], w1_wide[256:384, :])
    for p in range(size_x):
        e = p + 2 * deep
        m = marks3[mask_rows + e : mask_rows + e + 1, :].astype(F32)
        total = add_planes(n_out, FACE, lambda a: a - 1 - deep, pair, single, p)
        summed = (grads[e * FACE : (e + 1) * FACE, :].astype(F32) + total) * m
        result[p * FACE : (p + 1) * FACE, :] = summed.astype(BF)


def swap(value, axis, bits):
    count = lax.axis_size(axis)
    return lax.ppermute(value, axis, [(source, source ^ bits) for source in range(count)])


def cross(value, bits):
    count = lax.axis_size("blk")
    pairs = [
        (core * count + s, core * count + (s ^ bit))
        for core, bit in enumerate(bits)
        for s in range(count)
    ]
    return lax.ppermute(value, ("dp", "blk"), pairs)


def turned(k):
    return {0: 0, 1: 1 + lax.axis_index("dp"), 2: 2 - lax.axis_index("dp"), 3: 3}[k]


def split_rows(parts, kept, got, own, *sent):
    me = lax.axis_index("blk") % INNER
    rows = own.shape[0]
    for k in range(parts):
        at = pl.ds(pl.multiple_of((me ^ turned(k)) * rows, rows), rows)
        value = kept[at, :] + got[at, :].astype(F32)
        if k == 0:
            own[...] = value
        else:
            sent[k - 1][...] = value.astype(BF)


def split_columns(parts, *refs):
    kept, got, own, sent = refs[0], refs[1:INNER], refs[INNER], refs[INNER + 1 :]
    me = lax.axis_index("blk") // INNER
    columns = own.shape[1]
    for k in range(parts):
        at = pl.ds(pl.multiple_of((me ^ k) * columns, 128), columns)
        value = kept[:, at]
        for ref in got:
            value = value + ref[:, at].astype(F32)
        if k == 0:
            own[...] = value
        else:
            sent[k - 1][...] = value.astype(BF)


def add_pair(one, two, out):
    out[...] = (one[...].astype(F32) + two[...].astype(F32)).astype(BF)


def add_all(parts, *refs):
    value = refs[0][...]
    for ref in refs[1:parts]:
        value = value + ref[...].astype(F32)
    refs[parts][...] = value.astype(BF)


def join_columns(parts, *refs):
    me = lax.axis_index("blk") // INNER
    out = refs[parts]
    columns = refs[0].shape[1]
    for k in range(parts):
        out[:, pl.ds(pl.multiple_of((me ^ k) * columns, 128), columns)] = refs[k][...]


def join_rows(parts, *refs):
    me = lax.axis_index("blk") % INNER
    out = refs[parts]
    rows = refs[0].shape[0]
    for k in range(parts):
        out[pl.ds(pl.multiple_of((me ^ turned(k)) * rows, rows), rows), :] = refs[k][...]


def finish(own, other, out):
    core = lax.axis_index("dp")
    half = own.shape[0]

    def write(low, high):
        for at, ref in ((0, low), (half, high)):
            for tap in range(TAPS):
                out[pl.ds(at * TAPS + tap, half, stride=TAPS), :] = ref[
                    :, tap * 128 : (tap + 1) * 128
                ].astype(F32)

    @pl.when(core == 0)
    def _():
        write(own, other)

    @pl.when(core == 1)
    def _():
        write(other, own)


def after(value, *others):
    return lax.optimization_barrier((value, *others))[0]


def near(values):
    return [cross(v, bits) for v, bits in zip(values, ((1, 2), (2, 1), (3, 3)))]


def far(values):
    return [swap(v, "blk", INNER * (k + 1)) for k, v in enumerate(values)]


def split_stage(kept, got):
    half, columns = kept.shape
    rows = half // INNER
    return call(
        functools.partial(split_rows, INNER),
        [shape((rows, columns), F32)] + [shape((rows, columns), BF)] * (INNER - 1),
        [kept, got],
    )


def sum_stage(own, gots):
    parts = len(gots) + 1
    return call(functools.partial(add_all, parts), [shape(own.shape, BF)], [own] + gots)[0]


def pair_stage(value, got):
    return call(add_pair, [shape(value.shape, BF)], [value, got])[0]


def back_stage(wide, gots):
    rows, columns = wide.shape
    return call(
        functools.partial(join_rows, INNER), [shape((rows * INNER, columns), BF)], [wide] + gots
    )[0]


def wide_sum(own, gots):
    outer = lax.axis_size("blk") // INNER
    rows, columns = own.shape
    part = columns // outer
    own, *send = call(
        functools.partial(split_columns, outer),
        [shape((rows, part), F32)] + [shape((rows, part), BF)] * (outer - 1),
        [own] + gots,
    )
    done = sum_stage(own, far(send))
    return call(
        functools.partial(join_columns, outer),
        [shape((rows, columns), BF)],
        [done] + far([done] * (outer - 1)),
    )[0]


def finished(mine, other):
    return call(finish, [shape((2 * mine.shape[0] * TAPS, 128), F32)], [mine, other])[0]


def across(owns, gots, beside):
    outer = lax.axis_size("blk") // INNER
    if outer > 4:
        one, two = [wide_sum(own, got) for own, got in zip(owns, gots)]
        return one, two, beside(one)
    one = sum_stage(owns[0], gots[0])
    two = sum_stage(after(owns[1], one), gots[1])
    steps = [INNER << k for k in range(outer.bit_length() - 1)]
    other = None
    for bits in zip(steps, reversed(steps)):
        got_one, got_two = cross(one, bits), cross(two, bits)
        one = pair_stage(after(one, two), got_one)
        if other is None:
            other = beside(one)
            two = after(two, other)
        two = pair_stage(after(two, one), got_two)
    return one, two, other


def on_device(features, tile_mask, w_first, w_second, cotangent):
    width = features.shape[2]
    tiles = tile_mask.shape[1]
    size_x = tiles * TILE
    count = lax.axis_size("blk")
    deep = 1 if count // 16 > 1 else 0
    planes = size_x + 4 * deep
    feat, cot, mask = features[0], cotangent[0], tile_mask

    def along(value, stride, extent, toward):
        pairs = [
            (s, s + toward * stride)
            for s in range(count)
            if 0 <= s // stride % extent + toward < extent
        ]
        return lax.ppermute(value, "blk", pairs)

    if deep:
        wide_mask = jnp.broadcast_to(
            jnp.repeat(tile_mask[0], TILE)[:, None], (size_x, width)
        ).astype(BF)
        keep = jnp.repeat(wide_mask, FACE, axis=0)
        feat, cot = feat * keep, cot * keep
        slab = 2 * FACE
        up = jnp.concatenate([feat[-slab:], cot[-slab:], wide_mask[-16:]], 0)
        down = jnp.concatenate([feat[:slab], cot[:slab], wide_mask[:16]], 0)
        before = along(up, 16, count // 16, 1)
        behind = along(down, 16, count // 16, -1)
        feat = jnp.concatenate([before[:slab], feat, behind[:slab]], 0)
        cot = jnp.concatenate([before[slab : 2 * slab], cot, behind[slab : 2 * slab]], 0)
        ends = [v[2 * slab : 2 * slab + 1, :1].astype(jnp.int32) for v in (before, behind)]
        mask = jnp.concatenate([ends[0], tile_mask, ends[1]], 1)

    def tile_of(e):
        if not deep:
            return e // TILE
        return (e + TILE - 2) // TILE

    def beside(one, two, stride, extent):
        pairs = ([], [])
        for s in range(count):
            place = s // stride % extent
            if place + 1 < extent:
                pairs[place % 2].extend([(s, s + stride), (s + stride, s)])
        return lax.ppermute(one, "blk", pairs[0]), lax.ppermute(two, "blk", pairs[1])

    mask_rows = -(-planes // 16) * 16
    lines = planes * TILE
    cells = planes * FACE
    side = 4 * lines + mask_rows
    inp, grads, marks, even, odd = call(
        functools.partial(pack_depth, planes, tile_of, mask_rows),
        [shape((cells, width), BF)] * 2
        + [shape((mask_rows, width), BF)]
        + [shape((side, width), BF)] * 2,
        [mask, feat, cot],
        scratch=[pltpu.VMEM((cells, width), F32)],
        smem=(0,),
    )
    z_even, z_odd = beside(even, odd, 1, 4)
    broad = shape((3 * width, 9 * width), BF)
    upright = shape((9 * width, 3 * width), BF)

    def laid(weight, outs):
        return call(lay_weights, outs, [weight], scratch=[pltpu.VMEM((TAPS * width, width), F32)])

    (w2_wide,) = laid(w_second, [broad])
    w1_wide, w1_tall = laid(w_first, [broad, upright])
    inp = after(inp, w2_wide, w1_wide)
    edge = 4 * planes * GROWN + 3 * mask_rows
    even, odd, deep_in, deep_g, marks3 = call(
        functools.partial(pack_lines, planes, mask_rows),
        [shape((edge, width), BF)] * 2
        + [shape((lines * GROWN + SPARE, width), F32)] * 2
        + [shape((3 * mask_rows, width), BF)],
        [inp, grads, marks, z_even, z_odd],
    )
    y_even, y_odd = beside(even, odd, 4, 4)
    outer = count // INNER
    columns = TAPS * width if outer <= 4 else -(-TAPS // outer) * outer * width
    n_in = size_x + 2 + 2 * deep
    n_out = size_x + 2 * deep
    half = width // 2
    work = 2 * size_x * FACE * TAPS * width * width
    terms = [shape((half, columns), F32), shape((half, columns), BF)]

    def parts_of(rows):
        return [pltpu.VMEM((rows, 2 * width), F32), pltpu.VMEM((rows, width), F32)]

    inner_act, inner_back, in_t = call(
        functools.partial(ahead, planes, deep),
        [shape((n_out * INNER_PITCH, width), F32)] * 2
        + [shape((width, (n_out + 2) * FACE), BF)],
        [deep_in, deep_g, inp, w1_tall, w2_wide],
        scratch=[pltpu.VMEM((planes * INNER_PITCH, 9 * width), BF)]
        + parts_of(planes * INNER_PITCH)
        + [pltpu.VMEM(((n_out + 2) * FACE, width), F32)],
        flops=2 * work,
    )
    marks3 = after(marks3, in_t)
    kept_a, sent_a, act, grid_g = call(
        functools.partial(forward, planes, deep, mask_rows),
        terms + [shape((n_out * PITCH, width), F32), shape((n_in * IN_PITCH, width), F32)],
        [deep_in, deep_g, marks3, y_even, y_odd, inner_act, w1_tall],
        scratch=[
            pltpu.VMEM((n_in * IN_PITCH, width), F32),
            pltpu.VMEM((planes * OUTER_PITCH, 9 * width), BF),
        ]
        + parts_of(planes * OUTER_PITCH)
        + [
            pltpu.VMEM((planes * FACE, 9 * width), BF),
            pltpu.VMEM(((planes + 2) * FACE, width), F32),
        ],
        flops=2 * work,
    )
    own_a, *send_a = split_stage(kept_a, swap(sent_a, "dp", 1))
    kept_b, sent_b, st_own = call(
        functools.partial(backward, planes, deep, mask_rows, tile_of),
        terms + [shape((n_out * FACE, 9 * width), BF)],
        [grid_g, act, inner_back, in_t, marks3, y_even, y_odd, w2_wide],
        scratch=[pltpu.VMEM((planes * OUTER_PITCH, 9 * width), BF)]
        + parts_of(planes * OUTER_PITCH)
        + [pltpu.VMEM((n_out * PITCH, width), F32)],
        flops=2 * work,
    )
    own_b, *send_b = split_stage(kept_b, swap(sent_b, "dp", 1))
    gots_a = near(send_a)
    gots_b = near(send_b)
    own_a = after(own_a, own_b)

    def last_part(cue):
        return call(
            functools.partial(last, planes, deep, mask_rows),
            [shape((size_x * FACE, width), BF)],
            [after(st_own, cue), grads, marks3, w1_wide],
            scratch=parts_of(n_out * FACE),
            flops=work,
        )[0]

    value_a, value_b, result = across((own_a, own_b), (gots_a, gots_b), last_part)
    gots_a = near([value_a] * (INNER - 1))
    gots_b = near([value_b] * (INNER - 1))
    mine_a = back_stage(value_a, gots_a)
    mine_b = back_stage(value_b, gots_b)
    grad_second = finished(mine_a, swap(mine_a, "dp", 1))
    grad_first = finished(mine_b, swap(mine_b, "dp", 1))
    return (grad_first, grad_second, result[None])


def solution(mesh):
    in_specs = (P("dp", "blk", None), P("dp", "blk"), P(), P(), P("dp", "blk", None))
    out_specs = (P(), P(), P("dp", "blk", None))
    return jax.shard_map(
        on_device, mesh=mesh, in_specs=in_specs, out_specs=out_specs, check_vma=False
    )
```

```python
import functools

import jax
import jax.numpy as jnp
from jax import lax
from jax.experimental import pallas as pl
from jax.experimental.pallas import tpu as pltpu
from jax.sharding import PartitionSpec as P

TILE = 8
FACE = TILE * TILE
RIM = TILE + 2
GROWN = TILE + 4
IN_PITCH = 160
PITCH = 128
INNER_PITCH = 80
OUTER_PITCH = 48
EDGE = 24
SPARE = 16
TAPS = 27
INNER = 4
BF = jnp.bfloat16
F32 = jnp.float32
unscale = 1.0 / 512.0
LIMIT = 24 * 2**20

VM = pl.BlockSpec(memory_space=pltpu.VMEM)
SM = pl.BlockSpec(memory_space=pltpu.SMEM)


def call(body, outs, ins, scratch=(), smem=(), flops=0):
    specs = [SM if i in smem else VM for i in range(len(ins))]
    moved = sum(a.size * a.dtype.itemsize for a in list(ins) + list(outs))
    return pl.pallas_call(
        body,
        out_shape=list(outs),
        in_specs=specs,
        out_specs=[VM] * len(outs),
        scratch_shapes=list(scratch),
        compiler_params=pltpu.CompilerParams(vmem_limit_bytes=LIMIT),
        cost_estimate=pl.CostEstimate(flops=flops, bytes_accessed=moved, transcendentals=0),
    )(*ins)


def shape(dims, kind):
    return jax.ShapeDtypeStruct(dims, kind)


def parity(stride):
    return lax.axis_index("blk") // stride % 2


def pack_depth(planes, tile_of, mask_rows, mask, both, inp, grads, marks, even, odd, wide):
    lines = planes * TILE
    row = lax.broadcasted_iota(jnp.int32, (mask_rows, 128), 0)
    filled = jnp.zeros((mask_rows, 128), F32)
    kept_of = [mask[0, tile_of(e)].astype(F32) for e in range(planes)]
    for e in range(planes):
        filled = jnp.where(row == e, kept_of[e], filled)
    filled = filled.astype(BF)
    marks[...] = filled
    even[4 * lines :, :] = filled
    odd[4 * lines :, :] = filled
    side = parity(1)
    for at, dst in enumerate((inp, grads)):
        for e in range(planes):
            rows = slice(e * FACE, (e + 1) * FACE)
            kept = both[at, rows, :].astype(F32) * kept_of[e]
            wide[rows, :] = kept
            dst[rows, :] = kept.astype(BF)

        def faces(lo, hi, at=at):
            for k in range(2):
                to = slice((at * 2 + k) * lines, (at * 2 + k + 1) * lines)
                lo[to, :] = wide[pl.ds(k, lines, stride=TILE), :].astype(BF)
                hi[to, :] = wide[pl.ds(TILE - 2 + k, lines, stride=TILE), :].astype(BF)

        @pl.when(side == 0)
        def _():
            faces(odd, even)

        @pl.when(side == 1)
        def _():
            faces(even, odd)


def pack_lines(
    planes, mask_rows, inp, grads, marks, z_odd, z_even, even, odd, deep_in, deep_g, marks3
):
    lines = planes * TILE
    plane = TILE * GROWN
    edge = 2 * GROWN
    swapped = parity(1) == 0

    def sides(rows):
        one, two = z_even[rows, :].astype(F32), z_odd[rows, :].astype(F32)
        return jnp.where(swapped, two, one), jnp.where(swapped, one, two)

    left, right = sides(slice(4 * lines, 4 * lines + mask_rows))
    for at, rows in enumerate((left, marks[...].astype(F32), right)):
        marks3[at * mask_rows : (at + 1) * mask_rows, :] = rows.astype(BF)
    for ref in (even, odd):
        ref[4 * planes * GROWN :, :] = marks3[...]
    side = parity(4)
    for at, (src, dst) in enumerate(((inp, deep_in), (grads, deep_g))):
        dst[lines * GROWN :, :] = jnp.zeros((SPARE, 128), F32)
        for pair in range(0, lines, 2):
            cells = src[pair * TILE : (pair + 2) * TILE, :].astype(F32)
            top = pair * GROWN + 2
            dst[top : top + TILE, :] = cells[:TILE]
            dst[top + GROWN : top + GROWN + TILE, :] = cells[TILE:]
        for k in range(2):
            left, right = sides(slice((at * 2 + k) * lines, (at * 2 + k + 1) * lines))
            dst[pl.ds(k, lines, stride=GROWN), :] = left
            dst[pl.ds(2 + TILE + k, lines, stride=GROWN), :] = right

        def faces(lo, hi, at=at, dst=dst):
            for e in range(0, planes, 2):
                to = slice((at * planes + e) * edge, (at * planes + e + 2) * edge)
                for ref, start in ((lo, 0), (hi, plane - edge)):
                    ref[to, :] = jnp.concatenate(
                        [
                            dst[p * plane + start : p * plane + start + edge, :]
                            for p in (e, e + 1)
                        ],
                        0,
                    ).astype(BF)

        @pl.when(side == 0)
        def _():
            faces(odd, even)

        @pl.when(side == 1)
        def _():
            faces(even, odd)


def lay_weights(src, *refs):
    *outs, wide = refs
    wide[...] = src[...].astype(F32)
    for tap in range(TAPS):
        a, bc = tap // 9, tap % 9
        block = wide[pl.ds(tap, 128, stride=TAPS), :].astype(BF)
        outs[0][a * 128 : (a + 1) * 128, bc * 128 : (bc + 1) * 128] = block
        for out in outs[1:]:
            out[bc * 128 : (bc + 1) * 128, a * 128 : (a + 1) * 128] = block


def dot(a, b):
    return lax.dot_general(a, b, (((1,), (0,)), ((), ())), preferred_element_type=F32)


def dot_t(a, b):
    return lax.dot_general(a, b, (((1,), (1,)), ((), ())), preferred_element_type=F32)


def spread(planes, first_plane, at, deep, y_even, y_odd, grid):
    plane = TILE * GROWN
    edge = 2 * GROWN
    swapped = parity(4) == 0
    used = edge + plane + edge
    for p in range(grid.shape[0] // IN_PITCH):
        top = p * IN_PITCH
        if first_plane <= p < first_plane + planes:
            grid[top + used : top + IN_PITCH, :] = jnp.zeros((IN_PITCH - used, 128), F32)
            e = p - first_plane
            grid[top + edge : top + edge + plane, :] = deep[e * plane : (e + 1) * plane, :]
        else:
            grid[top : top + IN_PITCH, :] = jnp.zeros((IN_PITCH, 128), F32)
    for e in range(0, planes, 2):
        rows = slice((at * planes + e) * edge, (at * planes + e + 2) * edge)
        one, two = y_even[rows, :].astype(F32), y_odd[rows, :].astype(F32)
        low, high = jnp.where(swapped, two, one), jnp.where(swapped, one, two)
        for k in range(2):
            top = (first_plane + e + k) * IN_PITCH
            grid[top : top + edge, :] = low[k * edge : (k + 1) * edge]
            grid[top + edge + plane : top + used, :] = high[k * edge : (k + 1) * edge]


def stack(planes, first, pitch, parts, grid, stacked, out_pitch, flipped):
    for j in range(planes):
        for b in range(3):
            for c in range(3):
                step = (2 - b) * GROWN + 2 - c if flipped else b * GROWN + c
                at = (3 * b + c) * 128
                cells = [
                    grid[(j + first) * pitch + lo + step : (j + first) * pitch + lo + step + n, :]
                    for lo, n in parts
                ]
                cells = cells[0] if len(cells) == 1 else jnp.concatenate(cells, 0)
                to = j * out_pitch
                stacked[to : to + out_pitch, at : at + 128] = cells.astype(BF)


def add_planes(planes, pitch, shift, pair, single, p):
    total = jnp.zeros((pitch, 128), F32)
    for a, (ref, at) in enumerate(((pair, 0), (pair, 128), (single, 0))):
        j = p - shift(a)
        if 0 <= j < planes:
            total = total + ref[j * pitch : (j + 1) * pitch, at : at + 128]
    return total


def own_lines(grid, at):
    return jnp.concatenate([grid[at : at + TILE, :], grid[at + GROWN : at + GROWN + TILE, :]], 0)


def stack_own(planes, first, pitch, skip, grid, stacked):
    for p in range(planes):
        for y in range(0, TILE, 2):
            to = p * FACE + y * TILE
            for b in range(3):
                for c in range(3):
                    at = (p + first) * pitch + (y + skip + 2 - b) * GROWN + skip + 2 - c
                    stacked[to : to + 2 * TILE, (3 * b + c) * 128 : (3 * b + c + 1) * 128] = (
                        own_lines(grid, at).astype(BF)
                    )


def emit(core, at, value, kept, sent):
    half = value.shape[0] // 2
    columns = slice(at, at + value.shape[1])

    @pl.when(core == 0)
    def _():
        kept[:, columns] = value[:half]
        sent[:, columns] = value[half:]

    @pl.when(core == 1)
    def _():
        kept[:, columns] = value[half:]
        sent[:, columns] = value[:half]


def marked(planes, mask_rows, marks3, y_even, y_odd):
    tail = 4 * planes * GROWN
    swapped = parity(4) == 0

    def mark(by, bz, e):
        at = bz * mask_rows + e
        if by == 1:
            return marks3[at : at + 1, :].astype(F32)
        one = y_even[tail + at : tail + at + 1, :].astype(F32)
        two = y_odd[tail + at : tail + at + 1, :].astype(F32)
        return jnp.where(swapped, two, one) if by == 0 else jnp.where(swapped, one, two)

    return mark


def spans(rows, ends):
    row = lax.broadcasted_iota(jnp.int32, (rows, 128), 0)
    line = row // GROWN
    depth = row - line * GROWN
    return [(line >= lo) & (line <= hi) for lo, hi in ends], [
        (depth >= lo) & (depth <= hi) for lo, hi in ends
    ]


def pad_terms(*refs):
    used = TAPS * 128
    for ref in refs:
        if ref.shape[1] > used:
            ref[:, used:] = jnp.zeros((ref.shape[0], ref.shape[1] - used), ref.dtype)


def ahead(
    planes, deep,
    deep_in, deep_g, inp, w1_tall, w2_wide,
    act, back, in_t,
    stacked, pair, single, padded,
):
    size_x = planes - 4 * deep
    n_out = size_x + 2 * deep
    parts = ((0, INNER_PITCH),)
    plane = TILE * GROWN
    stack(planes, 0, plane, parts, deep_in, stacked, INNER_PITCH, False)
    pair[...] = dot(stacked[...], w1_tall[:, 0:256])
    single[...] = dot(stacked[...], w1_tall[:, 256:384])
    for p in range(n_out):
        act[p * INNER_PITCH : (p + 1) * INNER_PITCH, :] = add_planes(
            planes, INNER_PITCH, lambda a: 1 - deep - a, pair, single, p
        )
    stack(planes, 0, plane, parts, deep_g, stacked, INNER_PITCH, True)
    pair[...] = dot_t(stacked[...], w2_wide[0:256, :])
    single[...] = dot_t(stacked[...], w2_wide[256:384, :])
    for p in range(n_out):
        back[p * INNER_PITCH : (p + 1) * INNER_PITCH, :] = add_planes(
            planes, INNER_PITCH, lambda a: a - 1 - deep, pair, single, p
        )
    padded[...] = jnp.zeros_like(padded)
    top = (1 + deep) * FACE
    rows = size_x * FACE
    padded[top : top + rows, :] = inp[2 * deep * FACE : 2 * deep * FACE + rows, :].astype(F32)
    in_t[...] = padded[...].T.astype(BF)


def whole_plane(inner, outer, p):
    ends = outer[p * OUTER_PITCH : (p + 1) * OUTER_PITCH]
    middle = inner[p * INNER_PITCH : p * INNER_PITCH + PITCH - 2 * EDGE - TILE, :]
    rest = jnp.zeros((TILE, 128), F32)
    return jnp.concatenate([ends[:EDGE], middle, ends[EDGE:], rest], 0)


OUTER_PARTS = ((0, EDGE), (PITCH - EDGE - TILE, EDGE))


def correlate(turned_rows, stacked, columns):
    left = jnp.concatenate([turned_rows[:, a * FACE : a * FACE + columns] for a in range(3)], 0)
    return dot(left, stacked) * unscale


def forward(
    planes, deep, mask_rows,
    deep_in, deep_g, marks3, y_odd, y_even, inner, w1_tall,
    kept, sent, act, grid_g,
    grid_in, outer, pair, single, st_own, hidden,
):
    core = lax.axis_index("dp")
    size_x = planes - 4 * deep
    n_out = size_x + 2 * deep
    first = 1 - deep
    third = 9 * 128
    spread(planes, first, 0, deep_in, y_even, y_odd, grid_in)
    stack(planes, first, IN_PITCH, OUTER_PARTS, grid_in, outer, OUTER_PITCH, False)
    pair[...] = dot(outer[...], w1_tall[:, 0:256])
    single[...] = dot(outer[...], w1_tall[:, 256:384])
    for p in range(n_out):
        ends = add_planes(planes, OUTER_PITCH, lambda a: 1 - deep - a, pair, single, p)
        act[p * PITCH : (p + 1) * PITCH, :] = whole_plane(
            inner.at[p * INNER_PITCH : (p + 1) * INNER_PITCH, :], ends, 0
        )
    spread(planes, first, 1, deep_g, y_even, y_odd, grid_g)
    stack_own(planes, first, IN_PITCH, 1, grid_g, st_own)
    hidden[...] = jnp.zeros_like(hidden)
    for p in range(size_x):
        at = mask_rows + p + 2 * deep
        keep = marks3[at : at + 1, :].astype(F32)
        for y in range(0, TILE, 2):
            pre = own_lines(act, (p + deep) * PITCH + (y + 1) * GROWN + 1)
            to = (p + 1 + 2 * deep) * FACE + y * TILE
            hidden[to : to + 2 * TILE, :] = pre * jax.nn.sigmoid(pre) * keep
    part = correlate(hidden[...].T.astype(BF), st_own[...], planes * FACE)
    for a in range(3):
        emit(core, a * third, part[a * 128 : (a + 1) * 128], kept, sent)
    pad_terms(kept, sent)


def backward(
    planes, deep, mask_rows, tile_of,
    grid_g, act, inner, in_t, marks3, y_even, y_odd, w2_wide,
    kept, sent, st_own,
    outer, pair, single, pg,
):
    core = lax.axis_index("dp")
    size_x = planes - 4 * deep
    n_out = size_x + 2 * deep
    third = 9 * 128
    mark = marked(planes, mask_rows, marks3, y_even, y_odd)
    in_line, in_depth = spans(PITCH, ((0, 0), (1, TILE), (RIM - 1, RIM - 1)))
    stack(planes, 1 - deep, IN_PITCH, OUTER_PARTS, grid_g, outer, OUTER_PITCH, True)
    pair[...] = dot_t(outer[...], w2_wide[0:256, :])
    single[...] = dot_t(outer[...], w2_wide[256:384, :])
    tile, keep = None, None
    for p in range(n_out):
        if tile_of(p + deep) != tile:
            tile, keep = tile_of(p + deep), jnp.zeros((PITCH, 128), F32)
            for by in range(3):
                for bz in range(3):
                    keep = jnp.where(in_line[by] & in_depth[bz], mark(by, bz, p + deep), keep)
        ends = add_planes(planes, OUTER_PITCH, lambda a: a - 1 - deep, pair, single, p)
        back = whole_plane(inner.at[p * INNER_PITCH : (p + 1) * INNER_PITCH, :], ends, 0)
        pre = act[p * PITCH : (p + 1) * PITCH, :]
        sigma = jax.nn.sigmoid(pre)
        grad = back * sigma * (1.0 + pre * (1.0 - sigma))
        pg[p * PITCH : (p + 1) * PITCH, :] = (grad * keep).astype(BF).astype(F32)
    stack_own(n_out, 0, PITCH, 0, pg, st_own)
    part = correlate(in_t, st_own[...], n_out * FACE)
    for a in range(3):
        emit(core, a * third, part[a * 128 : (a + 1) * 128], kept, sent)
    pad_terms(kept, sent)


def last(planes, deep, mask_rows, st_own, grads, marks3, w1_wide, result, pair, single):
    size_x = planes - 4 * deep
    n_out = size_x + 2 * deep
    pair[...] = dot_t(st_own[...], w1_wide[0:256, :])
    single[...] = dot_t(st_own[...], w1_wide[256:384, :])
    for p in range(size_x):
        e = p + 2 * deep
        m = marks3[mask_rows + e : mask_rows + e + 1, :].astype(F32)
        total = add_planes(n_out, FACE, lambda a: a - 1 - deep, pair, single, p)
        summed = (grads[e * FACE : (e + 1) * FACE, :].astype(F32) + total) * m
        result[p * FACE : (p + 1) * FACE, :] = summed.astype(BF)


def swap(value, axis, bits):
    count = lax.axis_size(axis)
    return lax.ppermute(value, axis, [(source, source ^ bits) for source in range(count)])


def cross(value, bits):
    count = lax.axis_size("blk")
    pairs = [
        (core * count + s, core * count + (s ^ bit))
        for core, bit in enumerate(bits)
        for s in range(count)
    ]
    return lax.ppermute(value, ("dp", "blk"), pairs)


def turned(k):
    return {0: 0, 1: 3, 2: 1 + lax.axis_index("dp"), 3: 2 - lax.axis_index("dp")}[k]


def split_rows(parts, kept, got, own, *sent):
    me = lax.axis_index("blk") % INNER
    rows = own.shape[0]
    for k in range(parts):
        at = pl.ds(pl.multiple_of((me ^ turned(k)) * rows, rows), rows)
        value = kept[at, :] + got[at, :].astype(F32)
        if k == 0:
            own[...] = value
        else:
            sent[k - 1][...] = value.astype(BF)


def split_columns(parts, *refs):
    kept, got, own, sent = refs[0], refs[1:INNER], refs[INNER], refs[INNER + 1 :]
    me = lax.axis_index("blk") // INNER
    columns = own.shape[1]
    for k in range(parts):
        at = pl.ds(pl.multiple_of((me ^ k) * columns, 128), columns)
        value = kept[:, at]
        for ref in got:
            value = value + ref[:, at].astype(F32)
        if k == 0:
            own[...] = value
        else:
            sent[k - 1][...] = value.astype(BF)


def add_pair(one, two, out):
    out[...] = (one[...].astype(F32) + two[...].astype(F32)).astype(BF)


def lay_rows(one, two, out, wide):
    rows = one.shape[0]
    for tap in range(TAPS):
        columns = slice(tap * 128, (tap + 1) * 128)
        total = one[:, columns].astype(F32) + two[:, columns].astype(F32)
        wide[pl.ds(tap, rows, stride=TAPS), :] = total
    out[...] = wide[...].astype(BF)


def add_all(parts, *refs):
    value = refs[0][...]
    for ref in refs[1:parts]:
        value = value + ref[...].astype(F32)
    refs[parts][...] = value.astype(BF)


def join_columns(parts, *refs):
    me = lax.axis_index("blk") // INNER
    out = refs[parts]
    columns = refs[0].shape[1]
    for k in range(parts):
        out[:, pl.ds(pl.multiple_of((me ^ k) * columns, 128), columns)] = refs[k][...]


def join_rows(parts, *refs):
    me = lax.axis_index("blk") % INNER
    out = refs[parts]
    rows = refs[0].shape[0]
    for k in range(parts):
        out[pl.ds(pl.multiple_of((me ^ turned(k)) * rows, rows), rows), :] = refs[k][...]


def finish(own, other, out):
    core = lax.axis_index("dp")
    half = own.shape[0]

    @pl.when(core == 0)
    def _():
        out[:half, :] = own[...].astype(F32)
        out[half:, :] = other[...].astype(F32)

    @pl.when(core == 1)
    def _():
        out[:half, :] = other[...].astype(F32)
        out[half:, :] = own[...].astype(F32)


def after(value, *others):
    return lax.optimization_barrier((value, *others))[0]


def near(values):
    return [cross(v, bits) for v, bits in zip(values, ((3, 3), (1, 2), (2, 1)))]


def far(values):
    return [swap(v, "blk", INNER * (k + 1)) for k, v in enumerate(values)]


def split_stage(kept, got):
    half, columns = kept.shape
    rows = half // INNER
    return call(
        functools.partial(split_rows, INNER),
        [shape((rows, columns), F32)] + [shape((rows, columns), BF)] * (INNER - 1),
        [kept, got],
    )


def sum_stage(own, gots):
    parts = len(gots) + 1
    return call(functools.partial(add_all, parts), [shape(own.shape, BF)], [own] + gots)[0]


def laid_pair(value, got):
    laid = (value.shape[0] * TAPS, 128)
    return call(lay_rows, [shape(laid, BF)], [value, got], scratch=[pltpu.VMEM(laid, F32)])[0]


def pair_stage(value, got):
    return call(add_pair, [shape(value.shape, BF)], [value, got])[0]


def back_stage(wide, gots):
    rows, columns = wide.shape
    return call(
        functools.partial(join_rows, INNER), [shape((rows * INNER, columns), BF)], [wide] + gots
    )[0]


def wide_sum(own, gots):
    outer = lax.axis_size("blk") // INNER
    rows, columns = own.shape
    part = columns // outer
    own, *send = call(
        functools.partial(split_columns, outer),
        [shape((rows, part), F32)] + [shape((rows, part), BF)] * (outer - 1),
        [own] + gots,
    )
    done = sum_stage(own, far(send))
    return call(
        functools.partial(join_columns, outer),
        [shape((rows, columns), BF)],
        [done] + far([done] * (outer - 1)),
    )[0]


def finished(mine, other):
    return call(finish, [shape((2 * mine.shape[0], 128), F32)], [mine, other])[0]


def across(owns, gots, beside):
    outer = lax.axis_size("blk") // INNER
    if outer > 4:
        sums = [wide_sum(own, got) for own, got in zip(owns, gots)]
        one, two = [laid_pair(value, jnp.zeros_like(value)) for value in sums]
        return one, two, beside(one)
    one = sum_stage(owns[0], gots[0])
    two = sum_stage(after(owns[1], one), gots[1])
    steps = [INNER << k for k in range(outer.bit_length() - 1)]
    other = None
    for bits in zip(steps, reversed(steps)):
        add = laid_pair if bits[0] == steps[-1] else pair_stage
        got_one, got_two = cross(one, bits), cross(two, bits)
        one = add(after(one, two), got_one)
        if other is None:
            other = beside(one)
            two = after(two, other)
        two = add(after(two, one), got_two)
    return one, two, other


def on_device(features, tile_mask, w_first, w_second, cotangent):
    width = features.shape[2]
    tiles = tile_mask.shape[1]
    size_x = tiles * TILE
    count = lax.axis_size("blk")
    deep = 1 if count // 16 > 1 else 0
    planes = size_x + 4 * deep
    feat, cot, mask = features[0], cotangent[0], tile_mask

    def along(value, stride, extent, toward):
        pairs = [
            (s, s + toward * stride)
            for s in range(count)
            if 0 <= s // stride % extent + toward < extent
        ]
        return lax.ppermute(value, "blk", pairs)

    if deep:
        wide_mask = jnp.broadcast_to(
            jnp.repeat(tile_mask[0], TILE)[:, None], (size_x, width)
        ).astype(BF)
        keep = jnp.repeat(wide_mask, FACE, axis=0)
        feat, cot = feat * keep, cot * keep
        slab = 2 * FACE
        up = jnp.concatenate([feat[-slab:], cot[-slab:], wide_mask[-16:]], 0)
        down = jnp.concatenate([feat[:slab], cot[:slab], wide_mask[:16]], 0)
        before = along(up, 16, count // 16, 1)
        behind = along(down, 16, count // 16, -1)
        feat = jnp.concatenate([before[:slab], feat, behind[:slab]], 0)
        cot = jnp.concatenate([before[slab : 2 * slab], cot, behind[slab : 2 * slab]], 0)
        ends = [v[2 * slab : 2 * slab + 1, :1].astype(jnp.int32) for v in (before, behind)]
        mask = jnp.concatenate([ends[0], tile_mask, ends[1]], 1)

    def tile_of(e):
        if not deep:
            return e // TILE
        return (e + TILE - 2) // TILE

    def beside(one, two, stride, extent):
        pairs = ([], [])
        for s in range(count):
            place = s // stride % extent
            if place + 1 < extent:
                pairs[place % 2].extend([(s, s + stride), (s + stride, s)])
        return lax.ppermute(one, "blk", pairs[0]), lax.ppermute(two, "blk", pairs[1])

    mask_rows = -(-planes // 16) * 16
    lines = planes * TILE
    cells = planes * FACE
    side = 4 * lines + mask_rows
    inp, grads, marks, even, odd = call(
        functools.partial(pack_depth, planes, tile_of, mask_rows),
        [shape((cells, width), BF)] * 2
        + [shape((mask_rows, width), BF)]
        + [shape((side, width), BF)] * 2,
        [mask, jnp.stack([feat, cot])],
        scratch=[pltpu.VMEM((cells, width), F32)],
        smem=(0,),
    )
    z_even, z_odd = beside(even, odd, 1, 4)
    broad = shape((3 * width, 9 * width), BF)
    upright = shape((9 * width, 3 * width), BF)

    def laid(weight, outs):
        return call(lay_weights, outs, [weight], scratch=[pltpu.VMEM((TAPS * width, width), F32)])

    (w2_wide,) = laid(w_second, [broad])
    w1_wide, w1_tall = laid(w_first, [broad, upright])
    inp = after(inp, w2_wide, w1_wide)
    edge = 4 * planes * GROWN + 3 * mask_rows
    even, odd, deep_in, deep_g, marks3 = call(
        functools.partial(pack_lines, planes, mask_rows),
        [shape((edge, width), BF)] * 2
        + [shape((lines * GROWN + SPARE, width), F32)] * 2
        + [shape((3 * mask_rows, width), BF)],
        [inp, grads, marks, z_odd, z_even],
    )
    y_even, y_odd = beside(even, odd, 4, 4)
    outer = count // INNER
    columns = TAPS * width if outer <= 4 else -(-TAPS // outer) * outer * width
    n_in = size_x + 2 + 2 * deep
    n_out = size_x + 2 * deep
    half = width // 2
    work = 2 * size_x * FACE * TAPS * width * width
    terms = [shape((half, columns), F32)] * 2

    def parts_of(rows):
        return [pltpu.VMEM((rows, 2 * width), F32), pltpu.VMEM((rows, width), F32)]

    inner_act, inner_back, in_t = call(
        functools.partial(ahead, planes, deep),
        [shape((n_out * INNER_PITCH, width), F32)] * 2
        + [shape((width, (n_out + 2) * FACE), BF)],
        [deep_in, deep_g, inp, w1_tall, w2_wide],
        scratch=[pltpu.VMEM((planes * INNER_PITCH, 9 * width), BF)]
        + parts_of(planes * INNER_PITCH)
        + [pltpu.VMEM(((n_out + 2) * FACE, width), F32)],
        flops=2 * work,
    )
    marks3 = after(marks3, in_t)
    kept_a, sent_a, act, grid_g = call(
        functools.partial(forward, planes, deep, mask_rows),
        terms + [shape((n_out * PITCH, width), F32), shape((n_in * IN_PITCH, width), F32)],
        [deep_in, deep_g, marks3, y_odd, y_even, inner_act, w1_tall],
        scratch=[
            pltpu.VMEM((n_in * IN_PITCH, width), F32),
            pltpu.VMEM((planes * OUTER_PITCH, 9 * width), BF),
        ]
        + parts_of(planes * OUTER_PITCH)
        + [
            pltpu.VMEM((planes * FACE, 9 * width), BF),
            pltpu.VMEM(((planes + 2) * FACE, width), F32),
        ],
        flops=2 * work,
    )
    own_a, *send_a = split_stage(kept_a, swap(sent_a, "dp", 1))
    kept_b, sent_b, st_own = call(
        functools.partial(backward, planes, deep, mask_rows, tile_of),
        terms + [shape((n_out * FACE, 9 * width), BF)],
        [grid_g, act, inner_back, in_t, marks3, y_even, y_odd, w2_wide],
        scratch=[pltpu.VMEM((planes * OUTER_PITCH, 9 * width), BF)]
        + parts_of(planes * OUTER_PITCH)
        + [pltpu.VMEM((n_out * PITCH, width), F32)],
        flops=2 * work,
    )
    own_b, *send_b = split_stage(kept_b, swap(sent_b, "dp", 1))
    gots_a = near(send_a)
    gots_b = near(send_b)
    own_a = after(own_a, own_b)

    def last_part(cue):
        return call(
            functools.partial(last, planes, deep, mask_rows),
            [shape((size_x * FACE, width), BF)],
            [after(st_own, cue), grads, marks3, w1_wide],
            scratch=parts_of(n_out * FACE),
            flops=work,
        )[0]

    value_a, value_b, result = across((own_a, own_b), (gots_a, gots_b), last_part)
    gots_a = near([value_a] * (INNER - 1))
    gots_b = near([value_b] * (INNER - 1))
    mine_a = back_stage(value_a, gots_a)
    mine_b = back_stage(value_b, gots_b)
    grad_second = finished(mine_a, swap(mine_a, "dp", 1))
    grad_first = finished(mine_b, swap(mine_b, "dp", 1))
    return (grad_first, grad_second, result[None])


def solution(mesh):
    in_specs = (P("dp", "blk", None), P("dp", "blk"), P(), P(), P("dp", "blk", None))
    out_specs = (P(), P(), P("dp", "blk", None))
    return jax.shard_map(
        on_device, mesh=mesh, in_specs=in_specs, out_specs=out_specs, check_vma=False
    )
```

```python
import functools

import jax
import jax.numpy as jnp
from jax import lax
from jax.experimental import pallas as pl
from jax.experimental.pallas import tpu as pltpu
from jax.sharding import PartitionSpec as P

TILE = 8
FACE = TILE * TILE
RIM = TILE + 2
GROWN = TILE + 4
IN_PITCH = 160
PITCH = 128
INNER_PITCH = 80
OUTER_PITCH = 48
EDGE = 24
SPARE = 16
TAPS = 27
INNER = 4
BF = jnp.bfloat16
F32 = jnp.float32
unscale = 1.0 / 512.0
LIMIT = 24 * 2**20

VM = pl.BlockSpec(memory_space=pltpu.VMEM)
SM = pl.BlockSpec(memory_space=pltpu.SMEM)


def call(body, outs, ins, scratch=(), smem=(), flops=0):
    specs = [SM if i in smem else VM for i in range(len(ins))]
    moved = sum(a.size * a.dtype.itemsize for a in list(ins) + list(outs))
    return pl.pallas_call(
        body,
        out_shape=list(outs),
        in_specs=specs,
        out_specs=[VM] * len(outs),
        scratch_shapes=list(scratch),
        compiler_params=pltpu.CompilerParams(vmem_limit_bytes=LIMIT),
        cost_estimate=pl.CostEstimate(flops=flops, bytes_accessed=moved, transcendentals=0),
    )(*ins)


def shape(dims, kind):
    return jax.ShapeDtypeStruct(dims, kind)


def parity(stride):
    return lax.axis_index("blk") // stride % 2


def pack_depth(planes, tile_of, mask_rows, mask, both, inp, grads, marks, even, odd, wide):
    lines = planes * TILE
    row = lax.broadcasted_iota(jnp.int32, (mask_rows, 128), 0)
    filled = jnp.zeros((mask_rows, 128), F32)
    kept_of = [mask[0, tile_of(e)].astype(F32) for e in range(planes)]
    for e in range(planes):
        filled = jnp.where(row == e, kept_of[e], filled)
    filled = filled.astype(BF)
    marks[...] = filled
    even[4 * lines :, :] = filled
    odd[4 * lines :, :] = filled
    side = parity(1)
    for at, dst in enumerate((inp, grads)):
        for e in range(planes):
            rows = slice(e * FACE, (e + 1) * FACE)
            kept = both[at, rows, :].astype(F32) * kept_of[e]
            wide[rows, :] = kept
            dst[rows, :] = kept.astype(BF)

        def faces(lo, hi, at=at):
            for k in range(2):
                to = slice((at * 2 + k) * lines, (at * 2 + k + 1) * lines)
                lo[to, :] = wide[pl.ds(k, lines, stride=TILE), :].astype(BF)
                hi[to, :] = wide[pl.ds(TILE - 2 + k, lines, stride=TILE), :].astype(BF)

        @pl.when(side == 0)
        def _():
            faces(odd, even)

        @pl.when(side == 1)
        def _():
            faces(even, odd)


def pack_lines(
    planes, mask_rows, inp, grads, marks, z_odd, z_even, even, odd, deep_in, deep_g, marks3
):
    lines = planes * TILE
    plane = TILE * GROWN
    edge = 2 * GROWN
    swapped = parity(1) == 0

    def sides(rows):
        one, two = z_even[rows, :].astype(F32), z_odd[rows, :].astype(F32)
        return jnp.where(swapped, two, one), jnp.where(swapped, one, two)

    left, right = sides(slice(4 * lines, 4 * lines + mask_rows))
    for at, rows in enumerate((left, marks[...].astype(F32), right)):
        marks3[at * mask_rows : (at + 1) * mask_rows, :] = rows.astype(BF)
    for ref in (even, odd):
        ref[4 * planes * GROWN :, :] = marks3[...]
    side = parity(4)
    for at, (src, dst) in enumerate(((inp, deep_in), (grads, deep_g))):
        dst[lines * GROWN :, :] = jnp.zeros((SPARE, 128), F32)
        for pair in range(0, lines, 2):
            cells = src[pair * TILE : (pair + 2) * TILE, :].astype(F32)
            top = pair * GROWN + 2
            dst[top : top + TILE, :] = cells[:TILE]
            dst[top + GROWN : top + GROWN + TILE, :] = cells[TILE:]
        for k in range(2):
            left, right = sides(slice((at * 2 + k) * lines, (at * 2 + k + 1) * lines))
            dst[pl.ds(k, lines, stride=GROWN), :] = left
            dst[pl.ds(2 + TILE + k, lines, stride=GROWN), :] = right

        def faces(lo, hi, at=at, dst=dst):
            for e in range(0, planes, 2):
                to = slice((at * planes + e) * edge, (at * planes + e + 2) * edge)
                for ref, start in ((lo, 0), (hi, plane - edge)):
                    ref[to, :] = jnp.concatenate(
                        [
                            dst[p * plane + start : p * plane + start + edge, :]
                            for p in (e, e + 1)
                        ],
                        0,
                    ).astype(BF)

        @pl.when(side == 0)
        def _():
            faces(odd, even)

        @pl.when(side == 1)
        def _():
            faces(even, odd)


def lay_weights(src, wide_1, tall_1, wide_2, rows):
    for at, (broad, upright) in enumerate(((wide_1, tall_1), (wide_2, None))):
        rows[...] = src[at].astype(F32)
        for tap in range(TAPS):
            a, bc = tap // 9, tap % 9
            block = rows[pl.ds(tap, 128, stride=TAPS), :].astype(BF)
            broad[a * 128 : (a + 1) * 128, bc * 128 : (bc + 1) * 128] = block
            if upright is not None:
                upright[bc * 128 : (bc + 1) * 128, a * 128 : (a + 1) * 128] = block


def dot(a, b):
    return lax.dot_general(a, b, (((1,), (0,)), ((), ())), preferred_element_type=F32)


def dot_t(a, b):
    return lax.dot_general(a, b, (((1,), (1,)), ((), ())), preferred_element_type=F32)


def spread(planes, first_plane, at, deep, y_even, y_odd, grid):
    plane = TILE * GROWN
    edge = 2 * GROWN
    swapped = parity(4) == 0
    used = edge + plane + edge
    for p in range(grid.shape[0] // IN_PITCH):
        top = p * IN_PITCH
        if first_plane <= p < first_plane + planes:
            grid[top + used : top + IN_PITCH, :] = jnp.zeros((IN_PITCH - used, 128), F32)
            e = p - first_plane
            grid[top + edge : top + edge + plane, :] = deep[e * plane : (e + 1) * plane, :]
        else:
            grid[top : top + IN_PITCH, :] = jnp.zeros((IN_PITCH, 128), F32)
    for e in range(0, planes, 2):
        rows = slice((at * planes + e) * edge, (at * planes + e + 2) * edge)
        one, two = y_even[rows, :].astype(F32), y_odd[rows, :].astype(F32)
        low, high = jnp.where(swapped, two, one), jnp.where(swapped, one, two)
        for k in range(2):
            top = (first_plane + e + k) * IN_PITCH
            grid[top : top + edge, :] = low[k * edge : (k + 1) * edge]
            grid[top + edge + plane : top + used, :] = high[k * edge : (k + 1) * edge]


def stack(planes, first, pitch, parts, grid, stacked, out_pitch, flipped):
    for j in range(planes):
        for b in range(3):
            for c in range(3):
                step = (2 - b) * GROWN + 2 - c if flipped else b * GROWN + c
                at = (3 * b + c) * 128
                cells = [
                    grid[(j + first) * pitch + lo + step : (j + first) * pitch + lo + step + n, :]
                    for lo, n in parts
                ]
                cells = cells[0] if len(cells) == 1 else jnp.concatenate(cells, 0)
                to = j * out_pitch
                stacked[to : to + out_pitch, at : at + 128] = cells.astype(BF)


def add_planes(planes, pitch, shift, pair, single, p):
    total = jnp.zeros((pitch, 128), F32)
    for a, (ref, at) in enumerate(((pair, 0), (pair, 128), (single, 0))):
        j = p - shift(a)
        if 0 <= j < planes:
            total = total + ref[j * pitch : (j + 1) * pitch, at : at + 128]
    return total


def own_lines(grid, at):
    return jnp.concatenate([grid[at : at + TILE, :], grid[at + GROWN : at + GROWN + TILE, :]], 0)


def stack_own(planes, first, pitch, skip, grid, stacked):
    for p in range(planes):
        for y in range(0, TILE, 2):
            to = p * FACE + y * TILE
            for b in range(3):
                for c in range(3):
                    at = (p + first) * pitch + (y + skip + 2 - b) * GROWN + skip + 2 - c
                    stacked[to : to + 2 * TILE, (3 * b + c) * 128 : (3 * b + c + 1) * 128] = (
                        own_lines(grid, at).astype(BF)
                    )


def emit(core, at, value, kept, sent):
    half = value.shape[0] // 2
    columns = slice(at, at + value.shape[1])

    @pl.when(core == 0)
    def _():
        kept[:, columns] = value[:half]
        sent[:, columns] = value[half:]

    @pl.when(core == 1)
    def _():
        kept[:, columns] = value[half:]
        sent[:, columns] = value[:half]


def marked(planes, mask_rows, marks3, y_even, y_odd):
    tail = 4 * planes * GROWN
    swapped = parity(4) == 0

    def mark(by, bz, e):
        at = bz * mask_rows + e
        if by == 1:
            return marks3[at : at + 1, :].astype(F32)
        one = y_even[tail + at : tail + at + 1, :].astype(F32)
        two = y_odd[tail + at : tail + at + 1, :].astype(F32)
        return jnp.where(swapped, two, one) if by == 0 else jnp.where(swapped, one, two)

    return mark


def spans(rows, ends):
    row = lax.broadcasted_iota(jnp.int32, (rows, 128), 0)
    line = row // GROWN
    depth = row - line * GROWN
    return [(line >= lo) & (line <= hi) for lo, hi in ends], [
        (depth >= lo) & (depth <= hi) for lo, hi in ends
    ]


def pad_terms(*refs):
    used = TAPS * 128
    for ref in refs:
        if ref.shape[1] > used:
            ref[:, used:] = jnp.zeros((ref.shape[0], ref.shape[1] - used), ref.dtype)


def ahead(
    planes, deep,
    deep_in, deep_g, inp, w1_tall, w2_wide,
    act, back, in_t,
    stacked, pair, single, padded,
):
    size_x = planes - 4 * deep
    n_out = size_x + 2 * deep
    parts = ((0, INNER_PITCH),)
    plane = TILE * GROWN
    stack(planes, 0, plane, parts, deep_in, stacked, INNER_PITCH, False)
    pair[...] = dot(stacked[...], w1_tall[:, 0:256])
    single[...] = dot(stacked[...], w1_tall[:, 256:384])
    for p in range(n_out):
        act[p * INNER_PITCH : (p + 1) * INNER_PITCH, :] = add_planes(
            planes, INNER_PITCH, lambda a: 1 - deep - a, pair, single, p
        )
    stack(planes, 0, plane, parts, deep_g, stacked, INNER_PITCH, True)
    pair[...] = dot_t(stacked[...], w2_wide[0:256, :])
    single[...] = dot_t(stacked[...], w2_wide[256:384, :])
    for p in range(n_out):
        back[p * INNER_PITCH : (p + 1) * INNER_PITCH, :] = add_planes(
            planes, INNER_PITCH, lambda a: a - 1 - deep, pair, single, p
        )
    padded[...] = jnp.zeros_like(padded)
    top = (1 + deep) * FACE
    rows = size_x * FACE
    padded[top : top + rows, :] = inp[2 * deep * FACE : 2 * deep * FACE + rows, :].astype(F32)
    in_t[...] = padded[...].T.astype(BF)


def whole_plane(inner, outer, p):
    ends = outer[p * OUTER_PITCH : (p + 1) * OUTER_PITCH]
    middle = inner[p * INNER_PITCH : p * INNER_PITCH + PITCH - 2 * EDGE - TILE, :]
    rest = jnp.zeros((TILE, 128), F32)
    return jnp.concatenate([ends[:EDGE], middle, ends[EDGE:], rest], 0)


OUTER_PARTS = ((0, EDGE), (PITCH - EDGE - TILE, EDGE))


def correlate(turned_rows, stacked, columns):
    left = jnp.concatenate([turned_rows[:, a * FACE : a * FACE + columns] for a in range(3)], 0)
    return dot(left, stacked) * unscale


def forward(
    planes, deep, mask_rows,
    deep_in, deep_g, marks3, y_odd, y_even, inner, w1_tall,
    kept, sent, act, grid_g,
    grid_in, outer, pair, single, st_own, hidden,
):
    core = lax.axis_index("dp")
    size_x = planes - 4 * deep
    n_out = size_x + 2 * deep
    first = 1 - deep
    third = 9 * 128
    spread(planes, first, 0, deep_in, y_even, y_odd, grid_in)
    stack(planes, first, IN_PITCH, OUTER_PARTS, grid_in, outer, OUTER_PITCH, False)
    pair[...] = dot(outer[...], w1_tall[:, 0:256])
    single[...] = dot(outer[...], w1_tall[:, 256:384])
    for p in range(n_out):
        ends = add_planes(planes, OUTER_PITCH, lambda a: 1 - deep - a, pair, single, p)
        act[p * PITCH : (p + 1) * PITCH, :] = whole_plane(
            inner.at[p * INNER_PITCH : (p + 1) * INNER_PITCH, :], ends, 0
        )
    spread(planes, first, 1, deep_g, y_even, y_odd, grid_g)
    stack_own(planes, first, IN_PITCH, 1, grid_g, st_own)
    hidden[...] = jnp.zeros_like(hidden)
    for p in range(size_x):
        at = mask_rows + p + 2 * deep
        keep = marks3[at : at + 1, :].astype(F32)
        for y in range(0, TILE, 2):
            pre = own_lines(act, (p + deep) * PITCH + (y + 1) * GROWN + 1)
            to = (p + 1 + 2 * deep) * FACE + y * TILE
            hidden[to : to + 2 * TILE, :] = pre * jax.nn.sigmoid(pre) * keep
    part = correlate(hidden[...].T.astype(BF), st_own[...], planes * FACE)
    for a in range(3):
        emit(core, a * third, part[a * 128 : (a + 1) * 128], kept, sent)
    pad_terms(kept, sent)


def backward(
    planes, deep, mask_rows, tile_of,
    grid_g, act, inner, in_t, marks3, y_even, y_odd, w2_wide,
    kept, sent, st_own,
    outer, pair, single, pg,
):
    core = lax.axis_index("dp")
    size_x = planes - 4 * deep
    n_out = size_x + 2 * deep
    third = 9 * 128
    mark = marked(planes, mask_rows, marks3, y_even, y_odd)
    in_line, in_depth = spans(PITCH, ((0, 0), (1, TILE), (RIM - 1, RIM - 1)))
    stack(planes, 1 - deep, IN_PITCH, OUTER_PARTS, grid_g, outer, OUTER_PITCH, True)
    pair[...] = dot_t(outer[...], w2_wide[0:256, :])
    single[...] = dot_t(outer[...], w2_wide[256:384, :])
    tile, keep = None, None
    for p in range(n_out):
        if tile_of(p + deep) != tile:
            tile, keep = tile_of(p + deep), jnp.zeros((PITCH, 128), F32)
            for by in range(3):
                for bz in range(3):
                    keep = jnp.where(in_line[by] & in_depth[bz], mark(by, bz, p + deep), keep)
        ends = add_planes(planes, OUTER_PITCH, lambda a: a - 1 - deep, pair, single, p)
        back = whole_plane(inner.at[p * INNER_PITCH : (p + 1) * INNER_PITCH, :], ends, 0)
        pre = act[p * PITCH : (p + 1) * PITCH, :]
        sigma = jax.nn.sigmoid(pre)
        grad = back * sigma * (1.0 + pre * (1.0 - sigma))
        pg[p * PITCH : (p + 1) * PITCH, :] = (grad * keep).astype(BF).astype(F32)
    stack_own(n_out, 0, PITCH, 0, pg, st_own)
    part = correlate(in_t, st_own[...], n_out * FACE)
    for a in range(3):
        emit(core, a * third, part[a * 128 : (a + 1) * 128], kept, sent)
    pad_terms(kept, sent)


def last(planes, deep, mask_rows, st_own, grads, marks3, w1_wide, result, pair, single):
    size_x = planes - 4 * deep
    n_out = size_x + 2 * deep
    pair[...] = dot_t(st_own[...], w1_wide[0:256, :])
    single[...] = dot_t(st_own[...], w1_wide[256:384, :])
    for p in range(size_x):
        e = p + 2 * deep
        m = marks3[mask_rows + e : mask_rows + e + 1, :].astype(F32)
        total = add_planes(n_out, FACE, lambda a: a - 1 - deep, pair, single, p)
        summed = (grads[e * FACE : (e + 1) * FACE, :].astype(F32) + total) * m
        result[p * FACE : (p + 1) * FACE, :] = summed.astype(BF)


def swap(value, axis, bits):
    count = lax.axis_size(axis)
    return lax.ppermute(value, axis, [(source, source ^ bits) for source in range(count)])


def cross(value, bits):
    count = lax.axis_size("blk")
    pairs = [
        (core * count + s, core * count + (s ^ bit))
        for core, bit in enumerate(bits)
        for s in range(count)
    ]
    return lax.ppermute(value, ("dp", "blk"), pairs)


PLANE = ((1, 2), (2, 1), (0, 3, 1, 2))
MIXED = ((1, 4), (2, 4), (0, 3, 2, 1))


def spot(group):
    chip, core = lax.axis_index("blk"), lax.axis_index("dp")
    places = [chip // one % 2 + 2 * (chip // two % 2) for one, two in group[:2]]
    return jnp.where(core == 0, places[0], places[1])


def split_rows(group, kept, got, own, *sent):
    me = spot(group)
    rows = own.shape[0]
    for n, k in enumerate(group[2]):
        at = pl.ds(pl.multiple_of((me ^ k) * rows, rows), rows)
        value = kept[at, :] + got[at, :].astype(F32)
        if n == 0:
            own[...] = value
        else:
            sent[n - 1][...] = value.astype(BF)


def split_columns(parts, *refs):
    kept, got, own, sent = refs[0], refs[1:INNER], refs[INNER], refs[INNER + 1 :]
    me = lax.axis_index("blk") // INNER
    columns = own.shape[1]
    for k in range(parts):
        at = pl.ds(pl.multiple_of((me ^ k) * columns, 128), columns)
        value = kept[:, at]
        for ref in got:
            value = value + ref[:, at].astype(F32)
        if k == 0:
            own[...] = value
        else:
            sent[k - 1][...] = value.astype(BF)


def add_pair(one, two, out):
    out[...] = (one[...].astype(F32) + two[...].astype(F32)).astype(BF)


def lay_rows(one, two, out, wide):
    rows = one.shape[0]
    for tap in range(TAPS):
        columns = slice(tap * 128, (tap + 1) * 128)
        total = one[:, columns].astype(F32) + two[:, columns].astype(F32)
        wide[pl.ds(tap, rows, stride=TAPS), :] = total
    out[...] = wide[...].astype(BF)


def add_all(parts, *refs):
    value = refs[0][...]
    for ref in refs[1:parts]:
        value = value + ref[...].astype(F32)
    refs[parts][...] = value.astype(BF)


def join_columns(parts, *refs):
    me = lax.axis_index("blk") // INNER
    out = refs[parts]
    columns = refs[0].shape[1]
    for k in range(parts):
        out[:, pl.ds(pl.multiple_of((me ^ k) * columns, 128), columns)] = refs[k][...]


def join_rows(group, *refs):
    me = spot(group)
    out = refs[INNER]
    rows = refs[0].shape[0]
    for n, k in enumerate(group[2]):
        out[pl.ds(pl.multiple_of((me ^ k) * rows, rows), rows), :] = refs[n][...]


def finish(own, other, out):
    core = lax.axis_index("dp")
    half = own.shape[0]

    @pl.when(core == 0)
    def _():
        out[:half, :] = own[...].astype(F32)
        out[half:, :] = other[...].astype(F32)

    @pl.when(core == 1)
    def _():
        out[:half, :] = other[...].astype(F32)
        out[half:, :] = own[...].astype(F32)


def after(value, *others):
    return lax.optimization_barrier((value, *others))[0]


def near(group, values):
    return [
        cross(v, [one * (k % 2) + two * (k // 2) for one, two in group[:2]])
        for v, k in zip(values, group[2][1:])
    ]


def far(values):
    return [swap(v, "blk", INNER * (k + 1)) for k, v in enumerate(values)]


def split_stage(group, kept, got):
    half, columns = kept.shape
    rows = half // INNER
    return call(
        functools.partial(split_rows, group),
        [shape((rows, columns), F32)] + [shape((rows, columns), BF)] * (INNER - 1),
        [kept, got],
    )


def sum_stage(own, gots):
    parts = len(gots) + 1
    return call(functools.partial(add_all, parts), [shape(own.shape, BF)], [own] + gots)[0]


def laid_pair(value, got):
    laid = (value.shape[0] * TAPS, 128)
    return call(lay_rows, [shape(laid, BF)], [value, got], scratch=[pltpu.VMEM(laid, F32)])[0]


def pair_stage(value, got):
    return call(add_pair, [shape(value.shape, BF)], [value, got])[0]


def back_stage(group, wide, gots):
    rows, columns = wide.shape
    return call(
        functools.partial(join_rows, group), [shape((rows * INNER, columns), BF)], [wide] + gots
    )[0]


def wide_sum(own, gots):
    outer = lax.axis_size("blk") // INNER
    rows, columns = own.shape
    part = columns // outer
    own, *send = call(
        functools.partial(split_columns, outer),
        [shape((rows, part), F32)] + [shape((rows, part), BF)] * (outer - 1),
        [own] + gots,
    )
    done = sum_stage(own, far(send))
    return call(
        functools.partial(join_columns, outer),
        [shape((rows, columns), BF)],
        [done] + far([done] * (outer - 1)),
    )[0]


def finished(mine, other):
    return call(finish, [shape((2 * mine.shape[0], 128), F32)], [mine, other])[0]


def rest_steps(group):
    count = lax.axis_size("blk")
    bits = [1 << k for k in range(count.bit_length() - 1)]
    left = [[bit for bit in bits if bit not in used] for used in group[:2]]
    return list(zip(left[0], reversed(left[1])))


def across(groups, owns, gots, beside):
    if lax.axis_size("blk") // INNER > 4:
        sums = [wide_sum(own, got) for own, got in zip(owns, gots)]
        one, two = [laid_pair(value, jnp.zeros_like(value)) for value in sums]
        return one, two, beside(one)
    one = sum_stage(owns[0], gots[0])
    two = sum_stage(after(owns[1], one), gots[1])
    steps = [rest_steps(group) for group in groups]
    other = None
    for n, (bits_one, bits_two) in enumerate(zip(*steps)):
        add = laid_pair if n == len(steps[0]) - 1 else pair_stage
        got_one, got_two = cross(one, bits_one), cross(two, bits_two)
        one = add(after(one, two), got_one)
        if other is None:
            other = beside(one)
            two = after(two, other)
        two = add(after(two, one), got_two)
    return one, two, other


def on_device(features, tile_mask, w_first, w_second, cotangent):
    width = features.shape[2]
    tiles = tile_mask.shape[1]
    size_x = tiles * TILE
    count = lax.axis_size("blk")
    deep = 1 if count // 16 > 1 else 0
    planes = size_x + 4 * deep
    feat, cot, mask = features[0], cotangent[0], tile_mask

    def along(value, stride, extent, toward):
        pairs = [
            (s, s + toward * stride)
            for s in range(count)
            if 0 <= s // stride % extent + toward < extent
        ]
        return lax.ppermute(value, "blk", pairs)

    if deep:
        wide_mask = jnp.broadcast_to(
            jnp.repeat(tile_mask[0], TILE)[:, None], (size_x, width)
        ).astype(BF)
        keep = jnp.repeat(wide_mask, FACE, axis=0)
        feat, cot = feat * keep, cot * keep
        slab = 2 * FACE
        up = jnp.concatenate([feat[-slab:], cot[-slab:], wide_mask[-16:]], 0)
        down = jnp.concatenate([feat[:slab], cot[:slab], wide_mask[:16]], 0)
        before = along(up, 16, count // 16, 1)
        behind = along(down, 16, count // 16, -1)
        feat = jnp.concatenate([before[:slab], feat, behind[:slab]], 0)
        cot = jnp.concatenate([before[slab : 2 * slab], cot, behind[slab : 2 * slab]], 0)
        ends = [v[2 * slab : 2 * slab + 1, :1].astype(jnp.int32) for v in (before, behind)]
        mask = jnp.concatenate([ends[0], tile_mask, ends[1]], 1)

    def tile_of(e):
        if not deep:
            return e // TILE
        return (e + TILE - 2) // TILE

    def beside(one, two, stride, extent):
        pairs = ([], [])
        for s in range(count):
            place = s // stride % extent
            if place + 1 < extent:
                pairs[place % 2].extend([(s, s + stride), (s + stride, s)])
        return lax.ppermute(one, "blk", pairs[0]), lax.ppermute(two, "blk", pairs[1])

    mask_rows = -(-planes // 16) * 16
    lines = planes * TILE
    cells = planes * FACE
    side = 4 * lines + mask_rows
    inp, grads, marks, even, odd = call(
        functools.partial(pack_depth, planes, tile_of, mask_rows),
        [shape((cells, width), BF)] * 2
        + [shape((mask_rows, width), BF)]
        + [shape((side, width), BF)] * 2,
        [mask, jnp.stack([feat, cot])],
        scratch=[pltpu.VMEM((cells, width), F32)],
        smem=(0,),
    )
    z_even, z_odd = beside(even, odd, 1, 4)
    broad = shape((3 * width, 9 * width), BF)
    upright = shape((9 * width, 3 * width), BF)

    w1_wide, w1_tall, w2_wide = call(
        lay_weights,
        [broad, upright, broad],
        [jnp.stack([w_first, w_second])],
        scratch=[pltpu.VMEM((TAPS * width, width), F32)],
    )
    inp = after(inp, w2_wide)
    edge = 4 * planes * GROWN + 3 * mask_rows
    even, odd, deep_in, deep_g, marks3 = call(
        functools.partial(pack_lines, planes, mask_rows),
        [shape((edge, width), BF)] * 2
        + [shape((lines * GROWN + SPARE, width), F32)] * 2
        + [shape((3 * mask_rows, width), BF)],
        [inp, grads, marks, z_odd, z_even],
    )
    y_even, y_odd = beside(even, odd, 4, 4)
    outer = count // INNER
    columns = TAPS * width if outer <= 4 else -(-TAPS // outer) * outer * width
    n_in = size_x + 2 + 2 * deep
    n_out = size_x + 2 * deep
    half = width // 2
    work = 2 * size_x * FACE * TAPS * width * width
    terms = [shape((half, columns), F32)] * 2

    def parts_of(rows):
        return [pltpu.VMEM((rows, 2 * width), F32), pltpu.VMEM((rows, width), F32)]

    inner_act, inner_back, in_t = call(
        functools.partial(ahead, planes, deep),
        [shape((n_out * INNER_PITCH, width), F32)] * 2
        + [shape((width, (n_out + 2) * FACE), BF)],
        [deep_in, deep_g, inp, w1_tall, w2_wide],
        scratch=[pltpu.VMEM((planes * INNER_PITCH, 9 * width), BF)]
        + parts_of(planes * INNER_PITCH)
        + [pltpu.VMEM(((n_out + 2) * FACE, width), F32)],
        flops=2 * work,
    )
    marks3 = after(marks3, in_t)
    kept_a, sent_a, act, grid_g = call(
        functools.partial(forward, planes, deep, mask_rows),
        terms + [shape((n_out * PITCH, width), F32), shape((n_in * IN_PITCH, width), F32)],
        [deep_in, deep_g, marks3, y_odd, y_even, inner_act, w1_tall],
        scratch=[
            pltpu.VMEM((n_in * IN_PITCH, width), F32),
            pltpu.VMEM((planes * OUTER_PITCH, 9 * width), BF),
        ]
        + parts_of(planes * OUTER_PITCH)
        + [
            pltpu.VMEM((planes * FACE, 9 * width), BF),
            pltpu.VMEM(((planes + 2) * FACE, width), F32),
        ],
        flops=2 * work,
    )
    groups = (PLANE, MIXED if outer <= 4 else PLANE)
    own_a, *send_a = split_stage(groups[0], kept_a, swap(sent_a, "dp", 1))
    kept_b, sent_b, st_own = call(
        functools.partial(backward, planes, deep, mask_rows, tile_of),
        terms + [shape((n_out * FACE, 9 * width), BF)],
        [grid_g, act, inner_back, in_t, marks3, y_even, y_odd, w2_wide],
        scratch=[pltpu.VMEM((planes * OUTER_PITCH, 9 * width), BF)]
        + parts_of(planes * OUTER_PITCH)
        + [pltpu.VMEM((n_out * PITCH, width), F32)],
        flops=2 * work,
    )
    own_b, *send_b = split_stage(groups[1], kept_b, swap(sent_b, "dp", 1))
    gots_a = near(groups[0], send_a)
    gots_b = near(groups[1], send_b)
    own_a = after(own_a, own_b)

    def last_part(cue):
        return call(
            functools.partial(last, planes, deep, mask_rows),
            [shape((size_x * FACE, width), BF)],
            [after(st_own, cue), grads, marks3, w1_wide],
            scratch=parts_of(n_out * FACE),
            flops=work,
        )[0]

    value_a, value_b, result = across(groups, (own_a, own_b), (gots_a, gots_b), last_part)
    gots_a = near(groups[0], [value_a] * (INNER - 1))
    gots_b = near(groups[1], [value_b] * (INNER - 1))
    mine_a = back_stage(groups[0], value_a, gots_a)
    mine_b = back_stage(groups[1], value_b, gots_b)
    grad_second = finished(mine_a, swap(mine_a, "dp", 1))
    grad_first = finished(mine_b, swap(mine_b, "dp", 1))
    return (grad_first, grad_second, result[None])


def solution(mesh):
    in_specs = (P("dp", "blk", None), P("dp", "blk"), P(), P(), P("dp", "blk", None))
    out_specs = (P(), P(), P("dp", "blk", None))
    return jax.shard_map(
        on_device, mesh=mesh, in_specs=in_specs, out_specs=out_specs, check_vma=False
    )
```

```python
import functools

import jax
import jax.numpy as jnp
from jax import lax
from jax.experimental import pallas as pl
from jax.experimental.pallas import tpu as pltpu
from jax.sharding import PartitionSpec as P

TILE = 8
FACE = TILE * TILE
RIM = TILE + 2
GROWN = TILE + 4
IN_PITCH = 160
PITCH = 128
INNER_PITCH = 80
OUTER_PITCH = 48
EDGE = 24
LANES = 32
SPARE = 16
TAPS = 27
INNER = 4
BF = jnp.bfloat16
F32 = jnp.float32
unscale = 1.0 / 512.0
LIMIT = 24 * 2**20

VM = pl.BlockSpec(memory_space=pltpu.VMEM)
SM = pl.BlockSpec(memory_space=pltpu.SMEM)


def call(body, outs, ins, scratch=(), smem=(), flops=0):
    specs = [SM if i in smem else VM for i in range(len(ins))]
    moved = sum(a.size * a.dtype.itemsize for a in list(ins) + list(outs))
    return pl.pallas_call(
        body,
        out_shape=list(outs),
        in_specs=specs,
        out_specs=[VM] * len(outs),
        scratch_shapes=list(scratch),
        compiler_params=pltpu.CompilerParams(vmem_limit_bytes=LIMIT),
        cost_estimate=pl.CostEstimate(flops=flops, bytes_accessed=moved, transcendentals=0),
    )(*ins)


def shape(dims, kind):
    return jax.ShapeDtypeStruct(dims, kind)


def parity(stride):
    return lax.axis_index("blk") // stride % 2


def pack_depth(planes, tile_of, mask_rows, mask, both, inp, grads, marks, even, odd, wide):
    lines = planes * TILE
    row = lax.broadcasted_iota(jnp.int32, (mask_rows, 128), 0)
    filled = jnp.zeros((mask_rows, 128), F32)
    kept_of = [mask[0, tile_of(e)].astype(F32) for e in range(planes)]
    for e in range(planes):
        filled = jnp.where(row == e, kept_of[e], filled)
    filled = filled.astype(BF)
    marks[...] = filled
    even[4 * lines :, :] = filled
    odd[4 * lines :, :] = filled
    side = parity(1)
    for at, dst in enumerate((inp, grads)):
        for e in range(planes):
            rows = slice(e * FACE, (e + 1) * FACE)
            kept = both[at, rows, :].astype(F32) * kept_of[e]
            wide[rows, :] = kept
            dst[rows, :] = kept.astype(BF)

        def faces(lo, hi, at=at):
            for k in range(2):
                to = slice((at * 2 + k) * lines, (at * 2 + k + 1) * lines)
                lo[to, :] = wide[pl.ds(k, lines, stride=TILE), :].astype(BF)
                hi[to, :] = wide[pl.ds(TILE - 2 + k, lines, stride=TILE), :].astype(BF)

        @pl.when(side == 0)
        def _():
            faces(odd, even)

        @pl.when(side == 1)
        def _():
            faces(even, odd)


def pack_lines(
    planes, mask_rows, inp, grads, marks, z_odd, z_even, even, odd, deep_in, deep_g, marks3
):
    lines = planes * TILE
    plane = TILE * GROWN
    edge = 2 * GROWN
    swapped = parity(1) == 0

    def sides(rows):
        one, two = z_even[rows, :].astype(F32), z_odd[rows, :].astype(F32)
        return jnp.where(swapped, two, one), jnp.where(swapped, one, two)

    left, right = sides(slice(4 * lines, 4 * lines + mask_rows))
    for at, rows in enumerate((left, marks[...].astype(F32), right)):
        marks3[at * mask_rows : (at + 1) * mask_rows, :] = rows.astype(BF)
    lane = lax.broadcasted_iota(jnp.int32, (mask_rows, 128), 1)
    own = marks[...].astype(F32)
    packed = jnp.where(lane < LANES, left, jnp.where(lane < 2 * LANES, own, right)).astype(BF)
    for ref in (even, odd):
        ref[4 * planes * GROWN :, :] = packed
    side = parity(4)
    for at, (src, dst) in enumerate(((inp, deep_in), (grads, deep_g))):
        dst[lines * GROWN :, :] = jnp.zeros((SPARE, 128), F32)
        for pair in range(0, lines, 2):
            cells = src[pair * TILE : (pair + 2) * TILE, :].astype(F32)
            top = pair * GROWN + 2
            dst[top : top + TILE, :] = cells[:TILE]
            dst[top + GROWN : top + GROWN + TILE, :] = cells[TILE:]
        for k in range(2):
            left, right = sides(slice((at * 2 + k) * lines, (at * 2 + k + 1) * lines))
            dst[pl.ds(k, lines, stride=GROWN), :] = left
            dst[pl.ds(2 + TILE + k, lines, stride=GROWN), :] = right

        def faces(lo, hi, at=at, dst=dst):
            for e in range(0, planes, 2):
                to = slice((at * planes + e) * edge, (at * planes + e + 2) * edge)
                for ref, start in ((lo, 0), (hi, plane - edge)):
                    ref[to, :] = jnp.concatenate(
                        [
                            dst[p * plane + start : p * plane + start + edge, :]
                            for p in (e, e + 1)
                        ],
                        0,
                    ).astype(BF)

        @pl.when(side == 0)
        def _():
            faces(odd, even)

        @pl.when(side == 1)
        def _():
            faces(even, odd)


def lay_weights(src, wide_1, tall_1, wide_2, rows):
    for at, (broad, upright) in enumerate(((wide_1, tall_1), (wide_2, None))):
        rows[...] = src[at].astype(F32)
        for tap in range(TAPS):
            a, bc = tap // 9, tap % 9
            block = rows[pl.ds(tap, 128, stride=TAPS), :].astype(BF)
            broad[a * 128 : (a + 1) * 128, bc * 128 : (bc + 1) * 128] = block
            if upright is not None:
                upright[bc * 128 : (bc + 1) * 128, a * 128 : (a + 1) * 128] = block


def dot(a, b):
    return lax.dot_general(a, b, (((1,), (0,)), ((), ())), preferred_element_type=F32)


def dot_t(a, b):
    return lax.dot_general(a, b, (((1,), (1,)), ((), ())), preferred_element_type=F32)


def spread(planes, first_plane, at, deep, y_even, y_odd, grid):
    plane = TILE * GROWN
    edge = 2 * GROWN
    swapped = parity(4) == 0
    used = edge + plane + edge
    for p in range(grid.shape[0] // IN_PITCH):
        top = p * IN_PITCH
        if first_plane <= p < first_plane + planes:
            grid[top + used : top + IN_PITCH, :] = jnp.zeros((IN_PITCH - used, 128), F32)
            e = p - first_plane
            grid[top + edge : top + edge + plane, :] = deep[e * plane : (e + 1) * plane, :]
        else:
            grid[top : top + IN_PITCH, :] = jnp.zeros((IN_PITCH, 128), F32)
    for e in range(0, planes, 2):
        rows = slice((at * planes + e) * edge, (at * planes + e + 2) * edge)
        one, two = y_even[rows, :].astype(F32), y_odd[rows, :].astype(F32)
        low, high = jnp.where(swapped, two, one), jnp.where(swapped, one, two)
        for k in range(2):
            top = (first_plane + e + k) * IN_PITCH
            grid[top : top + edge, :] = low[k * edge : (k + 1) * edge]
            grid[top + edge + plane : top + used, :] = high[k * edge : (k + 1) * edge]


def stack(planes, first, pitch, parts, grid, stacked, out_pitch, flipped):
    for j in range(planes):
        for b in range(3):
            for c in range(3):
                step = (2 - b) * GROWN + 2 - c if flipped else b * GROWN + c
                at = (3 * b + c) * 128
                cells = [
                    grid[(j + first) * pitch + lo + step : (j + first) * pitch + lo + step + n, :]
                    for lo, n in parts
                ]
                cells = cells[0] if len(cells) == 1 else jnp.concatenate(cells, 0)
                to = j * out_pitch
                stacked[to : to + out_pitch, at : at + 128] = cells.astype(BF)


def add_planes(planes, pitch, shift, pair, single, p):
    total = jnp.zeros((pitch, 128), F32)
    for a, (ref, at) in enumerate(((pair, 0), (pair, 128), (single, 0))):
        j = p - shift(a)
        if 0 <= j < planes:
            total = total + ref[j * pitch : (j + 1) * pitch, at : at + 128]
    return total


def own_lines(grid, at):
    return jnp.concatenate([grid[at : at + TILE, :], grid[at + GROWN : at + GROWN + TILE, :]], 0)


def stack_own(planes, first, pitch, skip, grid, stacked):
    for p in range(planes):
        for y in range(0, TILE, 2):
            to = p * FACE + y * TILE
            for b in range(3):
                for c in range(3):
                    at = (p + first) * pitch + (y + skip + 2 - b) * GROWN + skip + 2 - c
                    stacked[to : to + 2 * TILE, (3 * b + c) * 128 : (3 * b + c + 1) * 128] = (
                        own_lines(grid, at).astype(BF)
                    )


def marked(planes, mask_rows, marks3, y_even, y_odd):
    tail = 4 * planes * GROWN
    swapped = parity(4) == 0

    def mark(by, bz, e):
        if by == 1:
            at = bz * mask_rows + e
            return marks3[at : at + 1, :].astype(F32)
        one = y_even[tail + e : tail + e + 1, :].astype(F32)
        two = y_odd[tail + e : tail + e + 1, :].astype(F32)
        row = jnp.where(swapped, two, one) if by == 0 else jnp.where(swapped, one, two)
        return row[:, LANES * bz : LANES * bz + 1]

    return mark


def spans(rows, ends):
    row = lax.broadcasted_iota(jnp.int32, (rows, 128), 0)
    line = row // GROWN
    depth = row - line * GROWN
    return [(line >= lo) & (line <= hi) for lo, hi in ends], [
        (depth >= lo) & (depth <= hi) for lo, hi in ends
    ]


def pad_terms(*refs):
    used = TAPS * 128
    for ref in refs:
        if ref.shape[1] > used:
            ref[:, used:] = jnp.zeros((ref.shape[0], ref.shape[1] - used), ref.dtype)


def ahead(
    planes, deep,
    deep_in, deep_g, inp, w1_tall, w2_wide,
    act, back, in_t,
    stacked, pair, single, padded,
):
    size_x = planes - 4 * deep
    n_out = size_x + 2 * deep
    parts = ((0, INNER_PITCH),)
    plane = TILE * GROWN
    stack(planes, 0, plane, parts, deep_in, stacked, INNER_PITCH, False)
    pair[...] = dot(stacked[...], w1_tall[:, 0:256])
    single[...] = dot(stacked[...], w1_tall[:, 256:384])
    for p in range(n_out):
        act[p * INNER_PITCH : (p + 1) * INNER_PITCH, :] = add_planes(
            planes, INNER_PITCH, lambda a: 1 - deep - a, pair, single, p
        )
    stack(planes, 0, plane, parts, deep_g, stacked, INNER_PITCH, True)
    pair[...] = dot_t(stacked[...], w2_wide[0:256, :])
    single[...] = dot_t(stacked[...], w2_wide[256:384, :])
    for p in range(n_out):
        back[p * INNER_PITCH : (p + 1) * INNER_PITCH, :] = add_planes(
            planes, INNER_PITCH, lambda a: a - 1 - deep, pair, single, p
        )
    padded[...] = jnp.zeros_like(padded)
    top = (1 + deep) * FACE
    rows = size_x * FACE
    padded[top : top + rows, :] = inp[2 * deep * FACE : 2 * deep * FACE + rows, :].astype(F32)
    in_t[...] = padded[...].T.astype(BF)


def whole_plane(inner, outer, p):
    ends = outer[p * OUTER_PITCH : (p + 1) * OUTER_PITCH]
    middle = inner[p * INNER_PITCH : p * INNER_PITCH + PITCH - 2 * EDGE - TILE, :]
    rest = jnp.zeros((TILE, 128), F32)
    return jnp.concatenate([ends[:EDGE], middle, ends[EDGE:], rest], 0)


OUTER_PARTS = ((0, EDGE), (PITCH - EDGE - TILE, EDGE))


def correlate(core, turned_rows, stacked, columns, kept, sent):
    half = kept.shape[0]
    third = stacked.shape[1]
    halves = [pl.ds(pl.multiple_of(side * half, half), half) for side in (core, 1 - core)]
    left = [
        turned_rows[rows, a * FACE : a * FACE + columns] for rows in halves for a in range(3)
    ]
    part = dot(jnp.concatenate(left, 0), stacked) * unscale
    for n, out in enumerate((kept, sent)):
        for a in range(3):
            at = (n * 3 + a) * half
            out[:, a * third : (a + 1) * third] = part[at : at + half]
    pad_terms(kept, sent)


def forward(
    planes, deep, mask_rows,
    deep_in, deep_g, marks3, y_odd, y_even, inner, w1_tall,
    kept, sent, act, grid_g,
    grid_in, outer, pair, single, st_own, hidden, hid_t,
):
    core = lax.axis_index("dp")
    size_x = planes - 4 * deep
    n_out = size_x + 2 * deep
    first = 1 - deep
    spread(planes, first, 0, deep_in, y_even, y_odd, grid_in)
    stack(planes, first, IN_PITCH, OUTER_PARTS, grid_in, outer, OUTER_PITCH, False)
    pair[...] = dot(outer[...], w1_tall[:, 0:256])
    single[...] = dot(outer[...], w1_tall[:, 256:384])
    for p in range(n_out):
        ends = add_planes(planes, OUTER_PITCH, lambda a: 1 - deep - a, pair, single, p)
        act[p * PITCH : (p + 1) * PITCH, :] = whole_plane(
            inner.at[p * INNER_PITCH : (p + 1) * INNER_PITCH, :], ends, 0
        )
    spread(planes, first, 1, deep_g, y_even, y_odd, grid_g)
    stack_own(planes, first, IN_PITCH, 1, grid_g, st_own)
    hidden[...] = jnp.zeros_like(hidden)
    for p in range(size_x):
        at = mask_rows + p + 2 * deep
        keep = marks3[at : at + 1, :].astype(F32)
        for y in range(0, TILE, 2):
            pre = own_lines(act, (p + deep) * PITCH + (y + 1) * GROWN + 1)
            to = (p + 1 + 2 * deep) * FACE + y * TILE
            hidden[to : to + 2 * TILE, :] = pre * jax.nn.sigmoid(pre) * keep
    hid_t[...] = hidden[...].T.astype(BF)
    correlate(core, hid_t, st_own[...], planes * FACE, kept, sent)


def backward(
    planes, deep, mask_rows, tile_of,
    grid_g, act, inner, in_t, marks3, y_even, y_odd, w2_wide,
    kept, sent, st_own,
    outer, pair, single, pg,
):
    core = lax.axis_index("dp")
    size_x = planes - 4 * deep
    n_out = size_x + 2 * deep
    mark = marked(planes, mask_rows, marks3, y_even, y_odd)
    in_line, in_depth = spans(PITCH, ((0, 0), (1, TILE), (RIM - 1, RIM - 1)))
    stack(planes, 1 - deep, IN_PITCH, OUTER_PARTS, grid_g, outer, OUTER_PITCH, True)
    pair[...] = dot_t(outer[...], w2_wide[0:256, :])
    single[...] = dot_t(outer[...], w2_wide[256:384, :])
    tile, keep = None, None
    for p in range(n_out):
        if tile_of(p + deep) != tile:
            tile, keep = tile_of(p + deep), jnp.zeros((PITCH, 128), F32)
            for by in range(3):
                for bz in range(3):
                    keep = jnp.where(in_line[by] & in_depth[bz], mark(by, bz, p + deep), keep)
        ends = add_planes(planes, OUTER_PITCH, lambda a: a - 1 - deep, pair, single, p)
        back = whole_plane(inner.at[p * INNER_PITCH : (p + 1) * INNER_PITCH, :], ends, 0)
        pre = act[p * PITCH : (p + 1) * PITCH, :]
        sigma = jax.nn.sigmoid(pre)
        grad = back * sigma * (1.0 + pre * (1.0 - sigma))
        pg[p * PITCH : (p + 1) * PITCH, :] = (grad * keep).astype(BF).astype(F32)
    stack_own(n_out, 0, PITCH, 0, pg, st_own)
    correlate(core, in_t, st_own[...], n_out * FACE, kept, sent)


def last(planes, deep, mask_rows, st_own, grads, marks3, w1_wide, result, pair, single):
    size_x = planes - 4 * deep
    n_out = size_x + 2 * deep
    pair[...] = dot_t(st_own[...], w1_wide[0:256, :])
    single[...] = dot_t(st_own[...], w1_wide[256:384, :])
    for p in range(size_x):
        e = p + 2 * deep
        m = marks3[mask_rows + e : mask_rows + e + 1, :].astype(F32)
        total = add_planes(n_out, FACE, lambda a: a - 1 - deep, pair, single, p)
        summed = (grads[e * FACE : (e + 1) * FACE, :].astype(F32) + total) * m
        result[p * FACE : (p + 1) * FACE, :] = summed.astype(BF)


def swap(value, axis, bits):
    count = lax.axis_size(axis)
    return lax.ppermute(value, axis, [(source, source ^ bits) for source in range(count)])


def cross(value, bits):
    count = lax.axis_size("blk")
    pairs = [
        (core * count + s, core * count + (s ^ bit))
        for core, bit in enumerate(bits)
        for s in range(count)
    ]
    return lax.ppermute(value, ("dp", "blk"), pairs)


PLANE = ((1, 2), (2, 1), ((0, 3, 1, 2), (0, 3, 1, 2)), ((0, 3, 1, 2), (0, 3, 2, 1)))
MIXED = ((1, 4), (2, 4), ((0, 1, 3, 2), (0, 3, 2, 1)), ((0, 3, 2, 1), (0, 3, 2, 1)))


def met(orders, n):
    return jnp.where(lax.axis_index("dp") == 0, orders[0][n], orders[1][n])


def spot(group):
    chip, core = lax.axis_index("blk"), lax.axis_index("dp")
    places = [chip // one % 2 + 2 * (chip // two % 2) for one, two in group[:2]]
    return jnp.where(core == 0, places[0], places[1])


def split_rows(group, kept, got, own, *sent):
    me = spot(group)
    rows = own.shape[0]
    for n in range(INNER):
        at = pl.ds(pl.multiple_of((me ^ met(group[2], n)) * rows, rows), rows)
        value = kept[at, :] + got[at, :].astype(F32)
        if n == 0:
            own[...] = value
        else:
            sent[n - 1][...] = value.astype(BF)


def split_columns(parts, *refs):
    kept, got, own, sent = refs[0], refs[1:INNER], refs[INNER], refs[INNER + 1 :]
    me = lax.axis_index("blk") // INNER
    columns = own.shape[1]
    for k in range(parts):
        at = pl.ds(pl.multiple_of((me ^ k) * columns, 128), columns)
        value = kept[:, at]
        for ref in got:
            value = value + ref[:, at].astype(F32)
        if k == 0:
            own[...] = value
        else:
            sent[k - 1][...] = value.astype(BF)


def add_pair(one, two, out):
    out[...] = (one[...].astype(F32) + two[...].astype(F32)).astype(BF)


def lay_rows(one, two, out, wide):
    rows = one.shape[0]
    for tap in range(TAPS):
        columns = slice(tap * 128, (tap + 1) * 128)
        total = one[:, columns].astype(F32) + two[:, columns].astype(F32)
        wide[pl.ds(tap, rows, stride=TAPS), :] = total
    out[...] = wide[...].astype(BF)


def add_all(parts, *refs):
    value = refs[0][...]
    for ref in refs[1:parts]:
        value = value + ref[...].astype(F32)
    refs[parts][...] = value.astype(BF)


def join_columns(parts, *refs):
    me = lax.axis_index("blk") // INNER
    out = refs[parts]
    columns = refs[0].shape[1]
    for k in range(parts):
        out[:, pl.ds(pl.multiple_of((me ^ k) * columns, 128), columns)] = refs[k][...]


def join_rows(group, *refs):
    me = spot(group)
    out = refs[INNER]
    rows = refs[0].shape[0]
    for n in range(INNER):
        out[pl.ds(pl.multiple_of((me ^ met(group[3], n)) * rows, rows), rows), :] = refs[n][...]


def finish(own, other, out):
    core = lax.axis_index("dp")
    half = own.shape[0]

    @pl.when(core == 0)
    def _():
        out[:half, :] = own[...].astype(F32)
        out[half:, :] = other[...].astype(F32)

    @pl.when(core == 1)
    def _():
        out[:half, :] = other[...].astype(F32)
        out[half:, :] = own[...].astype(F32)


def after(value, *others):
    return lax.optimization_barrier((value, *others))[0]


def near(group, values, orders):
    return [
        cross(v, [one * (k % 2) + two * (k // 2) for (one, two), k in zip(group, both)])
        for v, both in list(zip(values, zip(*[order[1:] for order in orders])))
    ]


def far(values):
    return [swap(v, "blk", INNER * (k + 1)) for k, v in enumerate(values)]


def split_stage(group, kept, got):
    half, columns = kept.shape
    rows = half // INNER
    return call(
        functools.partial(split_rows, group),
        [shape((rows, columns), F32)] + [shape((rows, columns), BF)] * (INNER - 1),
        [kept, got],
    )


def sum_stage(own, gots):
    parts = len(gots) + 1
    return call(functools.partial(add_all, parts), [shape(own.shape, BF)], [own] + gots)[0]


def laid_pair(value, got):
    laid = (value.shape[0] * TAPS, 128)
    return call(lay_rows, [shape(laid, BF)], [value, got], scratch=[pltpu.VMEM(laid, F32)])[0]


def pair_stage(value, got):
    return call(add_pair, [shape(value.shape, BF)], [value, got])[0]


def back_stage(group, wide, gots):
    rows, columns = wide.shape
    return call(
        functools.partial(join_rows, group), [shape((rows * INNER, columns), BF)], [wide] + gots
    )[0]


def wide_sum(own, gots):
    outer = lax.axis_size("blk") // INNER
    rows, columns = own.shape
    part = columns // outer
    own, *send = call(
        functools.partial(split_columns, outer),
        [shape((rows, part), F32)] + [shape((rows, part), BF)] * (outer - 1),
        [own] + gots,
    )
    done = sum_stage(own, far(send))
    return call(
        functools.partial(join_columns, outer),
        [shape((rows, columns), BF)],
        [done] + far([done] * (outer - 1)),
    )[0]


def finished(mine, other):
    return call(finish, [shape((2 * mine.shape[0], 128), F32)], [mine, other])[0]


def rest_steps(group):
    count = lax.axis_size("blk")
    bits = [1 << k for k in range(count.bit_length() - 1)]
    left = [[bit for bit in bits if bit not in used] for used in group[:2]]
    return list(zip(left[0], reversed(left[1])))


def across(groups, owns, gots, beside):
    if lax.axis_size("blk") // INNER > 4:
        sums = [wide_sum(own, got) for own, got in zip(owns, gots)]
        one, two = [laid_pair(value, jnp.zeros_like(value)) for value in sums]
        return one, two, beside(one)
    one = sum_stage(owns[0], gots[0])
    two = sum_stage(after(owns[1], one), gots[1])
    steps = [rest_steps(group) for group in groups]
    other = None
    for n, (bits_one, bits_two) in enumerate(zip(*steps)):
        add = laid_pair if n == len(steps[0]) - 1 else pair_stage
        got_one, got_two = cross(one, bits_one), cross(two, bits_two)
        one = add(after(one, two), got_one)
        if other is None:
            other = beside(one)
            two = after(two, other)
        two = add(after(two, one), got_two)
    return one, two, other


def on_device(features, tile_mask, w_first, w_second, cotangent):
    width = features.shape[2]
    tiles = tile_mask.shape[1]
    size_x = tiles * TILE
    count = lax.axis_size("blk")
    deep = 1 if count // 16 > 1 else 0
    planes = size_x + 4 * deep
    feat, cot, mask = features[0], cotangent[0], tile_mask

    def along(value, stride, extent, toward):
        pairs = [
            (s, s + toward * stride)
            for s in range(count)
            if 0 <= s // stride % extent + toward < extent
        ]
        return lax.ppermute(value, "blk", pairs)

    if deep:
        wide_mask = jnp.broadcast_to(
            jnp.repeat(tile_mask[0], TILE)[:, None], (size_x, width)
        ).astype(BF)
        keep = jnp.repeat(wide_mask, FACE, axis=0)
        feat, cot = feat * keep, cot * keep
        slab = 2 * FACE
        up = jnp.concatenate([feat[-slab:], cot[-slab:], wide_mask[-16:]], 0)
        down = jnp.concatenate([feat[:slab], cot[:slab], wide_mask[:16]], 0)
        before = along(up, 16, count // 16, 1)
        behind = along(down, 16, count // 16, -1)
        feat = jnp.concatenate([before[:slab], feat, behind[:slab]], 0)
        cot = jnp.concatenate([before[slab : 2 * slab], cot, behind[slab : 2 * slab]], 0)
        ends = [v[2 * slab : 2 * slab + 1, :1].astype(jnp.int32) for v in (before, behind)]
        mask = jnp.concatenate([ends[0], tile_mask, ends[1]], 1)

    def tile_of(e):
        if not deep:
            return e // TILE
        return (e + TILE - 2) // TILE

    def beside(one, two, stride, extent):
        pairs = ([], [])
        for s in range(count):
            place = s // stride % extent
            if place + 1 < extent:
                pairs[place % 2].extend([(s, s + stride), (s + stride, s)])
        return lax.ppermute(one, "blk", pairs[0]), lax.ppermute(two, "blk", pairs[1])

    mask_rows = -(-planes // 16) * 16
    lines = planes * TILE
    cells = planes * FACE
    side = 4 * lines + mask_rows
    inp, grads, marks, even, odd = call(
        functools.partial(pack_depth, planes, tile_of, mask_rows),
        [shape((cells, width), BF)] * 2
        + [shape((mask_rows, width), BF)]
        + [shape((side, width), BF)] * 2,
        [mask, jnp.stack([feat, cot])],
        scratch=[pltpu.VMEM((cells, width), F32)],
        smem=(0,),
    )
    z_even, z_odd = beside(even, odd, 1, 4)
    broad = shape((3 * width, 9 * width), BF)
    upright = shape((9 * width, 3 * width), BF)

    w1_wide, w1_tall, w2_wide = call(
        lay_weights,
        [broad, upright, broad],
        [jnp.stack([w_first, w_second])],
        scratch=[pltpu.VMEM((TAPS * width, width), F32)],
    )
    inp = after(inp, w2_wide)
    edge = 4 * planes * GROWN + mask_rows
    even, odd, deep_in, deep_g, marks3 = call(
        functools.partial(pack_lines, planes, mask_rows),
        [shape((edge, width), BF)] * 2
        + [shape((lines * GROWN + SPARE, width), F32)] * 2
        + [shape((3 * mask_rows, width), BF)],
        [inp, grads, marks, z_odd, z_even],
    )
    y_even, y_odd = beside(even, odd, 4, 4)
    outer = count // INNER
    columns = TAPS * width if outer <= 4 else -(-TAPS // outer) * outer * width
    n_in = size_x + 2 + 2 * deep
    n_out = size_x + 2 * deep
    half = width // 2
    work = 2 * size_x * FACE * TAPS * width * width
    terms = [shape((half, columns), F32)] * 2

    def parts_of(rows):
        return [pltpu.VMEM((rows, 2 * width), F32), pltpu.VMEM((rows, width), F32)]

    inner_act, inner_back, in_t = call(
        functools.partial(ahead, planes, deep),
        [shape((n_out * INNER_PITCH, width), F32)] * 2
        + [shape((width, (n_out + 2) * FACE), BF)],
        [deep_in, deep_g, inp, w1_tall, w2_wide],
        scratch=[pltpu.VMEM((planes * INNER_PITCH, 9 * width), BF)]
        + parts_of(planes * INNER_PITCH)
        + [pltpu.VMEM(((n_out + 2) * FACE, width), F32)],
        flops=2 * work,
    )
    marks3 = after(marks3, in_t)
    kept_a, sent_a, act, grid_g = call(
        functools.partial(forward, planes, deep, mask_rows),
        terms + [shape((n_out * PITCH, width), F32), shape((n_in * IN_PITCH, width), F32)],
        [deep_in, deep_g, marks3, y_odd, y_even, inner_act, w1_tall],
        scratch=[
            pltpu.VMEM((n_in * IN_PITCH, width), F32),
            pltpu.VMEM((planes * OUTER_PITCH, 9 * width), BF),
        ]
        + parts_of(planes * OUTER_PITCH)
        + [
            pltpu.VMEM((planes * FACE, 9 * width), BF),
            pltpu.VMEM(((planes + 2) * FACE, width), F32),
            pltpu.VMEM((width, (planes + 2) * FACE), BF),
        ],
        flops=2 * work,
    )
    groups = (PLANE, MIXED if outer <= 4 else PLANE)
    own_a, *send_a = split_stage(groups[0], kept_a, swap(sent_a, "dp", 1))
    kept_b, sent_b, st_own = call(
        functools.partial(backward, planes, deep, mask_rows, tile_of),
        terms + [shape((n_out * FACE, 9 * width), BF)],
        [grid_g, act, inner_back, in_t, marks3, y_even, y_odd, w2_wide],
        scratch=[pltpu.VMEM((planes * OUTER_PITCH, 9 * width), BF)]
        + parts_of(planes * OUTER_PITCH)
        + [pltpu.VMEM((n_out * PITCH, width), F32)],
        flops=2 * work,
    )
    own_b, *send_b = split_stage(groups[1], kept_b, swap(sent_b, "dp", 1))
    gots_a = near(groups[0], send_a, groups[0][2])
    gots_b = near(groups[1], send_b, groups[1][2])
    own_a = after(own_a, own_b)

    def last_part(cue):
        return call(
            functools.partial(last, planes, deep, mask_rows),
            [shape((size_x * FACE, width), BF)],
            [after(st_own, cue), grads, marks3, w1_wide],
            scratch=parts_of(n_out * FACE),
            flops=work,
        )[0]

    value_a, value_b, result = across(groups, (own_a, own_b), (gots_a, gots_b), last_part)
    gots_a = near(groups[0], [value_a] * (INNER - 1), groups[0][3])
    gots_b = near(groups[1], [value_b] * (INNER - 1), groups[1][3])
    mine_a = back_stage(groups[0], value_a, gots_a)
    mine_b = back_stage(groups[1], value_b, gots_b)
    grad_second = finished(mine_a, swap(mine_a, "dp", 1))
    grad_first = finished(mine_b, swap(mine_b, "dp", 1))
    return (grad_first, grad_second, result[None])


def solution(mesh):
    in_specs = (P("dp", "blk", None), P("dp", "blk"), P(), P(), P("dp", "blk", None))
    out_specs = (P(), P(), P("dp", "blk", None))
    return jax.shard_map(
        on_device, mesh=mesh, in_specs=in_specs, out_specs=out_specs, check_vma=False
    )
```

```python
import functools

import jax
import jax.numpy as jnp
from jax import lax
from jax.experimental import pallas as pl
from jax.experimental.pallas import tpu as pltpu
from jax.sharding import PartitionSpec as P

TILE = 8
FACE = TILE * TILE
RIM = TILE + 2
GROWN = TILE + 4
IN_PITCH = 160
PITCH = 128
INNER_PITCH = 80
OUTER_PITCH = 48
EDGE = 24
LANES = 32
SPARE = 16
TAPS = 27
INNER = 4
BF = jnp.bfloat16
F32 = jnp.float32
unscale = 1.0 / 512.0
LIMIT = 24 * 2**20

VM = pl.BlockSpec(memory_space=pltpu.VMEM)
SM = pl.BlockSpec(memory_space=pltpu.SMEM)


def call(body, outs, ins, scratch=(), smem=(), flops=0):
    specs = [SM if i in smem else VM for i in range(len(ins))]
    moved = sum(a.size * a.dtype.itemsize for a in list(ins) + list(outs))
    return pl.pallas_call(
        body,
        out_shape=list(outs),
        in_specs=specs,
        out_specs=[VM] * len(outs),
        scratch_shapes=list(scratch),
        compiler_params=pltpu.CompilerParams(vmem_limit_bytes=LIMIT),
        cost_estimate=pl.CostEstimate(flops=flops, bytes_accessed=moved, transcendentals=0),
    )(*ins)


def shape(dims, kind):
    return jax.ShapeDtypeStruct(dims, kind)


def parity(stride):
    return lax.axis_index("blk") // stride % 2


def pack_depth(planes, tile_of, mask_rows, mask, both, inp, grads, marks, even, odd, wide):
    lines = planes * TILE
    row = lax.broadcasted_iota(jnp.int32, (mask_rows, 128), 0)
    filled = jnp.zeros((mask_rows, 128), F32)
    kept_of = [mask[0, tile_of(e)].astype(F32) for e in range(planes)]
    for e in range(planes):
        filled = jnp.where(row == e, kept_of[e], filled)
    filled = filled.astype(BF)
    marks[...] = filled
    even[4 * lines :, :] = filled
    odd[4 * lines :, :] = filled
    side = parity(1)
    for at, dst in enumerate((inp, grads)):
        for e in range(planes):
            rows = slice(e * FACE, (e + 1) * FACE)
            kept = both[at, rows, :].astype(F32) * kept_of[e]
            wide[rows, :] = kept
            dst[rows, :] = kept.astype(BF)

        def faces(lo, hi, at=at):
            for k in range(2):
                to = slice((at * 2 + k) * lines, (at * 2 + k + 1) * lines)
                lo[to, :] = wide[pl.ds(k, lines, stride=TILE), :].astype(BF)
                hi[to, :] = wide[pl.ds(TILE - 2 + k, lines, stride=TILE), :].astype(BF)

        @pl.when(side == 0)
        def _():
            faces(odd, even)

        @pl.when(side == 1)
        def _():
            faces(even, odd)


def pack_lines(
    planes, mask_rows, inp, grads, marks, z_odd, z_even, even, odd, deep_in, deep_g, marks3
):
    lines = planes * TILE
    plane = TILE * GROWN
    edge = 2 * GROWN
    swapped = parity(1) == 0

    def sides(rows):
        one, two = z_even[rows, :].astype(F32), z_odd[rows, :].astype(F32)
        return jnp.where(swapped, two, one), jnp.where(swapped, one, two)

    left, right = sides(slice(4 * lines, 4 * lines + mask_rows))
    for at, rows in enumerate((left, marks[...].astype(F32), right)):
        marks3[at * mask_rows : (at + 1) * mask_rows, :] = rows.astype(BF)
    lane = lax.broadcasted_iota(jnp.int32, (mask_rows, 128), 1)
    own = marks[...].astype(F32)
    packed = jnp.where(lane < LANES, left, jnp.where(lane < 2 * LANES, own, right)).astype(BF)
    for ref in (even, odd):
        ref[4 * planes * GROWN :, :] = packed
    side = parity(4)
    for at, (src, dst) in enumerate(((inp, deep_in), (grads, deep_g))):
        dst[lines * GROWN :, :] = jnp.zeros((SPARE, 128), F32)
        for pair in range(0, lines, 2):
            cells = src[pair * TILE : (pair + 2) * TILE, :].astype(F32)
            top = pair * GROWN + 2
            dst[top : top + TILE, :] = cells[:TILE]
            dst[top + GROWN : top + GROWN + TILE, :] = cells[TILE:]
        for k in range(2):
            left, right = sides(slice((at * 2 + k) * lines, (at * 2 + k + 1) * lines))
            dst[pl.ds(k, lines, stride=GROWN), :] = left
            dst[pl.ds(2 + TILE + k, lines, stride=GROWN), :] = right

        def faces(lo, hi, at=at, dst=dst):
            for e in range(0, planes, 2):
                to = slice((at * planes + e) * edge, (at * planes + e + 2) * edge)
                for ref, start in ((lo, 0), (hi, plane - edge)):
                    ref[to, :] = jnp.concatenate(
                        [
                            dst[p * plane + start : p * plane + start + edge, :]
                            for p in (e, e + 1)
                        ],
                        0,
                    ).astype(BF)

        @pl.when(side == 0)
        def _():
            faces(odd, even)

        @pl.when(side == 1)
        def _():
            faces(even, odd)


def lay_weights(src, wide_1, tall_1, wide_2, rows):
    for at, (broad, upright) in enumerate(((wide_1, tall_1), (wide_2, None))):
        rows[...] = src[at].astype(F32)
        for tap in range(TAPS):
            a, bc = tap // 9, tap % 9
            block = rows[pl.ds(tap, 128, stride=TAPS), :].astype(BF)
            broad[a * 128 : (a + 1) * 128, bc * 128 : (bc + 1) * 128] = block
            if upright is not None:
                upright[bc * 128 : (bc + 1) * 128, a * 128 : (a + 1) * 128] = block


def dot(a, b):
    return lax.dot_general(a, b, (((1,), (0,)), ((), ())), preferred_element_type=F32)


def dot_t(a, b):
    return lax.dot_general(a, b, (((1,), (1,)), ((), ())), preferred_element_type=F32)


def spread(planes, first_plane, at, deep, y_even, y_odd, grid):
    plane = TILE * GROWN
    edge = 2 * GROWN
    swapped = parity(4) == 0
    used = edge + plane + edge
    for p in range(grid.shape[0] // IN_PITCH):
        top = p * IN_PITCH
        if first_plane <= p < first_plane + planes:
            grid[top + used : top + IN_PITCH, :] = jnp.zeros((IN_PITCH - used, 128), F32)
            e = p - first_plane
            grid[top + edge : top + edge + plane, :] = deep[e * plane : (e + 1) * plane, :]
        else:
            grid[top : top + IN_PITCH, :] = jnp.zeros((IN_PITCH, 128), F32)
    for e in range(0, planes, 2):
        rows = slice((at * planes + e) * edge, (at * planes + e + 2) * edge)
        one, two = y_even[rows, :].astype(F32), y_odd[rows, :].astype(F32)
        low, high = jnp.where(swapped, two, one), jnp.where(swapped, one, two)
        for k in range(2):
            top = (first_plane + e + k) * IN_PITCH
            grid[top : top + edge, :] = low[k * edge : (k + 1) * edge]
            grid[top + edge + plane : top + used, :] = high[k * edge : (k + 1) * edge]


def stack(planes, first, pitch, parts, grid, stacked, out_pitch, flipped):
    for j in range(planes):
        for b in range(3):
            for c in range(3):
                step = (2 - b) * GROWN + 2 - c if flipped else b * GROWN + c
                at = (3 * b + c) * 128
                cells = [
                    grid[(j + first) * pitch + lo + step : (j + first) * pitch + lo + step + n, :]
                    for lo, n in parts
                ]
                cells = cells[0] if len(cells) == 1 else jnp.concatenate(cells, 0)
                to = j * out_pitch
                stacked[to : to + out_pitch, at : at + 128] = cells.astype(BF)


def add_planes(planes, pitch, shift, pair, single, p):
    total = jnp.zeros((pitch, 128), F32)
    for a, (ref, at) in enumerate(((pair, 0), (pair, 128), (single, 0))):
        j = p - shift(a)
        if 0 <= j < planes:
            total = total + ref[j * pitch : (j + 1) * pitch, at : at + 128]
    return total


def own_lines(grid, at):
    return jnp.concatenate([grid[at : at + TILE, :], grid[at + GROWN : at + GROWN + TILE, :]], 0)


def stack_own(planes, first, pitch, skip, grid, stacked):
    for p in range(planes):
        for y in range(0, TILE, 2):
            to = p * FACE + y * TILE
            for b in range(3):
                for c in range(3):
                    at = (p + first) * pitch + (y + skip + 2 - b) * GROWN + skip + 2 - c
                    stacked[to : to + 2 * TILE, (3 * b + c) * 128 : (3 * b + c + 1) * 128] = (
                        own_lines(grid, at).astype(BF)
                    )


def marked(planes, mask_rows, marks3, y_even, y_odd):
    tail = 4 * planes * GROWN
    swapped = parity(4) == 0

    def mark(by, bz, e):
        if by == 1:
            at = bz * mask_rows + e
            return marks3[at : at + 1, :].astype(F32)
        one = y_even[tail + e : tail + e + 1, :].astype(F32)
        two = y_odd[tail + e : tail + e + 1, :].astype(F32)
        row = jnp.where(swapped, two, one) if by == 0 else jnp.where(swapped, one, two)
        return row[:, LANES * bz : LANES * bz + 1]

    return mark


def spans(rows, ends):
    row = lax.broadcasted_iota(jnp.int32, (rows, 128), 0)
    line = row // GROWN
    depth = row - line * GROWN
    return [(line >= lo) & (line <= hi) for lo, hi in ends], [
        (depth >= lo) & (depth <= hi) for lo, hi in ends
    ]


def pad_terms(*refs):
    used = TAPS * 128
    for ref in refs:
        if ref.shape[1] > used:
            ref[:, used:] = jnp.zeros((ref.shape[0], ref.shape[1] - used), ref.dtype)


def ahead(
    planes, deep,
    deep_in, deep_g, inp, w1_tall, w2_wide,
    act, back, in_t,
    stacked, pair, single, padded,
):
    size_x = planes - 4 * deep
    n_out = size_x + 2 * deep
    parts = ((0, INNER_PITCH),)
    plane = TILE * GROWN
    stack(planes, 0, plane, parts, deep_in, stacked, INNER_PITCH, False)
    pair[...] = dot(stacked[...], w1_tall[:, 0:256])
    single[...] = dot(stacked[...], w1_tall[:, 256:384])
    for p in range(n_out):
        act[p * INNER_PITCH : (p + 1) * INNER_PITCH, :] = add_planes(
            planes, INNER_PITCH, lambda a: 1 - deep - a, pair, single, p
        )
    stack(planes, 0, plane, parts, deep_g, stacked, INNER_PITCH, True)
    pair[...] = dot_t(stacked[...], w2_wide[0:256, :])
    single[...] = dot_t(stacked[...], w2_wide[256:384, :])
    for p in range(n_out):
        back[p * INNER_PITCH : (p + 1) * INNER_PITCH, :] = add_planes(
            planes, INNER_PITCH, lambda a: a - 1 - deep, pair, single, p
        )
    padded[...] = jnp.zeros_like(padded)
    top = (1 + deep) * FACE
    rows = size_x * FACE
    padded[top : top + rows, :] = inp[2 * deep * FACE : 2 * deep * FACE + rows, :].astype(F32)
    in_t[...] = padded[...].T.astype(BF)


def whole_plane(inner, outer, p):
    ends = outer[p * OUTER_PITCH : (p + 1) * OUTER_PITCH]
    middle = inner[p * INNER_PITCH : p * INNER_PITCH + PITCH - 2 * EDGE - TILE, :]
    rest = jnp.zeros((TILE, 128), F32)
    return jnp.concatenate([ends[:EDGE], middle, ends[EDGE:], rest], 0)


OUTER_PARTS = ((0, EDGE), (PITCH - EDGE - TILE, EDGE))


def correlate(core, turned_rows, stacked, columns, kept, sent):
    half = kept.shape[0]
    third = stacked.shape[1]
    halves = [pl.ds(pl.multiple_of(side * half, half), half) for side in (core, 1 - core)]
    left = [
        turned_rows[rows, a * FACE : a * FACE + columns] for rows in halves for a in range(3)
    ]
    part = dot(jnp.concatenate(left, 0), stacked) * unscale
    for n, out in enumerate((kept, sent)):
        for a in range(3):
            at = (n * 3 + a) * half
            out[:, a * third : (a + 1) * third] = part[at : at + half]
    pad_terms(kept, sent)


def forward(
    planes, deep, mask_rows,
    deep_in, deep_g, marks3, y_odd, y_even, inner, w1_tall,
    kept, sent, act, grid_g,
    grid_in, outer, pair, single, st_own, hidden, hid_t,
):
    core = lax.axis_index("dp")
    size_x = planes - 4 * deep
    n_out = size_x + 2 * deep
    first = 1 - deep
    spread(planes, first, 0, deep_in, y_even, y_odd, grid_in)
    stack(planes, first, IN_PITCH, OUTER_PARTS, grid_in, outer, OUTER_PITCH, False)
    pair[...] = dot(outer[...], w1_tall[:, 0:256])
    single[...] = dot(outer[...], w1_tall[:, 256:384])
    for p in range(n_out):
        ends = add_planes(planes, OUTER_PITCH, lambda a: 1 - deep - a, pair, single, p)
        act[p * PITCH : (p + 1) * PITCH, :] = whole_plane(
            inner.at[p * INNER_PITCH : (p + 1) * INNER_PITCH, :], ends, 0
        )
    spread(planes, first, 1, deep_g, y_even, y_odd, grid_g)
    stack_own(planes, first, IN_PITCH, 1, grid_g, st_own)
    hidden[...] = jnp.zeros_like(hidden)
    for p in range(size_x):
        at = mask_rows + p + 2 * deep
        keep = marks3[at : at + 1, :].astype(F32)
        for y in range(0, TILE, 2):
            pre = own_lines(act, (p + deep) * PITCH + (y + 1) * GROWN + 1)
            to = (p + 1 + 2 * deep) * FACE + y * TILE
            hidden[to : to + 2 * TILE, :] = pre * jax.nn.sigmoid(pre) * keep
    hid_t[...] = hidden[...].T.astype(BF)
    correlate(core, hid_t, st_own[...], planes * FACE, kept, sent)


def backward(
    planes, deep, mask_rows, tile_of,
    grid_g, act, inner, in_t, marks3, y_even, y_odd, w2_wide,
    kept, sent, st_own,
    outer, pair, single, pg,
):
    core = lax.axis_index("dp")
    size_x = planes - 4 * deep
    n_out = size_x + 2 * deep
    mark = marked(planes, mask_rows, marks3, y_even, y_odd)
    in_line, in_depth = spans(PITCH, ((0, 0), (1, TILE), (RIM - 1, RIM - 1)))
    stack(planes, 1 - deep, IN_PITCH, OUTER_PARTS, grid_g, outer, OUTER_PITCH, True)
    pair[...] = dot_t(outer[...], w2_wide[0:256, :])
    single[...] = dot_t(outer[...], w2_wide[256:384, :])
    tile, keep = None, None
    for p in range(n_out):
        if tile_of(p + deep) != tile:
            tile, keep = tile_of(p + deep), jnp.zeros((PITCH, 128), F32)
            for by in range(3):
                for bz in range(3):
                    keep = jnp.where(in_line[by] & in_depth[bz], mark(by, bz, p + deep), keep)
        ends = add_planes(planes, OUTER_PITCH, lambda a: a - 1 - deep, pair, single, p)
        back = whole_plane(inner.at[p * INNER_PITCH : (p + 1) * INNER_PITCH, :], ends, 0)
        pre = act[p * PITCH : (p + 1) * PITCH, :]
        sigma = jax.nn.sigmoid(pre)
        grad = back * sigma * (1.0 + pre * (1.0 - sigma))
        pg[p * PITCH : (p + 1) * PITCH, :] = (grad * keep).astype(BF).astype(F32)
    stack_own(n_out, 0, PITCH, 0, pg, st_own)
    correlate(core, in_t, st_own[...], n_out * FACE, kept, sent)


def last(planes, deep, mask_rows, st_own, grads, marks3, w1_wide, result, pair, single):
    size_x = planes - 4 * deep
    n_out = size_x + 2 * deep
    pair[...] = dot_t(st_own[...], w1_wide[0:256, :])
    single[...] = dot_t(st_own[...], w1_wide[256:384, :])
    for p in range(size_x):
        e = p + 2 * deep
        m = marks3[mask_rows + e : mask_rows + e + 1, :].astype(F32)
        total = add_planes(n_out, FACE, lambda a: a - 1 - deep, pair, single, p)
        summed = (grads[e * FACE : (e + 1) * FACE, :].astype(F32) + total) * m
        result[p * FACE : (p + 1) * FACE, :] = summed.astype(BF)


def swap(value, axis, bits):
    count = lax.axis_size(axis)
    return lax.ppermute(value, axis, [(source, source ^ bits) for source in range(count)])


def cross(value, bits):
    count = lax.axis_size("blk")
    pairs = [
        (core * count + s, core * count + (s ^ bit))
        for core, bit in enumerate(bits)
        for s in range(count)
    ]
    return lax.ppermute(value, ("dp", "blk"), pairs)


PLANE = ((1, 2), (2, 1), ((0, 3, 1, 2), (0, 3, 1, 2)), ((0, 3, 1, 2), (0, 3, 2, 1)))
MIXED = ((1, 4), (2, 4), ((0, 1, 3, 2), (0, 3, 2, 1)), ((0, 3, 2, 1), (0, 3, 2, 1)))


def met(orders, n):
    return jnp.where(lax.axis_index("dp") == 0, orders[0][n], orders[1][n])


def spot(group):
    chip, core = lax.axis_index("blk"), lax.axis_index("dp")
    places = [chip // one % 2 + 2 * (chip // two % 2) for one, two in group[:2]]
    return jnp.where(core == 0, places[0], places[1])


def split_rows(group, kept, got, own, *sent):
    me = spot(group)
    rows = own.shape[0]
    for n in range(INNER):
        at = pl.ds(pl.multiple_of((me ^ met(group[2], n)) * rows, rows), rows)
        value = kept[at, :] + got[at, :].astype(F32)
        if n == 0:
            own[...] = value
        else:
            sent[n - 1][...] = value.astype(BF)


def split_columns(parts, *refs):
    kept, got, own, sent = refs[0], refs[1:INNER], refs[INNER], refs[INNER + 1 :]
    me = lax.axis_index("blk") // INNER
    columns = own.shape[1]
    for k in range(parts):
        at = pl.ds(pl.multiple_of((me ^ k) * columns, 128), columns)
        value = kept[:, at]
        for ref in got:
            value = value + ref[:, at].astype(F32)
        if k == 0:
            own[...] = value
        else:
            sent[k - 1][...] = value.astype(BF)


def add_pair(one, two, out):
    out[...] = (one[...].astype(F32) + two[...].astype(F32)).astype(BF)


def lay_rows(one, two, out, wide):
    rows = one.shape[0]
    for tap in range(TAPS):
        columns = slice(tap * 128, (tap + 1) * 128)
        total = one[:, columns].astype(F32) + two[:, columns].astype(F32)
        wide[pl.ds(tap, rows, stride=TAPS), :] = total
    out[...] = wide[...].astype(BF)


def add_all(parts, *refs):
    value = refs[0][...]
    for ref in refs[1:parts]:
        value = value + ref[...].astype(F32)
    refs[parts][...] = value.astype(BF)


def join_columns(parts, *refs):
    me = lax.axis_index("blk") // INNER
    out = refs[parts]
    columns = refs[0].shape[1]
    for k in range(parts):
        out[:, pl.ds(pl.multiple_of((me ^ k) * columns, 128), columns)] = refs[k][...]


def join_rows(group, *refs):
    me = spot(group)
    out = refs[INNER]
    rows = refs[0].shape[0]
    for n in range(INNER):
        out[pl.ds(pl.multiple_of((me ^ met(group[3], n)) * rows, rows), rows), :] = refs[n][...]


def finish(own, other, out):
    core = lax.axis_index("dp")
    half = own.shape[0]

    @pl.when(core == 0)
    def _():
        out[:half, :] = own[...].astype(F32)
        out[half:, :] = other[...].astype(F32)

    @pl.when(core == 1)
    def _():
        out[:half, :] = other[...].astype(F32)
        out[half:, :] = own[...].astype(F32)


def after(value, *others):
    return lax.optimization_barrier((value, *others))[0]


def near(group, values, orders):
    return [
        cross(v, [one * (k % 2) + two * (k // 2) for (one, two), k in zip(group, both)])
        for v, both in list(zip(values, zip(*[order[1:] for order in orders])))
    ]


def far(values):
    return [swap(v, "blk", INNER * (k + 1)) for k, v in enumerate(values)]


def split_stage(group, kept, got):
    half, columns = kept.shape
    rows = half // INNER
    return call(
        functools.partial(split_rows, group),
        [shape((rows, columns), F32)] + [shape((rows, columns), BF)] * (INNER - 1),
        [kept, got],
    )


def sum_stage(own, gots):
    parts = len(gots) + 1
    return call(functools.partial(add_all, parts), [shape(own.shape, BF)], [own] + gots)[0]


def laid_pair(value, got):
    laid = (value.shape[0] * TAPS, 128)
    return call(lay_rows, [shape(laid, BF)], [value, got], scratch=[pltpu.VMEM(laid, F32)])[0]


def pair_stage(value, got):
    return call(add_pair, [shape(value.shape, BF)], [value, got])[0]


def back_stage(group, wide, gots):
    rows, columns = wide.shape
    return call(
        functools.partial(join_rows, group), [shape((rows * INNER, columns), BF)], [wide] + gots
    )[0]


def wide_sum(own, gots):
    outer = lax.axis_size("blk") // INNER
    rows, columns = own.shape
    part = columns // outer
    own, *send = call(
        functools.partial(split_columns, outer),
        [shape((rows, part), F32)] + [shape((rows, part), BF)] * (outer - 1),
        [own] + gots,
    )
    done = sum_stage(own, far(send))
    return call(
        functools.partial(join_columns, outer),
        [shape((rows, columns), BF)],
        [done] + far([done] * (outer - 1)),
    )[0]


def finished(mine, other):
    return call(finish, [shape((2 * mine.shape[0], 128), F32)], [mine, other])[0]


def rest_steps(group):
    count = lax.axis_size("blk")
    bits = [1 << k for k in range(count.bit_length() - 1)]
    left = [[bit for bit in bits if bit not in used] for used in group[:2]]
    return list(zip(left[0], reversed(left[1])))


def across(groups, owns, gots, beside):
    if lax.axis_size("blk") // INNER > 4:
        sums = [wide_sum(own, got) for own, got in zip(owns, gots)]
        one, two = [laid_pair(value, jnp.zeros_like(value)) for value in sums]
        return one, two, beside(one)
    one = sum_stage(owns[0], gots[0])
    two = sum_stage(after(owns[1], one), gots[1])
    steps = [rest_steps(group) for group in groups]
    other = None
    for n, (bits_one, bits_two) in enumerate(zip(*steps)):
        add = laid_pair if n == len(steps[0]) - 1 else pair_stage
        got_one, got_two = cross(one, bits_one), cross(two, bits_two)
        one = add(after(one, two), got_one)
        if other is None:
            other = beside(two)
        two = add(two, got_two)
    return one, two, other


def on_device(features, tile_mask, w_first, w_second, cotangent):
    width = features.shape[2]
    tiles = tile_mask.shape[1]
    size_x = tiles * TILE
    count = lax.axis_size("blk")
    deep = 1 if count // 16 > 1 else 0
    planes = size_x + 4 * deep
    feat, cot, mask = features[0], cotangent[0], tile_mask

    def along(value, stride, extent, toward):
        pairs = [
            (s, s + toward * stride)
            for s in range(count)
            if 0 <= s // stride % extent + toward < extent
        ]
        return lax.ppermute(value, "blk", pairs)

    if deep:
        wide_mask = jnp.broadcast_to(
            jnp.repeat(tile_mask[0], TILE)[:, None], (size_x, width)
        ).astype(BF)
        keep = jnp.repeat(wide_mask, FACE, axis=0)
        feat, cot = feat * keep, cot * keep
        slab = 2 * FACE
        up = jnp.concatenate([feat[-slab:], cot[-slab:], wide_mask[-16:]], 0)
        down = jnp.concatenate([feat[:slab], cot[:slab], wide_mask[:16]], 0)
        before = along(up, 16, count // 16, 1)
        behind = along(down, 16, count // 16, -1)
        feat = jnp.concatenate([before[:slab], feat, behind[:slab]], 0)
        cot = jnp.concatenate([before[slab : 2 * slab], cot, behind[slab : 2 * slab]], 0)
        ends = [v[2 * slab : 2 * slab + 1, :1].astype(jnp.int32) for v in (before, behind)]
        mask = jnp.concatenate([ends[0], tile_mask, ends[1]], 1)

    def tile_of(e):
        if not deep:
            return e // TILE
        return (e + TILE - 2) // TILE

    def beside(one, two, stride, extent):
        pairs = ([], [])
        for s in range(count):
            place = s // stride % extent
            if place + 1 < extent:
                pairs[place % 2].extend([(s, s + stride), (s + stride, s)])
        return lax.ppermute(one, "blk", pairs[0]), lax.ppermute(two, "blk", pairs[1])

    mask_rows = -(-planes // 16) * 16
    lines = planes * TILE
    cells = planes * FACE
    side = 4 * lines + mask_rows
    inp, grads, marks, even, odd = call(
        functools.partial(pack_depth, planes, tile_of, mask_rows),
        [shape((cells, width), BF)] * 2
        + [shape((mask_rows, width), BF)]
        + [shape((side, width), BF)] * 2,
        [mask, jnp.stack([feat, cot])],
        scratch=[pltpu.VMEM((cells, width), F32)],
        smem=(0,),
    )
    z_even, z_odd = beside(even, odd, 1, 4)
    broad = shape((3 * width, 9 * width), BF)
    upright = shape((9 * width, 3 * width), BF)

    w1_wide, w1_tall, w2_wide = call(
        lay_weights,
        [broad, upright, broad],
        [jnp.stack([w_first, w_second])],
        scratch=[pltpu.VMEM((TAPS * width, width), F32)],
    )
    inp = after(inp, w2_wide)
    edge = 4 * planes * GROWN + mask_rows
    even, odd, deep_in, deep_g, marks3 = call(
        functools.partial(pack_lines, planes, mask_rows),
        [shape((edge, width), BF)] * 2
        + [shape((lines * GROWN + SPARE, width), F32)] * 2
        + [shape((3 * mask_rows, width), BF)],
        [inp, grads, marks, z_odd, z_even],
    )
    y_even, y_odd = beside(even, odd, 4, 4)
    outer = count // INNER
    columns = TAPS * width if outer <= 4 else -(-TAPS // outer) * outer * width
    n_in = size_x + 2 + 2 * deep
    n_out = size_x + 2 * deep
    half = width // 2
    work = 2 * size_x * FACE * TAPS * width * width
    terms = [shape((half, columns), F32)] * 2

    def parts_of(rows):
        return [pltpu.VMEM((rows, 2 * width), F32), pltpu.VMEM((rows, width), F32)]

    inner_act, inner_back, in_t = call(
        functools.partial(ahead, planes, deep),
        [shape((n_out * INNER_PITCH, width), F32)] * 2
        + [shape((width, (n_out + 2) * FACE), BF)],
        [deep_in, deep_g, inp, w1_tall, w2_wide],
        scratch=[pltpu.VMEM((planes * INNER_PITCH, 9 * width), BF)]
        + parts_of(planes * INNER_PITCH)
        + [pltpu.VMEM(((n_out + 2) * FACE, width), F32)],
        flops=2 * work,
    )
    marks3 = after(marks3, in_t)
    kept_a, sent_a, act, grid_g = call(
        functools.partial(forward, planes, deep, mask_rows),
        terms + [shape((n_out * PITCH, width), F32), shape((n_in * IN_PITCH, width), F32)],
        [deep_in, deep_g, marks3, y_odd, y_even, inner_act, w1_tall],
        scratch=[
            pltpu.VMEM((n_in * IN_PITCH, width), F32),
            pltpu.VMEM((planes * OUTER_PITCH, 9 * width), BF),
        ]
        + parts_of(planes * OUTER_PITCH)
        + [
            pltpu.VMEM((planes * FACE, 9 * width), BF),
            pltpu.VMEM(((planes + 2) * FACE, width), F32),
            pltpu.VMEM((width, (planes + 2) * FACE), BF),
        ],
        flops=2 * work,
    )
    groups = (PLANE, MIXED if outer <= 4 else PLANE)
    own_a, *send_a = split_stage(groups[0], kept_a, swap(sent_a, "dp", 1))
    kept_b, sent_b, st_own = call(
        functools.partial(backward, planes, deep, mask_rows, tile_of),
        terms + [shape((n_out * FACE, 9 * width), BF)],
        [grid_g, act, inner_back, in_t, marks3, y_even, y_odd, w2_wide],
        scratch=[pltpu.VMEM((planes * OUTER_PITCH, 9 * width), BF)]
        + parts_of(planes * OUTER_PITCH)
        + [pltpu.VMEM((n_out * PITCH, width), F32)],
        flops=2 * work,
    )
    own_b, *send_b = split_stage(groups[1], kept_b, swap(sent_b, "dp", 1))
    gots_a = near(groups[0], send_a, groups[0][2])
    gots_b = near(groups[1], send_b, groups[1][2])

    def last_part(cue):
        return call(
            functools.partial(last, planes, deep, mask_rows),
            [shape((size_x * FACE, width), BF)],
            [after(st_own, cue), grads, marks3, w1_wide],
            scratch=parts_of(n_out * FACE),
            flops=work,
        )[0]

    value_a, value_b, result = across(groups, (own_a, own_b), (gots_a, gots_b), last_part)
    gots_a = near(groups[0], [value_a] * (INNER - 1), groups[0][3])
    gots_b = near(groups[1], [value_b] * (INNER - 1), groups[1][3])
    mine_a = back_stage(groups[0], value_a, gots_a)
    mine_b = back_stage(groups[1], value_b, gots_b)
    grad_second = finished(mine_a, swap(mine_a, "dp", 1))
    grad_first = finished(mine_b, swap(mine_b, "dp", 1))
    return (grad_first, grad_second, result[None])


def solution(mesh):
    in_specs = (P("dp", "blk", None), P("dp", "blk"), P(), P(), P("dp", "blk", None))
    out_specs = (P(), P(), P("dp", "blk", None))
    return jax.shard_map(
        on_device, mesh=mesh, in_specs=in_specs, out_specs=out_specs, check_vma=False
    )
```

```python
import functools

import jax
import jax.numpy as jnp
from jax import lax
from jax.experimental import pallas as pl
from jax.experimental.pallas import tpu as pltpu
from jax.sharding import PartitionSpec as P

TILE = 8
FACE = TILE * TILE
RIM = TILE + 2
GROWN = TILE + 4
IN_PITCH = 160
PITCH = 128
INNER_PITCH = 80
OUTER_PITCH = 48
EDGE = 24
LANES = 32
SPARE = 16
TAPS = 27
INNER = 4
BF = jnp.bfloat16
F32 = jnp.float32
unscale = 1.0 / 512.0
LIMIT = 24 * 2**20

VM = pl.BlockSpec(memory_space=pltpu.VMEM)
SM = pl.BlockSpec(memory_space=pltpu.SMEM)


def call(body, outs, ins, scratch=(), smem=(), flops=0):
    specs = [SM if i in smem else VM for i in range(len(ins))]
    moved = sum(a.size * a.dtype.itemsize for a in list(ins) + list(outs))
    return pl.pallas_call(
        body,
        out_shape=list(outs),
        in_specs=specs,
        out_specs=[VM] * len(outs),
        scratch_shapes=list(scratch),
        compiler_params=pltpu.CompilerParams(vmem_limit_bytes=LIMIT),
        cost_estimate=pl.CostEstimate(flops=flops, bytes_accessed=moved, transcendentals=0),
    )(*ins)


def shape(dims, kind):
    return jax.ShapeDtypeStruct(dims, kind)


def parity(stride):
    return lax.axis_index("blk") // stride % 2


def pack_depth(planes, tile_of, mask_rows, mask, both, inp, grads, marks, even, odd, wide):
    lines = planes * TILE
    row = lax.broadcasted_iota(jnp.int32, (mask_rows, 128), 0)
    filled = jnp.zeros((mask_rows, 128), F32)
    kept_of = [mask[0, tile_of(e)].astype(F32) for e in range(planes)]
    for e in range(planes):
        filled = jnp.where(row == e, kept_of[e], filled)
    filled = filled.astype(BF)
    marks[...] = filled
    even[4 * lines :, :] = filled
    odd[4 * lines :, :] = filled
    side = parity(1)
    for at, dst in enumerate((inp, grads)):
        for e in range(planes):
            rows = slice(e * FACE, (e + 1) * FACE)
            kept = both[at, rows, :].astype(F32) * kept_of[e]
            wide[rows, :] = kept
            dst[rows, :] = kept.astype(BF)

        def faces(lo, hi, at=at):
            for k in range(2):
                to = slice((at * 2 + k) * lines, (at * 2 + k + 1) * lines)
                lo[to, :] = wide[pl.ds(k, lines, stride=TILE), :].astype(BF)
                hi[to, :] = wide[pl.ds(TILE - 2 + k, lines, stride=TILE), :].astype(BF)

        @pl.when(side == 0)
        def _():
            faces(odd, even)

        @pl.when(side == 1)
        def _():
            faces(even, odd)


def pack_lines(
    planes, mask_rows, inp, grads, marks, z_odd, z_even, even, odd, deep_in, deep_g, marks3
):
    lines = planes * TILE
    plane = TILE * GROWN
    edge = 2 * GROWN
    swapped = parity(1) == 0

    def sides(rows):
        one, two = z_even[rows, :].astype(F32), z_odd[rows, :].astype(F32)
        return jnp.where(swapped, two, one), jnp.where(swapped, one, two)

    left, right = sides(slice(4 * lines, 4 * lines + mask_rows))
    for at, rows in enumerate((left, marks[...].astype(F32), right)):
        marks3[at * mask_rows : (at + 1) * mask_rows, :] = rows.astype(BF)
    lane = lax.broadcasted_iota(jnp.int32, (mask_rows, 128), 1)
    own = marks[...].astype(F32)
    packed = jnp.where(lane < LANES, left, jnp.where(lane < 2 * LANES, own, right)).astype(BF)
    for ref in (even, odd):
        ref[4 * planes * GROWN :, :] = packed
    side = parity(4)
    for at, (src, dst) in enumerate(((inp, deep_in), (grads, deep_g))):
        dst[lines * GROWN :, :] = jnp.zeros((SPARE, 128), F32)
        for pair in range(0, lines, 2):
            cells = src[pair * TILE : (pair + 2) * TILE, :].astype(F32)
            top = pair * GROWN + 2
            dst[top : top + TILE, :] = cells[:TILE]
            dst[top + GROWN : top + GROWN + TILE, :] = cells[TILE:]
        for k in range(2):
            left, right = sides(slice((at * 2 + k) * lines, (at * 2 + k + 1) * lines))
            dst[pl.ds(k, lines, stride=GROWN), :] = left
            dst[pl.ds(2 + TILE + k, lines, stride=GROWN), :] = right

        def faces(lo, hi, at=at, dst=dst):
            for e in range(0, planes, 2):
                to = slice((at * planes + e) * edge, (at * planes + e + 2) * edge)
                for ref, start in ((lo, 0), (hi, plane - edge)):
                    ref[to, :] = jnp.concatenate(
                        [
                            dst[p * plane + start : p * plane + start + edge, :]
                            for p in (e, e + 1)
                        ],
                        0,
                    ).astype(BF)

        @pl.when(side == 0)
        def _():
            faces(odd, even)

        @pl.when(side == 1)
        def _():
            faces(even, odd)


def lay_weights(src, wide_1, tall_1, wide_2, rows):
    for at, (broad, upright) in enumerate(((wide_1, tall_1), (wide_2, None))):
        rows[...] = src[at].astype(F32)
        for tap in range(TAPS):
            a, bc = tap // 9, tap % 9
            block = rows[pl.ds(tap, 128, stride=TAPS), :].astype(BF)
            broad[a * 128 : (a + 1) * 128, bc * 128 : (bc + 1) * 128] = block
            if upright is not None:
                upright[bc * 128 : (bc + 1) * 128, a * 128 : (a + 1) * 128] = block


def dot(a, b):
    return lax.dot_general(a, b, (((1,), (0,)), ((), ())), preferred_element_type=F32)


def dot_t(a, b):
    return lax.dot_general(a, b, (((1,), (1,)), ((), ())), preferred_element_type=F32)


def spread(planes, first_plane, at, deep, y_even, y_odd, grid):
    plane = TILE * GROWN
    edge = 2 * GROWN
    swapped = parity(4) == 0
    used = edge + plane + edge
    for p in range(grid.shape[0] // IN_PITCH):
        top = p * IN_PITCH
        if first_plane <= p < first_plane + planes:
            grid[top + used : top + IN_PITCH, :] = jnp.zeros((IN_PITCH - used, 128), F32)
            e = p - first_plane
            grid[top + edge : top + edge + plane, :] = deep[e * plane : (e + 1) * plane, :]
        else:
            grid[top : top + IN_PITCH, :] = jnp.zeros((IN_PITCH, 128), F32)
    for e in range(0, planes, 2):
        rows = slice((at * planes + e) * edge, (at * planes + e + 2) * edge)
        one, two = y_even[rows, :].astype(F32), y_odd[rows, :].astype(F32)
        low, high = jnp.where(swapped, two, one), jnp.where(swapped, one, two)
        for k in range(2):
            top = (first_plane + e + k) * IN_PITCH
            grid[top : top + edge, :] = low[k * edge : (k + 1) * edge]
            grid[top + edge + plane : top + used, :] = high[k * edge : (k + 1) * edge]


def stack(planes, first, pitch, parts, grid, stacked, out_pitch, flipped):
    for j in range(planes):
        for b in range(3):
            for c in range(3):
                step = (2 - b) * GROWN + 2 - c if flipped else b * GROWN + c
                at = (3 * b + c) * 128
                cells = [
                    grid[(j + first) * pitch + lo + step : (j + first) * pitch + lo + step + n, :]
                    for lo, n in parts
                ]
                cells = cells[0] if len(cells) == 1 else jnp.concatenate(cells, 0)
                to = j * out_pitch
                stacked[to : to + out_pitch, at : at + 128] = cells.astype(BF)


def add_planes(planes, pitch, shift, pair, single, p):
    total = jnp.zeros((pitch, 128), F32)
    for a, (ref, at) in enumerate(((pair, 0), (pair, 128), (single, 0))):
        j = p - shift(a)
        if 0 <= j < planes:
            total = total + ref[j * pitch : (j + 1) * pitch, at : at + 128]
    return total


def own_lines(grid, at):
    return jnp.concatenate([grid[at : at + TILE, :], grid[at + GROWN : at + GROWN + TILE, :]], 0)


def stack_own(planes, first, pitch, skip, grid, stacked):
    for p in range(planes):
        for y in range(0, TILE, 2):
            to = p * FACE + y * TILE
            for b in range(3):
                for c in range(3):
                    at = (p + first) * pitch + (y + skip + 2 - b) * GROWN + skip + 2 - c
                    stacked[to : to + 2 * TILE, (3 * b + c) * 128 : (3 * b + c + 1) * 128] = (
                        own_lines(grid, at).astype(BF)
                    )


def marked(planes, mask_rows, marks3, y_even, y_odd):
    tail = 4 * planes * GROWN
    swapped = parity(4) == 0

    def mark(by, bz, e):
        if by == 1:
            at = bz * mask_rows + e
            return marks3[at : at + 1, :].astype(F32)
        one = y_even[tail + e : tail + e + 1, :].astype(F32)
        two = y_odd[tail + e : tail + e + 1, :].astype(F32)
        row = jnp.where(swapped, two, one) if by == 0 else jnp.where(swapped, one, two)
        return row[:, LANES * bz : LANES * bz + 1]

    return mark


def spans(rows, ends):
    row = lax.broadcasted_iota(jnp.int32, (rows, 128), 0)
    line = row // GROWN
    depth = row - line * GROWN
    return [(line >= lo) & (line <= hi) for lo, hi in ends], [
        (depth >= lo) & (depth <= hi) for lo, hi in ends
    ]


def pad_terms(*refs):
    used = TAPS * 128
    for ref in refs:
        if ref.shape[1] > used:
            ref[:, used:] = jnp.zeros((ref.shape[0], ref.shape[1] - used), ref.dtype)


def ahead(
    planes, deep,
    deep_in, deep_g, inp, w1_tall, w2_wide,
    act, back, in_t,
    stacked, pair, single, padded,
):
    size_x = planes - 4 * deep
    n_out = size_x + 2 * deep
    parts = ((0, INNER_PITCH),)
    plane = TILE * GROWN
    stack(planes, 0, plane, parts, deep_in, stacked, INNER_PITCH, False)
    pair[...] = dot(stacked[...], w1_tall[:, 0:256])
    single[...] = dot(stacked[...], w1_tall[:, 256:384])
    for p in range(n_out):
        act[p * INNER_PITCH : (p + 1) * INNER_PITCH, :] = add_planes(
            planes, INNER_PITCH, lambda a: 1 - deep - a, pair, single, p
        )
    stack(planes, 0, plane, parts, deep_g, stacked, INNER_PITCH, True)
    pair[...] = dot_t(stacked[...], w2_wide[0:256, :])
    single[...] = dot_t(stacked[...], w2_wide[256:384, :])
    for p in range(n_out):
        back[p * INNER_PITCH : (p + 1) * INNER_PITCH, :] = add_planes(
            planes, INNER_PITCH, lambda a: a - 1 - deep, pair, single, p
        )
    padded[...] = jnp.zeros_like(padded)
    top = (1 + deep) * FACE
    rows = size_x * FACE
    padded[top : top + rows, :] = inp[2 * deep * FACE : 2 * deep * FACE + rows, :].astype(F32)
    in_t[...] = padded[...].T.astype(BF)


def whole_plane(inner, outer, p):
    ends = outer[p * OUTER_PITCH : (p + 1) * OUTER_PITCH]
    middle = inner[p * INNER_PITCH : p * INNER_PITCH + PITCH - 2 * EDGE - TILE, :]
    rest = jnp.zeros((TILE, 128), F32)
    return jnp.concatenate([ends[:EDGE], middle, ends[EDGE:], rest], 0)


OUTER_PARTS = ((0, EDGE), (PITCH - EDGE - TILE, EDGE))


def correlate(core, turned_rows, stacked, columns, kept, sent):
    half = kept.shape[0]
    third = stacked.shape[1]
    halves = [pl.ds(pl.multiple_of(side * half, half), half) for side in (core, 1 - core)]
    left = [
        turned_rows[rows, a * FACE : a * FACE + columns] for rows in halves for a in range(3)
    ]
    part = dot(jnp.concatenate(left, 0), stacked) * unscale
    for n, out in enumerate((kept, sent)):
        for a in range(3):
            at = (n * 3 + a) * half
            out[:, a * third : (a + 1) * third] = part[at : at + half]
    pad_terms(kept, sent)


def forward(
    planes, deep, mask_rows,
    deep_in, deep_g, marks3, y_odd, y_even, inner, w1_tall,
    kept, sent, act, grid_g,
    grid_in, outer, pair, single, st_own, hidden, hid_t,
):
    core = lax.axis_index("dp")
    size_x = planes - 4 * deep
    n_out = size_x + 2 * deep
    first = 1 - deep
    spread(planes, first, 0, deep_in, y_even, y_odd, grid_in)
    stack(planes, first, IN_PITCH, OUTER_PARTS, grid_in, outer, OUTER_PITCH, False)
    pair[...] = dot(outer[...], w1_tall[:, 0:256])
    single[...] = dot(outer[...], w1_tall[:, 256:384])
    for p in range(n_out):
        ends = add_planes(planes, OUTER_PITCH, lambda a: 1 - deep - a, pair, single, p)
        act[p * PITCH : (p + 1) * PITCH, :] = whole_plane(
            inner.at[p * INNER_PITCH : (p + 1) * INNER_PITCH, :], ends, 0
        )
    spread(planes, first, 1, deep_g, y_even, y_odd, grid_g)
    stack_own(planes, first, IN_PITCH, 1, grid_g, st_own)
    hidden[...] = jnp.zeros_like(hidden)
    for p in range(size_x):
        at = mask_rows + p + 2 * deep
        keep = marks3[at : at + 1, :].astype(F32)
        for y in range(0, TILE, 2):
            pre = own_lines(act, (p + deep) * PITCH + (y + 1) * GROWN + 1)
            to = (p + 1 + 2 * deep) * FACE + y * TILE
            hidden[to : to + 2 * TILE, :] = pre * jax.nn.sigmoid(pre) * keep
    hid_t[...] = hidden[...].T.astype(BF)
    correlate(core, hid_t, st_own[...], planes * FACE, kept, sent)


def backward(
    planes, deep, mask_rows, tile_of,
    grid_g, act, inner, in_t, marks3, y_even, y_odd, w2_wide,
    kept, sent, st_own,
    outer, pair, single, pg,
):
    core = lax.axis_index("dp")
    size_x = planes - 4 * deep
    n_out = size_x + 2 * deep
    mark = marked(planes, mask_rows, marks3, y_even, y_odd)
    in_line, in_depth = spans(PITCH, ((0, 0), (1, TILE), (RIM - 1, RIM - 1)))
    stack(planes, 1 - deep, IN_PITCH, OUTER_PARTS, grid_g, outer, OUTER_PITCH, True)
    pair[...] = dot_t(outer[...], w2_wide[0:256, :])
    single[...] = dot_t(outer[...], w2_wide[256:384, :])
    tile, keep = None, None
    for p in range(n_out):
        if tile_of(p + deep) != tile:
            tile, keep = tile_of(p + deep), jnp.zeros((PITCH, 128), F32)
            for by in range(3):
                for bz in range(3):
                    keep = jnp.where(in_line[by] & in_depth[bz], mark(by, bz, p + deep), keep)
        ends = add_planes(planes, OUTER_PITCH, lambda a: a - 1 - deep, pair, single, p)
        back = whole_plane(inner.at[p * INNER_PITCH : (p + 1) * INNER_PITCH, :], ends, 0)
        pre = act[p * PITCH : (p + 1) * PITCH, :]
        sigma = jax.nn.sigmoid(pre)
        grad = back * sigma * (1.0 + pre * (1.0 - sigma))
        pg[p * PITCH : (p + 1) * PITCH, :] = (grad * keep).astype(BF).astype(F32)
    stack_own(n_out, 0, PITCH, 0, pg, st_own)
    correlate(core, in_t, st_own[...], n_out * FACE, kept, sent)


def last(planes, deep, mask_rows, st_own, grads, marks3, w1_wide, result, pair, single):
    size_x = planes - 4 * deep
    n_out = size_x + 2 * deep
    pair[...] = dot_t(st_own[...], w1_wide[0:256, :])
    single[...] = dot_t(st_own[...], w1_wide[256:384, :])
    for p in range(size_x):
        e = p + 2 * deep
        m = marks3[mask_rows + e : mask_rows + e + 1, :].astype(F32)
        total = add_planes(n_out, FACE, lambda a: a - 1 - deep, pair, single, p)
        summed = (grads[e * FACE : (e + 1) * FACE, :].astype(F32) + total) * m
        result[p * FACE : (p + 1) * FACE, :] = summed.astype(BF)


def swap(value, axis, bits):
    count = lax.axis_size(axis)
    return lax.ppermute(value, axis, [(source, source ^ bits) for source in range(count)])


def cross(value, bits):
    count = lax.axis_size("blk")
    pairs = [
        (core * count + s, core * count + (s ^ bit))
        for core, bit in enumerate(bits)
        for s in range(count)
    ]
    return lax.ppermute(value, ("dp", "blk"), pairs)


PLANE = ((1, 2), (2, 1), ((0, 3, 1, 2), (0, 3, 1, 2)), ((0, 3, 1, 2), (0, 3, 2, 1)))
MIXED = ((1, 4), (2, 4), ((0, 1, 3, 2), (0, 3, 2, 1)), ((0, 3, 2, 1), (0, 3, 2, 1)))


def met(orders, n):
    return jnp.where(lax.axis_index("dp") == 0, orders[0][n], orders[1][n])


def spot(group):
    chip, core = lax.axis_index("blk"), lax.axis_index("dp")
    places = [chip // one % 2 + 2 * (chip // two % 2) for one, two in group[:2]]
    return jnp.where(core == 0, places[0], places[1])


def split_rows(group, kept, got, own, *sent):
    me = spot(group)
    rows = own.shape[0]
    for n in range(INNER):
        at = pl.ds(pl.multiple_of((me ^ met(group[2], n)) * rows, rows), rows)
        value = kept[at, :] + got[at, :].astype(F32)
        if n == 0:
            own[...] = value
        else:
            sent[n - 1][...] = value.astype(BF)


def split_columns(parts, *refs):
    kept, got, own, sent = refs[0], refs[1:INNER], refs[INNER], refs[INNER + 1 :]
    me = lax.axis_index("blk") // INNER
    columns = own.shape[1]
    for k in range(parts):
        at = pl.ds(pl.multiple_of((me ^ k) * columns, 128), columns)
        value = kept[:, at]
        for ref in got:
            value = value + ref[:, at].astype(F32)
        if k == 0:
            own[...] = value
        else:
            sent[k - 1][...] = value.astype(BF)


def add_pair(one, two, out):
    out[...] = (one[...].astype(F32) + two[...].astype(F32)).astype(BF)


def lay_rows(one, two, out, wide):
    rows = one.shape[0]
    for tap in range(TAPS):
        columns = slice(tap * 128, (tap + 1) * 128)
        total = one[:, columns].astype(F32) + two[:, columns].astype(F32)
        wide[pl.ds(tap, rows, stride=TAPS), :] = total
    out[...] = wide[...].astype(BF)


def add_all(parts, *refs):
    value = refs[0][...]
    for ref in refs[1:parts]:
        value = value + ref[...].astype(F32)
    refs[parts][...] = value.astype(BF)


def join_columns(parts, *refs):
    me = lax.axis_index("blk") // INNER
    out = refs[parts]
    columns = refs[0].shape[1]
    for k in range(parts):
        out[:, pl.ds(pl.multiple_of((me ^ k) * columns, 128), columns)] = refs[k][...]


def join_rows(group, *refs):
    me = spot(group)
    out = refs[INNER]
    rows = refs[0].shape[0]
    for n in range(INNER):
        out[pl.ds(pl.multiple_of((me ^ met(group[3], n)) * rows, rows), rows), :] = refs[n][...]


def finish(own, other, out):
    core = lax.axis_index("dp")
    half = own.shape[0]

    @pl.when(core == 0)
    def _():
        out[:half, :] = own[...].astype(F32)
        out[half:, :] = other[...].astype(F32)

    @pl.when(core == 1)
    def _():
        out[:half, :] = other[...].astype(F32)
        out[half:, :] = own[...].astype(F32)


def after(value, *others):
    return lax.optimization_barrier((value, *others))[0]


def near(group, values, orders):
    return [
        cross(v, [one * (k % 2) + two * (k // 2) for (one, two), k in zip(group, both)])
        for v, both in list(zip(values, zip(*[order[1:] for order in orders])))
    ]


def far(values):
    return [swap(v, "blk", INNER * (k + 1)) for k, v in enumerate(values)]


def split_stage(group, kept, got):
    half, columns = kept.shape
    rows = half // INNER
    return call(
        functools.partial(split_rows, group),
        [shape((rows, columns), F32)] + [shape((rows, columns), BF)] * (INNER - 1),
        [kept, got],
    )


def sum_stage(own, gots):
    parts = len(gots) + 1
    return call(functools.partial(add_all, parts), [shape(own.shape, BF)], [own] + gots)[0]


def laid_pair(value, got):
    laid = (value.shape[0] * TAPS, 128)
    return call(lay_rows, [shape(laid, BF)], [value, got], scratch=[pltpu.VMEM(laid, F32)])[0]


def pair_stage(value, got):
    return call(add_pair, [shape(value.shape, BF)], [value, got])[0]


def back_stage(group, wide, gots):
    rows, columns = wide.shape
    return call(
        functools.partial(join_rows, group), [shape((rows * INNER, columns), BF)], [wide] + gots
    )[0]


def wide_sum(own, gots):
    outer = lax.axis_size("blk") // INNER
    rows, columns = own.shape
    part = columns // outer
    own, *send = call(
        functools.partial(split_columns, outer),
        [shape((rows, part), F32)] + [shape((rows, part), BF)] * (outer - 1),
        [own] + gots,
    )
    done = sum_stage(own, far(send))
    return call(
        functools.partial(join_columns, outer),
        [shape((rows, columns), BF)],
        [done] + far([done] * (outer - 1)),
    )[0]


def finished(mine, other):
    return call(finish, [shape((2 * mine.shape[0], 128), F32)], [mine, other])[0]


def rest_steps(group):
    count = lax.axis_size("blk")
    bits = [1 << k for k in range(count.bit_length() - 1)]
    left = [[bit for bit in bits if bit not in used] for used in group[:2]]
    return list(zip(left[0], reversed(left[1])))


def across(groups, owns, gots, beside):
    if lax.axis_size("blk") // INNER > 4:
        sums = [wide_sum(own, got) for own, got in zip(owns, gots)]
        one, two = [laid_pair(value, jnp.zeros_like(value)) for value in sums]
        return one, two, beside(one)
    one = sum_stage(owns[0], gots[0])
    two = sum_stage(after(owns[1], one), gots[1])
    steps = [rest_steps(group) for group in groups]
    other = None
    for n, (bits_one, bits_two) in enumerate(zip(*steps)):
        add = laid_pair if n == len(steps[0]) - 1 else pair_stage
        got_one, got_two = cross(one, bits_one), cross(two, bits_two)
        one = add(one, got_one)
        if other is None:
            other = beside(two)
        two = add(two, got_two)
    return one, two, other


def on_device(features, tile_mask, w_first, w_second, cotangent):
    width = features.shape[2]
    tiles = tile_mask.shape[1]
    size_x = tiles * TILE
    count = lax.axis_size("blk")
    deep = 1 if count // 16 > 1 else 0
    planes = size_x + 4 * deep
    feat, cot, mask = features[0], cotangent[0], tile_mask

    def along(value, stride, extent, toward):
        pairs = [
            (s, s + toward * stride)
            for s in range(count)
            if 0 <= s // stride % extent + toward < extent
        ]
        return lax.ppermute(value, "blk", pairs)

    if deep:
        wide_mask = jnp.broadcast_to(
            jnp.repeat(tile_mask[0], TILE)[:, None], (size_x, width)
        ).astype(BF)
        keep = jnp.repeat(wide_mask, FACE, axis=0)
        feat, cot = feat * keep, cot * keep
        slab = 2 * FACE
        up = jnp.concatenate([feat[-slab:], cot[-slab:], wide_mask[-16:]], 0)
        down = jnp.concatenate([feat[:slab], cot[:slab], wide_mask[:16]], 0)
        before = along(up, 16, count // 16, 1)
        behind = along(down, 16, count // 16, -1)
        feat = jnp.concatenate([before[:slab], feat, behind[:slab]], 0)
        cot = jnp.concatenate([before[slab : 2 * slab], cot, behind[slab : 2 * slab]], 0)
        ends = [v[2 * slab : 2 * slab + 1, :1].astype(jnp.int32) for v in (before, behind)]
        mask = jnp.concatenate([ends[0], tile_mask, ends[1]], 1)

    def tile_of(e):
        if not deep:
            return e // TILE
        return (e + TILE - 2) // TILE

    def beside(one, two, stride, extent):
        pairs = ([], [])
        for s in range(count):
            place = s // stride % extent
            if place + 1 < extent:
                pairs[place % 2].extend([(s, s + stride), (s + stride, s)])
        return lax.ppermute(one, "blk", pairs[0]), lax.ppermute(two, "blk", pairs[1])

    mask_rows = -(-planes // 16) * 16
    lines = planes * TILE
    cells = planes * FACE
    side = 4 * lines + mask_rows
    inp, grads, marks, even, odd = call(
        functools.partial(pack_depth, planes, tile_of, mask_rows),
        [shape((cells, width), BF)] * 2
        + [shape((mask_rows, width), BF)]
        + [shape((side, width), BF)] * 2,
        [mask, jnp.stack([feat, cot])],
        scratch=[pltpu.VMEM((cells, width), F32)],
        smem=(0,),
    )
    z_even, z_odd = beside(even, odd, 1, 4)
    broad = shape((3 * width, 9 * width), BF)
    upright = shape((9 * width, 3 * width), BF)

    w1_wide, w1_tall, w2_wide = call(
        lay_weights,
        [broad, upright, broad],
        [jnp.stack([w_first, w_second])],
        scratch=[pltpu.VMEM((TAPS * width, width), F32)],
    )
    inp = after(inp, w2_wide)
    edge = 4 * planes * GROWN + mask_rows
    even, odd, deep_in, deep_g, marks3 = call(
        functools.partial(pack_lines, planes, mask_rows),
        [shape((edge, width), BF)] * 2
        + [shape((lines * GROWN + SPARE, width), F32)] * 2
        + [shape((3 * mask_rows, width), BF)],
        [inp, grads, marks, z_odd, z_even],
    )
    y_even, y_odd = beside(even, odd, 4, 4)
    outer = count // INNER
    columns = TAPS * width if outer <= 4 else -(-TAPS // outer) * outer * width
    n_in = size_x + 2 + 2 * deep
    n_out = size_x + 2 * deep
    half = width // 2
    work = 2 * size_x * FACE * TAPS * width * width
    terms = [shape((half, columns), F32)] * 2

    def parts_of(rows):
        return [pltpu.VMEM((rows, 2 * width), F32), pltpu.VMEM((rows, width), F32)]

    inner_act, inner_back, in_t = call(
        functools.partial(ahead, planes, deep),
        [shape((n_out * INNER_PITCH, width), F32)] * 2
        + [shape((width, (n_out + 2) * FACE), BF)],
        [deep_in, deep_g, inp, w1_tall, w2_wide],
        scratch=[pltpu.VMEM((planes * INNER_PITCH, 9 * width), BF)]
        + parts_of(planes * INNER_PITCH)
        + [pltpu.VMEM(((n_out + 2) * FACE, width), F32)],
        flops=2 * work,
    )
    marks3 = after(marks3, in_t)
    kept_a, sent_a, act, grid_g = call(
        functools.partial(forward, planes, deep, mask_rows),
        terms + [shape((n_out * PITCH, width), F32), shape((n_in * IN_PITCH, width), F32)],
        [deep_in, deep_g, marks3, y_odd, y_even, inner_act, w1_tall],
        scratch=[
            pltpu.VMEM((n_in * IN_PITCH, width), F32),
            pltpu.VMEM((planes * OUTER_PITCH, 9 * width), BF),
        ]
        + parts_of(planes * OUTER_PITCH)
        + [
            pltpu.VMEM((planes * FACE, 9 * width), BF),
            pltpu.VMEM(((planes + 2) * FACE, width), F32),
            pltpu.VMEM((width, (planes + 2) * FACE), BF),
        ],
        flops=2 * work,
    )
    groups = (PLANE, MIXED if outer <= 4 else PLANE)
    own_a, *send_a = split_stage(groups[0], kept_a, swap(sent_a, "dp", 1))
    kept_b, sent_b, st_own = call(
        functools.partial(backward, planes, deep, mask_rows, tile_of),
        terms + [shape((n_out * FACE, 9 * width), BF)],
        [grid_g, act, inner_back, in_t, marks3, y_even, y_odd, w2_wide],
        scratch=[pltpu.VMEM((planes * OUTER_PITCH, 9 * width), BF)]
        + parts_of(planes * OUTER_PITCH)
        + [pltpu.VMEM((n_out * PITCH, width), F32)],
        flops=2 * work,
    )
    own_b, *send_b = split_stage(groups[1], kept_b, swap(sent_b, "dp", 1))
    gots_a = near(groups[0], send_a, groups[0][2])
    gots_b = near(groups[1], send_b, groups[1][2])

    def last_part(cue):
        return call(
            functools.partial(last, planes, deep, mask_rows),
            [shape((size_x * FACE, width), BF)],
            [after(st_own, cue), grads, marks3, w1_wide],
            scratch=parts_of(n_out * FACE),
            flops=work,
        )[0]

    value_a, value_b, result = across(groups, (own_a, own_b), (gots_a, gots_b), last_part)
    gots_a = near(groups[0], [value_a] * (INNER - 1), groups[0][3])
    gots_b = near(groups[1], [value_b] * (INNER - 1), groups[1][3])
    mine_a = back_stage(groups[0], value_a, gots_a)
    mine_b = back_stage(groups[1], value_b, gots_b)
    grad_second = finished(mine_a, swap(mine_a, "dp", 1))
    grad_first = finished(mine_b, swap(mine_b, "dp", 1))
    return (grad_first, grad_second, result[None])


def solution(mesh):
    in_specs = (P("dp", "blk", None), P("dp", "blk"), P(), P(), P("dp", "blk", None))
    out_specs = (P(), P(), P("dp", "blk", None))
    return jax.shard_map(
        on_device, mesh=mesh, in_specs=in_specs, out_specs=out_specs, check_vma=False
    )
```
